32 devices in a mesh: dp: 8 (over z, y), expert: 4 (over x, core).
Axes of the slice: x: 2, y: 2, z: 4, core: 2. Of those that a mesh axis runs over, the one named last changes fastest.
Arguments:
- tokens: bfloat16 [4096, 2048], P(('dp', 'expert')), may hold values from -6 to 6
- cotangent: bfloat16 [4096, 2048], P(('dp', 'expert')), may hold values from -6 to 6
- segments: int32 [32, 128], P(('dp', 'expert')), may hold values from 0 to 5, never falling along the last dimension, each value on 1 to 64 neighbouring positions
- routes: int32 [4096, 8], P(('dp', 'expert')), may hold values from 0 to 31, as said below
- slot_index: int32 [4096, 8], P(('dp', 'expert')), may hold values from 0 to 35, as said below
- in_projection: bfloat16 [2048, 6144], P(('dp', 'expert')), may hold values from -0.13258252 to 0.13258252
- out_projection: bfloat16 [2048, 2048], P(('dp', 'expert')), may hold values from -0.375 to 0.375
- router_weight: bfloat16 [2048, 32], P(('dp', 'expert')), may hold values from -0.06629126 to 0.06629126
- norm_gains: bfloat16 [4, 2048], P(None, ('dp', 'expert')), may hold values from 0.4 to 2
- expert_in: bfloat16 [32, 2048, 2048], P('expert', 'dp'), may hold values from -0.125 to 0.125
- expert_down: bfloat16 [32, 1024, 2048], P('expert', 'dp'), may hold values from -1.5 to 1.5
Outputs:
- block_out: float32 [4096, 2048], P(('dp', 'expert'))
- input_grad: float32 [4096, 2048], P(('dp', 'expert'))
- grad_in_projection: float32 [2048, 6144], P(('dp', 'expert'))
- grad_out_projection: float32 [2048, 2048], P(('dp', 'expert'))
- grad_router: float32 [2048, 32], P(('dp', 'expert'))
- grad_norm_gains: float32 [4, 2048], P(None, ('dp', 'expert'))
- grad_expert_in: float32 [32, 2048, 2048], P('expert', 'dp')
- grad_expert_down: float32 [32, 1024, 2048], P('expert', 'dp')
The draws below stay inside these ranges and needn't reach their ends.
Inputs may be any that keep to these rules, and one draw needn't show every extreme that they name: `routes`: each token names 8 different experts. Among the 128 tokens of one device no expert is named more than 36 times, and on every device one expert is named exactly 36 times, the same one on all devices of one index of dp. `slot_index`: among the tokens of one device, an expert named c times takes each slot 0 to c - 1 once.
All inputs are finite; a program needn't handle non-finite values.
Results may differ from the reference program's by a relative error of at most 0.012.
The reference program's roundings to bfloat16 on the way count: a program that leaves them out, or rounds other values in their place, can miss the bound.
Values may be sent and summed in bfloat16 or wider, within the bound.
No kernel may reach another device: no remote copies, remote signals or barrier semaphores. Data moves between devices by JAX's collectives and lax.ppermute only.
A program may use at most 320 MiB of HBM per device.

```python
import math
import jax
import jax.numpy as jnp
import numpy as np
from jax import lax

D = 2048
HEADS = 16
HEAD_DIM = 128
FF = 1024
TOP = 8
TOK_DEV = 128
SPREAD = 4
SEG_COUNT = 6
EXPERTS = 32
MEAN_LOAD = 32
CAP = 36
SEQS = 32
TOKENS = 4096
N_EXPERT = 4


def route_tables(key):
    base_key = jax.random.fold_in(key, 11)
    pick_key, block_key = jax.random.split(base_key)
    chosen = jax.random.randint(pick_key, (SEQS // N_EXPERT,), 0, EXPERTS)

    def one_block(block_index):
        block_seed = jax.random.fold_in(block_key, block_index)
        seed_order, seed_shift, seed_rows, seed_cols = jax.random.split(block_seed, 4)
        expert_order = jax.random.permutation(seed_order, EXPERTS).astype(jnp.int32)
        fullest = chosen[block_index // N_EXPERT]
        location = jnp.argmax(expert_order == fullest)
        leading = expert_order[0]
        expert_order = expert_order.at[location].set(leading).at[0].set(fullest)
        shifts = jax.random.randint(seed_shift, (EXPERTS // 2,), 0, SPREAD + 1).at[0].set(SPREAD)
        counts = jnp.zeros((EXPERTS,), jnp.int32)
        counts = counts.at[expert_order[0::2]].set(MEAN_LOAD + shifts)
        counts = counts.at[expert_order[1::2]].set(MEAN_LOAD - shifts)
        ending = jnp.cumsum(counts)
        starting = ending - counts
        position = jnp.arange(TOK_DEV * TOP, dtype=jnp.int32)
        labels = jnp.sum((ending[None, :] <= position[:, None]).astype(jnp.int32), axis=1)
        places = position - starting[labels]
        labels = labels.reshape(TOP, TOK_DEV).T
        places = places.reshape(TOP, TOK_DEV).T
        shuffle = jax.random.permutation(seed_rows, TOK_DEV)
        labels = labels[shuffle]
        places = places[shuffle]
        scores = jax.random.randint(seed_cols, (TOK_DEV, TOP), 0, 1048576) * TOP + jnp.arange(TOP, dtype=jnp.int32)[None, :]
        column_order = jnp.argsort(scores, axis=1)
        return (jnp.take_along_axis(labels, column_order, axis=1), jnp.take_along_axis(places, column_order, axis=1))
    labels, places = jax.vmap(one_block)(jnp.arange(SEQS))
    return (labels.reshape(TOKENS, TOP).astype(jnp.int32), places.reshape(TOKENS, TOP).astype(jnp.int32))


def draw_routes(key, part):
    return route_tables(key)[0]


def draw_slot_index(key, part):
    return route_tables(key)[1]


def draw_norm_gains(key, part):
    seed_norm, seed_head = jax.random.split(jax.random.fold_in(key, 23))
    norm_rows = jax.random.uniform(seed_norm, (2, D), jnp.float32, 0.5, 1.5)
    log_values = jax.random.uniform(seed_head, (2, D), jnp.float32, math.log(0.5), math.log(2.0))
    head_rows = jnp.exp(log_values)
    return jnp.concatenate([norm_rows, head_rows], axis=0).astype(jnp.bfloat16)


def draw_in_projection(key, part):
    seed_main = jax.random.fold_in(key, 31)
    noise = jnp.clip(jax.random.normal(seed_main, (D, 3 * D), jnp.float32), -6.0, 6.0)
    return (noise * D ** (-0.5)).astype(jnp.bfloat16)


def draw_router_weight(key, part):
    seed_main = jax.random.fold_in(key, 41)
    noise = jnp.clip(jax.random.normal(seed_main, (D, EXPERTS), jnp.float32), -6.0, 6.0)
    return (noise * 0.5 * D ** (-0.5)).astype(jnp.bfloat16)


def block_levels(key, shape, pieces, low, top_value):
    gain, own = 1.0, jax.random.fold_in(key, 6)
    for dim, parts in pieces:
        heights = jnp.exp(jax.random.uniform(jax.random.fold_in(own, dim), (parts,), jnp.float32, low / len(pieces), top_value / len(pieces)))
        gain = gain * jnp.repeat(heights, shape[dim] // parts).reshape([-1 if axis == dim else 1 for axis in range(len(shape))])
    return gain


def profile(count, total, limit, lean):
    weights = [(1 << 20) // math.isqrt(rank ** lean) + 1 for rank in range(2, count + 1)]
    surplus, given = total - limit - (count - 1), [1] * (count - 1)
    while surplus > 0:
        movable = [i for i in range(count - 1) if given[i] < limit]
        pool, budget = sum([weights[i] for i in movable]), surplus
        for i in movable:
            extra = min(limit - given[i], max(1, budget * weights[i] // pool), surplus)
            given[i] = given[i] + extra
            surplus = surplus - extra
    return np.array([limit] + given)


def ragged(key, count, total, most, slope):
    if count == 2:
        one = jax.random.randint(key, (), max(1, total - most), min(most, total - 1) + 1)
        return jnp.stack([one, total - one])
    lengths = jnp.asarray(profile(count, total, most, slope), jnp.int32)
    twos = (count - 1) // 2
    source_of, taker = lengths[1:1 + 2 * twos:2], lengths[2:2 + 2 * twos:2]
    slack = jnp.minimum(source_of - 1, most - taker)
    passed = jax.random.randint(jax.random.fold_in(key, 1), (twos,), 0, 1 << 20) % (slack + 1)
    lengths = lengths.at[1:1 + 2 * twos:2].set(source_of - passed).at[2:2 + 2 * twos:2].set(taker + passed)
    return lengths[jax.random.permutation(jax.random.fold_in(key, 2), count)]


def normal_values(rng, dims, spread, bound, cuts=(), kind=jnp.bfloat16):
    drawn = spread * jax.random.normal(rng, dims, jnp.float32)
    if cuts:
        drawn = drawn * block_levels(rng, dims, cuts, -0.22, 0.18)
    return jnp.clip(drawn, -bound, bound).astype(kind)


def setup_inputs(seed: int = 0) -> dict:
    arg_keys = jax.random.split(jax.random.key(seed), 12)
    tokens = normal_values(arg_keys[0], (TOKENS, D), 1.0, 6.0, ((0, 32),))
    cotangent = normal_values(arg_keys[1], (TOKENS, D), 1.0, 6.0, ((0, 32),))
    segments = jax.vmap(lambda own: jnp.searchsorted(jnp.cumsum(ragged(own, SEG_COUNT, TOK_DEV, TOK_DEV // 2, 2)), jnp.arange(TOK_DEV), side="right"))(jax.random.split(arg_keys[2], SEQS)).reshape((SEQS, TOK_DEV)).astype(jnp.int32)
    routes = draw_routes(jax.random.fold_in(arg_keys[11], 71), 0)
    slot_index = draw_slot_index(jax.random.fold_in(arg_keys[11], 71), 0)
    in_projection = draw_in_projection(jax.random.fold_in(arg_keys[11], 71), 0)
    out_projection = normal_values(arg_keys[6], (D, D), (D // 8) ** -0.5, 0.375, ((0, 32),))
    router_weight = draw_router_weight(jax.random.fold_in(arg_keys[11], 71), 0)
    norm_gains = draw_norm_gains(jax.random.fold_in(arg_keys[11], 71), 0)
    expert_in = normal_values(arg_keys[9], (EXPERTS, D, 2 * FF), D ** -0.5, 0.125, ((0, 4), (1, 8)))
    expert_down = normal_values(arg_keys[10], (EXPERTS, FF, D), (FF // 64) ** -0.5, 1.5, ((0, 4), (1, 8)))
    return dict(tokens=tokens, cotangent=cotangent, segments=segments, routes=routes, slot_index=slot_index, in_projection=in_projection, out_projection=out_projection, router_weight=router_weight, norm_gains=norm_gains, expert_in=expert_in, expert_down=expert_down)


EPSILON = 1e-05
ROPE_BASE = 10000.0
MASKED = -1e+30

def normalize(tensor):
    factor = lax.rsqrt(lax.optimization_barrier(jnp.mean(tensor * tensor, axis=-1, keepdims=True)) + EPSILON)
    return (tensor * factor, factor)

def normalize_back(upstream, normed, factor):
    return factor * (upstream - normed * lax.optimization_barrier(jnp.mean(upstream * normed, axis=-1, keepdims=True)))

def rope_tables(length):
    half_dim = HEAD_DIM // 2
    position = jnp.arange(length).astype(jnp.float32)
    frequency = ROPE_BASE ** (-2.0 * jnp.arange(half_dim).astype(jnp.float32) / HEAD_DIM)
    angles = position[:, None] * frequency[None, :]
    return (jnp.cos(angles)[:, None, :], jnp.sin(angles)[:, None, :])

def rotate(tensor, cosine, sine_table, inverse):
    length = tensor.shape[0]
    halves = tensor.reshape(length, HEADS, 2, HEAD_DIM // 2)
    first_half = halves[:, :, 0, :]
    second_half = halves[:, :, 1, :]
    if inverse:
        sine_table = -sine_table
    turned = jnp.stack([first_half * cosine - second_half * sine_table, second_half * cosine + first_half * sine_table], axis=2)
    return turned.reshape(length, HEADS * HEAD_DIM)

def split_heads(tensor):
    return tensor.reshape(tensor.shape[0], HEADS, HEAD_DIM).astype(jnp.float32)

def masked_scores(queries, key_rows, segment):
    length = queries.shape[0]
    raw_scores = jnp.einsum('qhd,khd->hqk', split_heads(queries), split_heads(key_rows)) * HEAD_DIM ** (-0.5)
    row_index = lax.broadcasted_iota(jnp.int32, (length, length), 0)
    col_index = lax.broadcasted_iota(jnp.int32, (length, length), 1)
    allowed = (segment[:, None] == segment[None, :]) & (col_index <= row_index)
    return (jnp.where(allowed[None], raw_scores, MASKED), allowed)

def attend(queries, key_rows, values, segment):
    length = queries.shape[0]
    scores, allowed = masked_scores(queries, key_rows, segment)
    row_max = lax.optimization_barrier(jnp.max(scores, axis=-1, keepdims=True))
    exp_terms = jnp.exp(scores - row_max)
    row_total = lax.optimization_barrier(jnp.sum(exp_terms, axis=-1, keepdims=True))
    log_total = row_max + jnp.log(row_total)
    weights_b = (exp_terms / row_total).astype(jnp.bfloat16)
    attended = jnp.einsum('hqk,khd->qhd', weights_b.astype(jnp.float32), split_heads(values))
    return (attended.astype(jnp.bfloat16).reshape(length, HEADS * HEAD_DIM), log_total)

def attend_back(queries, key_rows, values, segment, log_total, attended, grad_attended):
    length = queries.shape[0]
    scores, allowed = masked_scores(queries, key_rows, segment)
    weights_f = jnp.where(allowed[None], jnp.exp(scores - log_total), 0.0)
    weights_b = weights_f.astype(jnp.bfloat16).astype(jnp.float32)
    grad_heads = split_heads(grad_attended)
    grad_values = jnp.einsum('hqk,qhd->khd', weights_b, grad_heads)
    grad_weights = jnp.einsum('qhd,khd->hqk', grad_heads, split_heads(values))
    row_delta = lax.optimization_barrier(jnp.sum(grad_heads * split_heads(attended), axis=-1)).T
    grad_scores = (weights_f * (grad_weights - row_delta[:, :, None]) * HEAD_DIM ** (-0.5)).astype(jnp.bfloat16)
    grad_scores = grad_scores.astype(jnp.float32)
    grad_queries = jnp.einsum('hqk,khd->qhd', grad_scores, split_heads(key_rows))
    grad_keys = jnp.einsum('hqk,qhd->khd', grad_scores, split_heads(queries))
    width = HEADS * HEAD_DIM
    return (grad_queries.reshape(length, width), grad_keys.reshape(length, width), grad_values.reshape(length, width))

def activate(pre_act):
    half_width = pre_act.shape[1] // 2
    return (jax.nn.silu(pre_act[:, :half_width]) * pre_act[:, half_width:]).astype(jnp.bfloat16)

def expert_back(pre_act, row_block, grad_rows, weight_in, weight_down):
    half_width = pre_act.shape[1] // 2
    gate_part = pre_act[:, :half_width]
    up_part = pre_act[:, half_width:]
    act_rows = activate(pre_act)
    grad_weight_down = jnp.dot(act_rows.T, grad_rows, preferred_element_type=jnp.float32)
    grad_act = jnp.dot(grad_rows, weight_down.T, preferred_element_type=jnp.float32)
    gate_sigmoid = jax.nn.sigmoid(gate_part)
    grad_gate = grad_act * up_part * gate_sigmoid * (1.0 + gate_part * (1.0 - gate_sigmoid))
    grad_up = grad_act * gate_part * gate_sigmoid
    grad_pre = jnp.concatenate([grad_gate, grad_up], axis=1).astype(jnp.bfloat16)
    grad_weight_in = jnp.dot(row_block.T, grad_pre, preferred_element_type=jnp.float32)
    grad_in_rows = jnp.dot(grad_pre, weight_in.T, preferred_element_type=jnp.float32).astype(jnp.bfloat16)
    return (grad_weight_in, grad_weight_down, grad_in_rows)

def forward_sequence(token_rows, segment, in_projection, out_projection, gain_rows, cosine, sine_table):
    residual = token_rows.astype(jnp.float32)
    normed1, factor1 = normalize(residual)
    hidden1 = (normed1 * gain_rows[0]).astype(jnp.bfloat16)
    projected = jnp.dot(hidden1, in_projection, preferred_element_type=jnp.float32)
    query_normed, query_factor = normalize(projected[:, :D])
    key_normed, key_factor = normalize(projected[:, D:2 * D])
    queries = rotate(query_normed * gain_rows[2], cosine, sine_table, False).astype(jnp.bfloat16)
    key_rows = rotate(key_normed * gain_rows[3], cosine, sine_table, False).astype(jnp.bfloat16)
    values = projected[:, 2 * D:].astype(jnp.bfloat16)
    attended, log_total = attend(queries, key_rows, values, segment)
    middle = residual + jnp.dot(attended, out_projection, preferred_element_type=jnp.float32)
    return (normed1, factor1, hidden1, query_normed, query_factor, key_normed, key_factor, queries, key_rows, values, attended, log_total, middle)

def reference(tokens, cotangent, segments, routes, slot_index, in_projection, out_projection, router_weight, norm_gains, expert_in, expert_down):
    gain_rows = norm_gains.astype(jnp.float32)
    cosine, sine_table = rope_tables(TOK_DEV)
    token_seqs = tokens.reshape(SEQS, TOK_DEV, D)

    def forward_step(carried, inputs):
        token_rows, segment = inputs
        kept_state = forward_sequence(token_rows, segment, in_projection, out_projection, gain_rows, cosine, sine_table)
        middle_rows = kept_state[-1]
        normed2, factor2 = normalize(middle_rows)
        return (carried, (middle_rows, (normed2 * gain_rows[1]).astype(jnp.bfloat16)))
    _, (middle, hidden2) = lax.scan(forward_step, 0, (token_seqs, segments))
    middle = middle.reshape(TOKENS, D)
    hidden2 = hidden2.reshape(TOKENS, D)
    logits = jnp.dot(hidden2, router_weight, preferred_element_type=jnp.float32)
    router_probs = jax.nn.softmax(logits, axis=-1)
    chosen = (routes[:, :, None] == jnp.arange(EXPERTS, dtype=jnp.int32)[None, None, :]).astype(jnp.float32)
    gate_values = lax.optimization_barrier(jnp.sum(router_probs[:, None, :] * chosen, axis=-1))
    owner_device = (jnp.arange(TOKENS, dtype=jnp.int32) // TOK_DEV).astype(jnp.int32)
    column = (owner_device[:, None] * CAP + slot_index).astype(jnp.int32)
    entry_ids = jnp.arange(TOKENS * TOP, dtype=jnp.int32)
    slot_table = jnp.zeros((EXPERTS, SEQS * CAP), jnp.int32).at[routes.reshape(-1), column.reshape(-1)].set(entry_ids)
    filled = jnp.zeros((EXPERTS, SEQS * CAP), jnp.float32).at[routes.reshape(-1), column.reshape(-1)].set(1.0)
    gate_flat = gate_values.reshape(-1)
    grad_top = cotangent.astype(jnp.float32)

    def expert_step(carried, inputs):
        mixture, grad_hidden2, grad_gates = carried
        entries, live_mask, weight_in, weight_down = inputs
        owners = (entries // TOP).astype(jnp.int32)
        present = live_mask[:, None] > 0.5
        row_block = jnp.where(present, hidden2[owners], jnp.zeros((), hidden2.dtype))
        pre_act = jnp.dot(row_block, weight_in, preferred_element_type=jnp.float32)
        outputs = jnp.dot(activate(pre_act), weight_down, preferred_element_type=jnp.float32).astype(jnp.bfloat16)
        out_float = outputs.astype(jnp.float32)
        gate_rows = jnp.where(live_mask > 0.5, gate_flat[entries], 0.0)
        mixture = mixture.at[owners].add(gate_rows[:, None] * out_float)
        top_rows = grad_top[owners]
        grad_gates = grad_gates.at[entries].add(jnp.where(live_mask > 0.5, lax.optimization_barrier(jnp.sum(top_rows * out_float, axis=-1)), 0.0))
        grad_rows = (gate_rows[:, None] * top_rows).astype(jnp.bfloat16)
        grad_weight_in, grad_weight_down, grad_in_rows = expert_back(pre_act, row_block, grad_rows, weight_in, weight_down)
        grad_hidden2 = grad_hidden2.at[owners].add(jnp.where(present, grad_in_rows.astype(jnp.float32), 0.0))
        return ((mixture, grad_hidden2, grad_gates), (grad_weight_in, grad_weight_down))
    start_state = (jnp.zeros((TOKENS, D), jnp.float32), jnp.zeros((TOKENS, D), jnp.float32), jnp.zeros((TOKENS * TOP,), jnp.float32))
    (mixture, grad_hidden2, grad_gates), (grad_expert_in, grad_expert_down) = lax.scan(expert_step, start_state, (slot_table, filled, expert_in, expert_down))
    block_out = middle + mixture
    grad_probs = lax.optimization_barrier(jnp.sum(grad_gates.reshape(TOKENS, TOP)[:, :, None] * chosen, axis=1))
    grad_logits = (router_probs * (grad_probs - lax.optimization_barrier(jnp.sum(router_probs * grad_probs, axis=-1, keepdims=True)))).astype(jnp.bfloat16)
    grad_router = jnp.dot(hidden2.T, grad_logits, preferred_element_type=jnp.float32)
    grad_hidden2 = grad_hidden2 + jnp.dot(grad_logits, router_weight.T, preferred_element_type=jnp.float32)
    normed2, factor2 = normalize(middle)
    grad_gain_moe = lax.optimization_barrier(jnp.sum(grad_hidden2 * normed2, axis=0))
    grad_middle = grad_top + normalize_back(grad_hidden2 * gain_rows[1], normed2, factor2)

    def backward_step(carried, inputs):
        total_qkv, total_out, total_gains = carried
        token_rows, segment, grad_mid = inputs
        normed1, factor1, hidden1, query_normed, query_factor, key_normed, key_factor, queries, key_rows, values, attended, log_total, middle_rows = forward_sequence(token_rows, segment, in_projection, out_projection, gain_rows, cosine, sine_table)
        grad_mid_b = grad_mid.astype(jnp.bfloat16)
        total_out = total_out + jnp.dot(attended.T, grad_mid_b, preferred_element_type=jnp.float32)
        grad_attended = jnp.dot(grad_mid_b, out_projection.T, preferred_element_type=jnp.float32).astype(jnp.bfloat16)
        grad_queries, grad_keys, grad_values = attend_back(queries, key_rows, values, segment, log_total, attended, grad_attended)
        grad_qscaled = rotate(grad_queries, cosine, sine_table, True)
        grad_kscaled = rotate(grad_keys, cosine, sine_table, True)
        grad_query_raw = normalize_back(grad_qscaled * gain_rows[2], query_normed, query_factor)
        grad_key_raw = normalize_back(grad_kscaled * gain_rows[3], key_normed, key_factor)
        grad_projected = jnp.concatenate([grad_query_raw, grad_key_raw, grad_values], axis=1).astype(jnp.bfloat16)
        total_qkv = total_qkv + jnp.dot(hidden1.T, grad_projected, preferred_element_type=jnp.float32)
        grad_hidden1 = jnp.dot(grad_projected, in_projection.T, preferred_element_type=jnp.float32)
        total_gains = total_gains + jnp.stack([lax.optimization_barrier(jnp.sum(grad_hidden1 * normed1, axis=0)), lax.optimization_barrier(jnp.sum(grad_qscaled * query_normed, axis=0)), lax.optimization_barrier(jnp.sum(grad_kscaled * key_normed, axis=0))])
        input_rows = grad_mid + normalize_back(grad_hidden1 * gain_rows[0], normed1, factor1)
        return ((total_qkv, total_out, total_gains), input_rows)
    start_back = (jnp.zeros((D, 3 * D), jnp.float32), jnp.zeros((D, D), jnp.float32), jnp.zeros((3, D), jnp.float32))
    (grad_in_projection, grad_out_projection, grad_three), input_grad = lax.scan(backward_step, start_back, (token_seqs, segments, grad_middle.reshape(SEQS, TOK_DEV, D)))
    grad_norm_gains = jnp.stack([grad_three[0], grad_gain_moe, grad_three[1], grad_three[2]])
    return (block_out, input_grad.reshape(TOKENS, D), grad_in_projection, grad_out_projection, grad_router, grad_norm_gains, grad_expert_in, grad_expert_down)
```

```python
import functools

import jax
import jax.numpy as jnp
import numpy as np
from jax import lax
from jax.experimental import pallas as pl
from jax.experimental.pallas import tpu as pltpu
from jax.sharding import PartitionSpec as P

HEADS = 16
HEAD_DIM = 128
EPSILON = 1e-05
ROPE_BASE = 10000.0
MASKED = -1e30
AXES = ("dp", "expert")
BF16 = jnp.bfloat16
F32 = jnp.float32
ROWS_BACK = (((1,), (1,)), ((), ()))
SUM_ROWS = (((0,), (0,)), ((), ()))


def dot(left, right, dims=(((1,), (0,)), ((), ()))):
    return lax.dot_general(left, right, dims, preferred_element_type=F32)


def after(value, *others):
    return lax.optimization_barrier((value,) + others)[0]


def normalize(tensor):
    factor = lax.rsqrt(jnp.mean(tensor * tensor, axis=-1, keepdims=True) + EPSILON)
    return (tensor * factor, factor)


def normalize_back(upstream, normed, factor):
    return factor * (upstream - normed * jnp.mean(upstream * normed, axis=-1, keepdims=True))


def rope_tables(length):
    half_dim = HEAD_DIM // 2
    position = jnp.arange(length).astype(F32)
    frequency = ROPE_BASE ** (-2.0 * jnp.arange(half_dim).astype(F32) / HEAD_DIM)
    angles = position[:, None] * frequency[None, :]
    return (jnp.cos(angles), jnp.sin(angles))


def rotate(tensor, cosine, sine_table, inverse):
    half = HEAD_DIM // 2
    first_half, second_half = tensor[..., :half], tensor[..., half:]
    cosine, sine_table = cosine[None, :, None, :], sine_table[None, :, None, :]
    if inverse:
        sine_table = -sine_table
    return jnp.concatenate(
        [
            first_half * cosine - second_half * sine_table,
            second_half * cosine + first_half * sine_table,
        ],
        axis=-1,
    )


class Grid:
    def __init__(self, swap=True):
        self.dp = lax.axis_size("dp")
        self.ex = lax.axis_size("expert")
        self.count = self.dp * self.ex
        self.size = {"z": 4, "y": self.dp // 4, "x": self.ex // 2, "c": 2}
        self.swap = swap and self.size["x"] == self.size["y"]
        self.size["A"], self.size["B"] = self.size["y"], self.size["x"]
        d, e = lax.axis_index("dp"), lax.axis_index("expert")
        self.linear = d * self.ex + e
        ny = self.size["y"]
        self.at = {"z": d // ny, "y": d % ny, "x": e // 2, "c": e % 2}

    def real(self, axis, core):
        if axis in "AB":
            return "yx"[(axis == "B") != (core == 1 and self.swap)]
        return axis

    def index(self, p):
        return (p["z"] * self.size["y"] + p["y"]) * self.ex + p["x"] * 2 + p["c"]

    def move(self, value, axis, kind="pair"):
        s = self.size
        if s[axis] == 2:
            moves = {0: 1, 1: 0}
        else:
            moves = {
                "pair": {0: 1, 1: 0, 2: 3, 3: 2},
                "mid": {1: 2, 2: 1},
                "out": {1: 0, 2: 3},
                "in": {0: 1, 3: 2},
            }[kind]
        pairs = []
        for i in range(self.count):
            d, e = divmod(i, self.ex)
            here = {"z": d // s["y"], "y": d % s["y"], "x": e // 2, "c": e % 2}
            line = self.real(axis, here["c"])
            if here[line] in moves:
                pairs.append((i, self.index({**here, line: moves[here[line]]})))
        return lax.ppermute(value, AXES, pairs)

    def position(self, axis):
        if axis in "AB" and self.swap:
            other = self.real(axis, 1)
            return jnp.where(self.at["c"] == 0, self.at[self.real(axis, 0)], self.at[other])
        return self.at[self.real(axis, 0)]

    def slots(self, axis):
        n = self.size[axis]
        table = {
            1: [[0]],
            2: [[0, 1], [1, 0]],
            4: [[0, 1, 2, 3], [1, 0, 2, 3], [2, 3, 1, 0], [3, 2, 1, 0]],
        }[n]
        return jnp.asarray(np.array(table, np.int32))[self.at[axis]]

    def sources(self):
        c, y, x, z = [self.slots(a) for a in "cyxz"]
        z = z.reshape(2, 1, 1, 1, 2)
        c = c.reshape(1, -1, 1, 1, 1)
        along_a = (1, 1, 1, -1, 1)
        along_b = (1, 1, -1, 1, 1)
        xs, ys = x.reshape(along_b), y.reshape(along_a)
        if self.swap:
            xs = jnp.where(c == 0, xs, x.reshape(along_a))
            ys = jnp.where(c == 0, ys, y.reshape(along_b))
        return ((z * self.size["y"] + ys) * self.ex + xs * 2 + c).reshape(-1)

    def dp_sources(self):
        z = self.slots("z").reshape(2, 1, 2)
        return (z * self.size["y"] + self.slots("y").reshape(1, -1, 1)).reshape(-1)

    def line_gather(self, value, axis):
        n = self.size[axis]
        if n == 1:
            return [value]
        pair = self.move(value, axis)
        if n == 2:
            return [value, pair]
        m0, m1 = self.move(value, axis, "mid"), self.move(pair, axis, "mid")
        o0, o1 = self.move(m0, axis, "out"), self.move(m1, axis, "out")
        at = self.position(axis)
        mid = (at == 1) | (at == 2)
        return [value, pair, jnp.where(mid, m0, o0), jnp.where(mid, m1, o1)]

    def line_reduce(self, slots, axis, kind=BF16):
        n = self.size[axis]

        def sent(value, *way):
            return self.move(value.astype(kind), axis, *way).astype(F32)

        if n == 1:
            return slots[0]
        if n == 2:
            return slots[0] + sent(slots[1])
        m3 = sent(slots[3] + sent(slots[3], "in"), "mid")
        m2 = sent(slots[2] + sent(slots[2], "in"), "mid")
        return slots[0] + m2 + sent(slots[1] + m3)

    def gather(self, value):
        pieces = self.line_gather(value, "z")
        out = []
        for h in range(2):
            near = jnp.stack(pieces[2 * h : 2 * h + 2])
            table = [self.line_gather(a, "B") for a in self.line_gather(near, "A")]
            block = jnp.concatenate([row[b] for b in range(self.size["B"]) for row in table])
            out += self.line_gather(block, "c")
        return out

    def scatter(self, groups):
        halves = [None, None]
        for h in (1, 0):
            total = self.line_reduce(groups[2 * h : 2 * h + 2], "c")
            nb, na = self.size["B"], self.size["A"]
            total = total.reshape((nb, na, 2) + total.shape[1:])
            total = self.line_reduce([total[i] for i in range(nb)], "B")
            halves[h] = self.line_reduce([total[i] for i in range(na)], "A")
        return self.line_reduce([halves[0][0], halves[0][1], halves[1][0], halves[1][1]], "z")

    def dp_gather(self, value):
        pieces = self.line_gather(value, "z")
        z, y = self.slots("z"), self.slots("y")
        n = value.shape[0]
        whole = jnp.zeros((n * self.dp,) + value.shape[1:], value.dtype)
        for h in range(2):
            near = jnp.stack(pieces[2 * h : 2 * h + 2])
            for j, got in enumerate(self.line_gather(near, "y")):
                for k in range(2):
                    place = (z[2 * h + k] * self.size["y"] + y[j]) * n
                    whole = lax.dynamic_update_slice_in_dim(whole, got[k], place, 0)
        return whole, pieces[3]

    def dp_scatter(self, halves):
        sums = [None, None]
        for h in (1, 0):
            sums[h] = self.line_reduce([halves[h][i] for i in range(self.size["y"])], "y")
        return self.line_reduce([sums[0][0], sums[0][1], sums[1][0], sums[1][1]], "z")

    def flip(self, value, bit):
        return lax.ppermute(value, AXES, [(i, i ^ bit) for i in range(self.count)])

    def small_gather(self, value):
        held, bit = value[None], 1
        while bit < self.count:
            held = jnp.concatenate([held, self.flip(held, bit)])
            bit *= 2
        return held[self.linear ^ jnp.arange(self.count)]

    def small_scatter(self, value):
        held = value[self.linear ^ jnp.arange(self.count)]
        bit = self.count // 2
        while bit:
            held = held[:bit] + self.flip(held[bit:], bit)
            bit //= 2
        return held[0]

    def group_sum(self, value):
        total = value
        for r in range(1, self.ex):
            total = total + self.flip(value, r)
        return total


def exchange(value):
    return lax.all_to_all(value, "expert", split_axis=0, concat_axis=0, tiled=True)


def moe_kernel(ff, local, x_ref, lift_ref, gate_ref, w_ref, grad_ref, act_ref, sum_ref, back_ref):
    x = x_ref[...]
    per = 128 // ff
    lane = lax.broadcasted_iota(jnp.int32, (x.shape[0], 128), 1)
    for b in range(local // per):
        wide, narrow = pl.ds(256 * b, 256), pl.ds(128 * b, 128)
        pre_act = dot(x, w_ref[:, wide])
        gate_part, up_part = pre_act[:, :128], pre_act[:, 128:]
        spread = jnp.broadcast_to(gate_ref[:, pl.ds(b * per, 1)], lane.shape)
        for k in range(1, per):
            spread = jnp.where(
                lane < k * ff,
                spread,
                jnp.broadcast_to(gate_ref[:, pl.ds(b * per + k, 1)], lane.shape),
            )
        lifted = lift_ref[:, narrow]
        sig = 1.0 / (1.0 + jnp.exp(-gate_part))
        act = (gate_part * sig * up_part).astype(BF16).astype(F32)
        act_ref[:, narrow] = (act * spread).astype(BF16)
        terms = act * lifted
        for k in range(per):
            mine = jnp.where((lane >= k * ff) & (lane < (k + 1) * ff), terms, 0.0)
            sum_ref[:, pl.ds(b * per + k, 1)] = jnp.sum(mine, axis=1, keepdims=True)
        grad_act = lifted * spread
        grad_gate = grad_act * up_part * sig * (1.0 + gate_part * (1.0 - sig))
        grad_ref[:, pl.ds(256 * b, 128)] = grad_gate.astype(BF16)
        grad_ref[:, pl.ds(256 * b + 128, 128)] = (grad_act * gate_part * sig).astype(BF16)
    back_ref[...] = dot(grad_ref[...], w_ref[...], ROWS_BACK).astype(back_ref.dtype)


def moe_rows(x, lifted, gates, weight, ff, start, total, kind):
    width, wide = weight.shape
    local = gates.shape[1]
    tile = 256 if total % 256 == 0 else 128
    skip = start // tile
    row = lambda n: pl.BlockSpec((tile, n), lambda i: (i + skip, 0))
    out = lambda n: pl.BlockSpec((tile, n), lambda i: (i, 0))
    return pl.pallas_call(
        functools.partial(moe_kernel, ff, local),
        grid=(total // tile,),
        in_specs=[
            row(width),
            row(wide // 2),
            row(local),
            pl.BlockSpec((width, wide), lambda i: (0, 0)),
        ],
        out_specs=[out(wide), out(wide // 2), out(local), out(width)],
        out_shape=[
            jax.ShapeDtypeStruct((total, wide), BF16),
            jax.ShapeDtypeStruct((total, wide // 2), BF16),
            jax.ShapeDtypeStruct((total, local), F32),
            jax.ShapeDtypeStruct((total, width), kind),
        ],
        compiler_params=pltpu.CompilerParams(vmem_limit_bytes=56 * 1024 * 1024),
        cost_estimate=pl.CostEstimate(
            flops=4 * total * width * wide, bytes_accessed=total * width * 12, transcendentals=0
        ),
    )(x, lifted, gates, weight)


def deal_kernel(dp, stage_ref, in_ref, *out_refs):
    for r in range(dp):
        place = pl.multiple_of(lax.bitwise_xor(stage_ref[0], r) * 128, 128)
        out_refs[r][...] = in_ref[0, :, pl.ds(place, 128)]


def deal(expert_in, stage, dp):
    local, rows, wide = expert_in.shape
    half = wide // 2
    return pl.pallas_call(
        functools.partial(deal_kernel, dp),
        grid_spec=pltpu.PrefetchScalarGridSpec(
            num_scalar_prefetch=1,
            grid=(local, 2),
            in_specs=[pl.BlockSpec((1, rows, half), lambda e, g, s: (e, 0, g))],
            out_specs=[pl.BlockSpec((rows, 128), lambda e, g, s: (0, 2 * e + g))] * dp,
        ),
        out_shape=[jax.ShapeDtypeStruct((rows, local * 256), expert_in.dtype)] * dp,
        compiler_params=pltpu.CompilerParams(vmem_limit_bytes=32 * 1024 * 1024),
    )(stage.reshape(1), expert_in)


def undeal_kernel(dp, stage_ref, *refs):
    out_ref = refs[dp]
    e, g = pl.program_id(0), pl.program_id(1)
    column = pl.multiple_of((2 * e + g) * 128, 128)
    for r in range(dp):
        place = pl.multiple_of(lax.bitwise_xor(stage_ref[0], r) * 128, 128)
        out_ref[0, :, pl.ds(place, 128)] = refs[r][:, pl.ds(column, 128)].astype(F32)


def undeal(pieces, stage):
    dp = len(pieces)
    rows, wide = pieces[0].shape
    local = wide // 256
    return pl.pallas_call(
        functools.partial(undeal_kernel, dp),
        grid_spec=pltpu.PrefetchScalarGridSpec(
            num_scalar_prefetch=1,
            grid=(local, 2),
            in_specs=[pl.BlockSpec((rows, wide), lambda e, g, s: (0, 0))] * dp,
            out_specs=pl.BlockSpec((1, rows, dp * 128), lambda e, g, s: (e, 0, g)),
        ),
        out_shape=jax.ShapeDtypeStruct((local, rows, 2 * dp * 128), F32),
        compiler_params=pltpu.CompilerParams(vmem_limit_bytes=48 * 1024 * 1024),
    )(stage.reshape(1), *pieces)


def deal_narrow(expert_in, stage, dp):
    local, rows, wide = expert_in.shape
    ff = wide // 2 // dp
    split = expert_in.reshape(local * ff // 128, 128 // ff, rows, 2, dp, ff)
    out = []
    for r in range(dp):
        piece = lax.dynamic_index_in_dim(split, stage ^ r, 4, False)
        out.append(piece.transpose(2, 0, 3, 1, 4).reshape(rows, 2 * local * ff))
    return out


def undeal_narrow(pieces, stage, local):
    dp = len(pieces)
    rows, wide = pieces[0].shape
    ff = wide // 2 // local
    whole = jnp.stack(pieces)[stage ^ jnp.arange(dp)]
    whole = whole.reshape(dp, rows, wide // 256, 2, 128 // ff, ff).astype(F32)
    return whole.transpose(2, 4, 1, 3, 0, 5).reshape(local, rows, 2 * dp * ff)


def masked(segment):
    length = segment.shape[1]
    row_index = lax.broadcasted_iota(jnp.int32, (length, length), 0)
    col_index = lax.broadcasted_iota(jnp.int32, (length, length), 1)
    return (segment[:, :, None] == segment[:, None, :]) & (col_index <= row_index)[None]


def attend(queries, key_rows, values, allowed):
    raw = jnp.einsum("sqhd,skhd->shqk", queries, key_rows, preferred_element_type=F32)
    scores = jnp.where(allowed[:, None], raw * HEAD_DIM ** (-0.5), MASKED)
    row_max = jnp.max(scores, axis=-1, keepdims=True)
    exp_terms = jnp.exp(scores - row_max)
    weights_f = exp_terms / jnp.sum(exp_terms, axis=-1, keepdims=True)
    attended = jnp.einsum(
        "shqk,skhd->sqhd", weights_f.astype(BF16), values, preferred_element_type=F32
    )
    return (attended.astype(BF16), weights_f)


def attend_back(queries, key_rows, values, weights_f, attended, grad_heads):
    weights_b = weights_f.astype(BF16)
    grad_values = jnp.einsum("shqk,sqhd->skhd", weights_b, grad_heads, preferred_element_type=F32)
    grad_weights = jnp.einsum("sqhd,skhd->shqk", grad_heads, values, preferred_element_type=F32)
    row_delta = jnp.sum(grad_heads.astype(F32) * attended.astype(F32), axis=-1)
    row_delta = jnp.swapaxes(row_delta, 1, 2)[..., None]
    grad_scores = (weights_f * (grad_weights - row_delta) * HEAD_DIM ** (-0.5)).astype(BF16)
    grad_queries = jnp.einsum(
        "shqk,skhd->sqhd", grad_scores, key_rows, preferred_element_type=F32
    )
    grad_keys = jnp.einsum("shqk,sqhd->skhd", grad_scores, queries, preferred_element_type=F32)
    return (grad_queries, grad_keys, grad_values)


def per_device(
    tokens,
    cotangent,
    segments,
    routes,
    slot_index,
    in_projection,
    out_projection,
    router_weight,
    norm_gains,
    expert_in,
    expert_down,
):
    grid, wide_x = Grid(), Grid(False)
    length, width = tokens.shape
    count, dp, ex = grid.count, grid.dp, grid.ex
    local = expert_in.shape[0]
    expert_count = ex * local
    top = routes.shape[1]
    ff = expert_down.shape[1]
    rows = width // count
    block = width // dp
    heads = HEADS // ex
    span = heads * HEAD_DIM
    group = lax.axis_index("expert")
    stage = lax.axis_index("dp")
    cosine, sine_table = rope_tables(length)
    source, out_source = grid.sources(), wide_x.sources()
    back, out_back = jnp.argsort(source), jnp.argsort(out_source)
    dp_source = grid.dp_sources()

    def reorder(tensor, order):
        parts = order.shape[0]
        return jnp.take(
            tensor.reshape(tensor.shape[0], parts, width // parts), order, axis=1
        ).reshape(tensor.shape[0], width)

    small = jnp.concatenate(
        [
            norm_gains.reshape(-1),
            router_weight.reshape(-1),
            routes.astype(BF16).reshape(-1),
            segments.astype(BF16).reshape(-1),
        ]
    )
    small = jnp.pad(small, (0, -small.shape[0] % 128)).reshape(-1, 128)
    small = grid.small_gather(small).reshape(count, -1)
    cuts = np.cumsum([4 * rows, rows * expert_count, length * top, length])
    all_gains, all_router, all_routes, all_segments, _ = jnp.split(small, cuts, axis=1)
    gains = jnp.swapaxes(all_gains.reshape(count, 4, rows), 0, 1).reshape(4, width).astype(F32)
    router = all_router.reshape(width, expert_count)
    all_routes = all_routes.reshape(count, length, top).astype(jnp.int32)
    segment = lax.dynamic_slice_in_dim(
        all_segments.reshape(dp, ex, length), stage, 1, 0
    )[0].astype(jnp.int32)
    allowed = masked(segment)
    gain_q = lax.dynamic_slice_in_dim(gains[2], group * span, span)
    gain_k = lax.dynamic_slice_in_dim(gains[3], group * span, span)

    piece = in_projection.reshape(rows, 3, ex, span).transpose(2, 0, 1, 3)
    piece = exchange(piece.reshape(ex, rows, 3 * span)).reshape(block, 3 * span)
    tokens_g = exchange(jnp.broadcast_to(tokens[None], (ex, length, width)))
    proj, arrived = grid.dp_gather(piece)
    proj_out = jnp.concatenate(wide_x.gather(after(out_projection, arrived))).reshape(width, width)

    others = list(range(dp - 1, 0, -1))
    weight_in = jnp.zeros((width, 2 * local * ff), BF16)
    dealt = (deal if ff == 128 else deal_narrow)(expert_in, stage, dp)
    gone = [arrived, arrived]
    for r in [0] + others:
        got = dealt[r]
        if r:
            got = lax.ppermute(after(got, gone[-2]), "dp", [(i, i ^ r) for i in range(dp)])
            gone.append(got)
        weight_in = lax.dynamic_update_slice_in_dim(weight_in, got, (stage ^ r) * block, 0)
    weight_down = expert_down.reshape(local * ff, width)

    chunks = max(1, length * count // 4096)
    size = length // chunks

    def gather_rows(tensor, i):
        return jnp.concatenate(grid.gather(tensor[i * size : (i + 1) * size])).reshape(-1, width)

    normed1_g, factor1 = normalize(tokens_g.reshape(ex * length, width).astype(F32))
    hidden1_g = (normed1_g * gains[0]).astype(BF16)
    projected = dot(hidden1_g, proj)
    query_raw, key_raw = projected[:, :span], projected[:, span : 2 * span]
    squares = jnp.stack([jnp.sum(query_raw**2, axis=-1), jnp.sum(key_raw**2, axis=-1)])
    factors = lax.rsqrt(grid.group_sum(squares) / width + EPSILON)[:, :, None]
    query_factor, key_factor = factors[0], factors[1]
    query_normed, key_normed = query_raw * query_factor, key_raw * key_factor

    def by_heads(tensor):
        return tensor.reshape(ex, length, heads, HEAD_DIM)

    queries = rotate(by_heads(query_normed * gain_q), cosine, sine_table, False).astype(BF16)
    key_rows = rotate(by_heads(key_normed * gain_k), cosine, sine_table, False).astype(BF16)
    values = by_heads(projected[:, 2 * span :].astype(BF16))
    attended_h, weights_f = attend(queries, key_rows, values, allowed)
    attended = exchange(attended_h.reshape(ex, length, span))
    attended_s = reorder(jnp.swapaxes(attended, 0, 1).reshape(length, width), out_source)
    residual = tokens.astype(F32)
    middle = residual + dot(attended_s, proj_out)
    normed2, factor2 = normalize(middle)
    hidden2 = (normed2 * gains[1]).astype(BF16)
    router_probs = jax.nn.softmax(dot(hidden2, router), axis=-1)
    grad_top = cotangent.astype(F32)

    routes_s = all_routes[source]
    mine = group * local + jnp.arange(local, dtype=jnp.int32)
    mixtures, grad_h2s, probs_parts = [], [], []
    grad_in_w, grad_down_w = [0.0] * dp, 0.0
    for i in range(chunks):
        ready = (grad_h2s[-1], mixtures[-1], grad_in_w, grad_down_w) if i else (arrived,)
        cot = gather_rows(after(cotangent, *ready), i)
        hid = gather_rows(after(hidden2, *ready), i)
        total = hid.shape[0]
        probs = jax.nn.softmax(dot(hid, router), axis=-1)
        probs = lax.dynamic_slice_in_dim(probs, group * local, local, 1)
        named = routes_s[:, i * size : (i + 1) * size, :].reshape(total, top)
        chosen = jnp.any(named[:, :, None] == mine[None, None, :], axis=1)
        gate_dense = jnp.where(chosen, probs, 0.0)
        lifted = dot(cot, weight_down, ROWS_BACK)
        part = total // 4
        slotted = (count // 4, size, width)
        done = [None] * 4
        for j in (3, 2, 1, 0):
            kind = BF16 if j % 2 else F32
            done[j] = moe_rows(
                hid, lifted, gate_dense, weight_in, ff, j * part, part, kind
            )
        grad_h2s.append(grid.scatter([d[3].reshape(slotted) for d in done]))
        mixtures.append(grid.scatter([dot(d[1], weight_down).reshape(slotted) for d in done]))
        probs_part = jnp.where(chosen, jnp.concatenate([d[2] for d in done]), 0.0)
        probs_parts.append(probs_part.reshape(count, size, local))
        grad_pre = jnp.concatenate([d[0] for d in done])
        act_gated = jnp.concatenate([d[1] for d in done])
        grad_down_w += dot(act_gated, cot, SUM_ROWS)
        for r in others + [0]:
            rows_in = lax.dynamic_slice_in_dim(hid, (stage ^ r) * block, block, 1)
            grad_in_w[r] += dot(rows_in, grad_pre, SUM_ROWS)

    home = [None] * dp
    gone = []
    for r in others + [0]:
        piece = grad_in_w[r].astype(BF16)
        if r:
            if len(gone) > 1:
                piece = after(piece, gone[-2])
            piece = lax.ppermute(piece, "dp", [(i, i ^ r) for i in range(dp)])
            gone.append(piece)
        home[r] = piece
    grad_expert_in = undeal(home, stage) if ff == 128 else undeal_narrow(home, stage, local)
    grad_expert_down = grad_down_w.reshape(local, ff, width)

    probs_all = jnp.concatenate(probs_parts, axis=1)[back]
    place = (jnp.arange(expert_count) // local == group).astype(F32)
    probs_wide = (jnp.tile(probs_all, (1, 1, ex)) * place).reshape(
        count, length * expert_count // 128, 128
    )
    grad_probs = grid.small_scatter(probs_wide).reshape(length, expert_count)

    block_out = middle + jnp.concatenate(mixtures)
    grad_logits = (
        router_probs * (grad_probs - jnp.sum(router_probs * grad_probs, axis=-1, keepdims=True))
    ).astype(BF16)
    grad_router_part = dot(hidden2, grad_logits, SUM_ROWS)
    grad_hidden2 = jnp.concatenate(grad_h2s) + dot(grad_logits, router, ROWS_BACK)
    grad_gain_moe = jnp.sum(grad_hidden2 * normed2, axis=0)
    grad_middle = grad_top + normalize_back(grad_hidden2 * gains[1], normed2, factor2)
    grad_mid_b = grad_middle.astype(BF16)
    grad_attended = reorder(dot(grad_mid_b, proj_out, ROWS_BACK).astype(BF16), out_back)
    grad_heads = by_heads(
        exchange(jnp.swapaxes(grad_attended.reshape(length, ex, span), 0, 1)).reshape(
            ex * length, span
        )
    )
    quarter = width // 4
    grad_out_projection = wide_x.scatter(
        [
            dot(attended_s[:, j * quarter : (j + 1) * quarter], grad_mid_b, SUM_ROWS).reshape(
                count // 4, rows, width
            )
            for j in range(4)
        ]
    )
    grad_queries, grad_keys, grad_values = attend_back(
        queries, key_rows, values, weights_f, attended_h, grad_heads
    )
    flat = (ex * length, span)
    grad_qscaled = rotate(grad_queries, cosine, sine_table, True).reshape(flat)
    grad_kscaled = rotate(grad_keys, cosine, sine_table, True).reshape(flat)
    up_q, up_k = grad_qscaled * gain_q, grad_kscaled * gain_k
    along = jnp.stack([jnp.sum(up_q * query_normed, axis=-1), jnp.sum(up_k * key_normed, axis=-1)])
    along = (grid.group_sum(along) / width)[:, :, None]
    grad_projected = jnp.concatenate(
        [
            query_factor * (up_q - query_normed * along[0]),
            key_factor * (up_k - key_normed * along[1]),
            grad_values.reshape(flat),
        ],
        axis=1,
    ).astype(BF16)
    mid = width // 2
    hidden1_s = reorder(hidden1_g, dp_source)
    grad_proj = grid.dp_scatter(
        [
            dot(hidden1_s[:, h * mid : (h + 1) * mid], grad_projected, SUM_ROWS).reshape(
                grid.size["y"], 2, block, 3 * span
            )
            for h in range(2)
        ]
    )
    grad_proj = exchange(grad_proj.astype(BF16).reshape(ex, rows, 3 * span)).astype(F32)
    grad_in_projection = (
        grad_proj.reshape(ex, rows, 3, span).transpose(1, 2, 0, 3).reshape(rows, 3 * width)
    )
    grad_hidden1 = dot(grad_projected, proj, ROWS_BACK).astype(BF16)
    grad_hidden1 = jnp.sum(exchange(grad_hidden1.reshape(ex, length, width)).astype(F32), axis=0)
    own = lax.dynamic_slice_in_dim(normed1_g, group * length, length, 0)
    own_factor = lax.dynamic_slice_in_dim(factor1, group * length, length, 0)
    gain_one = jnp.sum(grad_hidden1 * own, axis=0)
    input_grad = grad_middle + normalize_back(grad_hidden1 * gains[0], own, own_factor)

    def widen(values):
        return lax.dynamic_update_slice_in_dim(jnp.zeros((width,), F32), values, group * span, 0)

    grad_gain_part = jnp.stack(
        [
            gain_one,
            grad_gain_moe,
            widen(jnp.sum(grad_qscaled * query_normed, axis=0)),
            widen(jnp.sum(grad_kscaled * key_normed, axis=0)),
        ]
    )
    last = jnp.concatenate(
        [
            jnp.swapaxes(grad_gain_part.reshape(4, count, rows), 0, 1).reshape(count, -1),
            grad_router_part.reshape(count, -1),
        ],
        axis=1,
    )
    last = grid.small_scatter(last.reshape(count, -1, 128 if last.shape[1] % 128 == 0 else 64))
    last = last.reshape(-1)
    grad_norm_gains = last[: 4 * rows].reshape(4, rows)
    grad_router = last[4 * rows :].reshape(rows, expert_count)
    return (
        block_out,
        input_grad,
        grad_in_projection,
        grad_out_projection,
        grad_router,
        grad_norm_gains,
        grad_expert_in,
        grad_expert_down,
    )


def solution(mesh):
    both = P(AXES, None)
    split = P("expert", "dp", None)
    in_specs = (both,) * 8 + (P(None, AXES), split, split)
    out_specs = (both,) * 5 + (P(None, AXES), split, split)
    return jax.shard_map(
        per_device, mesh=mesh, in_specs=in_specs, out_specs=out_specs, check_vma=False
    )
```

```python
import functools

import jax
import jax.numpy as jnp
import numpy as np
from jax import lax
from jax.experimental import pallas as pl
from jax.experimental.pallas import tpu as pltpu
from jax.sharding import PartitionSpec as P

HEADS = 16
HEAD_DIM = 128
EPSILON = 1e-05
ROPE_BASE = 10000.0
MASKED = -1e30
AXES = ("dp", "expert")
BF16 = jnp.bfloat16
F32 = jnp.float32
ROWS_BACK = (((1,), (1,)), ((), ()))
SUM_ROWS = (((0,), (0,)), ((), ()))


def dot(left, right, dims=(((1,), (0,)), ((), ()))):
    return lax.dot_general(left, right, dims, preferred_element_type=F32)


def after(value, *others):
    return lax.optimization_barrier((value,) + others)[0] if others else value


class Flow:
    def __init__(self, steps):
        self.steps, self.hops, self.result = steps, [], None
        next(steps)

    def go(self, *events):
        if self.result is not None:
            return
        try:
            self.hops.append(self.steps.send(events))
        except StopIteration as stop:
            self.result = stop.value
            assert self.result is not None

    def finish(self):
        while self.result is None:
            self.go()
        return self.result


def normalize(tensor):
    factor = lax.rsqrt(jnp.mean(tensor * tensor, axis=-1, keepdims=True) + EPSILON)
    return (tensor * factor, factor)


def normalize_back(upstream, normed, factor):
    return factor * (upstream - normed * jnp.mean(upstream * normed, axis=-1, keepdims=True))


def rope_tables(length):
    half_dim = HEAD_DIM // 2
    position = jnp.arange(length).astype(F32)
    frequency = ROPE_BASE ** (-2.0 * jnp.arange(half_dim).astype(F32) / HEAD_DIM)
    angles = position[:, None] * frequency[None, :]
    return (jnp.cos(angles), jnp.sin(angles))


def rotate(tensor, cosine, sine_table, inverse):
    half = HEAD_DIM // 2
    first_half, second_half = tensor[..., :half], tensor[..., half:]
    cosine, sine_table = cosine[None, :, None, :], sine_table[None, :, None, :]
    if inverse:
        sine_table = -sine_table
    return jnp.concatenate(
        [
            first_half * cosine - second_half * sine_table,
            second_half * cosine + first_half * sine_table,
        ],
        axis=-1,
    )


class Grid:
    def __init__(self):
        self.dp = lax.axis_size("dp")
        self.ex = lax.axis_size("expert")
        self.count = self.dp * self.ex
        self.size = {"z": 4, "y": self.dp // 4, "x": self.ex // 2, "c": 2}
        self.size["A"], self.size["B"] = self.size["y"], self.size["x"]
        self.swap = self.size["x"] == self.size["y"]
        d, e = lax.axis_index("dp"), lax.axis_index("expert")
        self.linear = d * self.ex + e
        ny = self.size["y"]
        self.at = {"z": d // ny, "y": d % ny, "x": e // 2, "c": e % 2}

    def real(self, axis, core):
        if axis in "AB":
            return "yx"[(axis == "B") != (core == 1 and self.swap)]
        return axis

    def index(self, p):
        return (p["z"] * self.size["y"] + p["y"]) * self.ex + p["x"] * 2 + p["c"]

    def move(self, value, axis, kind="pair"):
        s = self.size
        if s[axis] == 2:
            moves = {0: 1, 1: 0}
        else:
            moves = {
                "pair": {0: 1, 1: 0, 2: 3, 3: 2},
                "mid": {1: 2, 2: 1},
                "out": {1: 0, 2: 3},
                "in": {0: 1, 3: 2},
            }[kind]
        pairs = []
        for i in range(self.count):
            d, e = divmod(i, self.ex)
            here = {"z": d // s["y"], "y": d % s["y"], "x": e // 2, "c": e % 2}
            line = self.real(axis, here["c"])
            if here[line] in moves:
                pairs.append((i, self.index({**here, line: moves[here[line]]})))
        return lax.ppermute(value, AXES, pairs)

    def middle(self, axis):
        at = self.at[self.real(axis, 0)]
        if axis in "AB" and self.swap:
            at = jnp.where(self.at["c"] == 0, at, self.at[self.real(axis, 1)])
        return (at == 1) | (at == 2)

    def slots(self, axis):
        n = self.size[axis]
        table = {
            1: [[0]],
            2: [[0, 1], [1, 0]],
            4: [[0, 1, 2, 3], [1, 0, 2, 3], [2, 3, 1, 0], [3, 2, 1, 0]],
        }[n]
        return jnp.asarray(np.array(table, np.int32))[self.at[axis]]

    def sources(self):
        c, y, x, z = [self.slots(a) for a in "cyxz"]
        z, c = z.reshape(2, 1, 1, 1, 2), c.reshape(1, -1, 1, 1, 1)
        along_b, along_a = (1, 1, -1, 1, 1), (1, 1, 1, -1, 1)
        xs, ys = x.reshape(along_b), y.reshape(along_a)
        if self.swap:
            xs = jnp.where(c == 0, xs, x.reshape(along_a))
            ys = jnp.where(c == 0, ys, y.reshape(along_b))
        return ((z * self.size["y"] + ys) * self.ex + xs * 2 + c).reshape(-1)

    def dp_sources(self):
        z = self.slots("z").reshape(2, 1, 2)
        return (z * self.size["y"] + self.slots("y").reshape(1, -1, 1)).reshape(-1)

    def line_gather(self, value, axis):
        n = self.size[axis]
        if n == 1:
            return [value]
        pair = self.move(value, axis)
        if n == 2:
            return [value, pair]
        m0, m1 = self.move(value, axis, "mid"), self.move(pair, axis, "mid")
        o0, o1 = self.move(m0, axis, "out"), self.move(m1, axis, "out")
        mid = self.middle(axis)
        return [value, pair, jnp.where(mid, m0, o0), jnp.where(mid, m1, o1)]

    def line_reduce(self, slots, axis, kind=BF16):
        n = self.size[axis]
        slots = [slots[0].astype(F32)] + list(slots[1:])

        def sent(value, *way):
            return self.move(value.astype(kind), axis, *way).astype(F32)

        if n == 1:
            return slots[0]
        if n == 2:
            return slots[0] + sent(slots[1])
        m3 = sent(slots[3] + sent(slots[3], "in"), "mid")
        m2 = sent(slots[2] + sent(slots[2], "in"), "mid")
        return slots[0] + m2 + sent(slots[1] + m3)

    def z_hops(self, value, events):
        value = after(value, *events)
        pair, m0 = self.move(value, "z"), self.move(value, "z", "mid")
        events = yield (pair, m0)
        pair, m0 = after((pair, m0), *events)
        m1, o0 = self.move(pair, "z", "mid"), self.move(m0, "z", "out")
        events = yield (m1, o0)
        mid = self.middle("z")
        near = jnp.stack([value, pair])
        m1, near = after((m1, near), *events)
        o1 = self.move(m1, "z", "out")
        return near, lambda o1: jnp.stack([jnp.where(mid, m0, o0), jnp.where(mid, m1, o1)]), o1

    def gather(self, value):
        events = yield
        near, far, o1 = yield from self.z_hops(value, events)
        na = self.line_gather(near, "A")
        events = yield (o1, *na[1:])
        o1, na = after((o1, na), *events)
        fa, nb = self.line_gather(far(o1), "A"), [self.line_gather(na[0], "B")]
        events = yield (*fa[1:], *nb[0][1:])
        na, fa = after((na, fa), *events)
        nb += [self.line_gather(v, "B") for v in na[1:]]
        fb = [self.line_gather(fa[0], "B")]
        events = yield (*nb[1][1:], *fb[0][1:])
        nb, fa = after((nb, fa), *events)
        fb += [self.line_gather(v, "B") for v in fa[1:]]
        count = self.size["B"]
        block = jnp.concatenate([row[i] for i in range(count) for row in nb])
        nc = self.line_gather(block, "c")
        events = yield (*fb[1][1:], *nc[1:])
        fb = after(fb, *events)
        block = jnp.concatenate([row[i] for i in range(count) for row in fb])
        return nc + self.line_gather(block, "c")

    def lines(self, total):
        return [total[i] for i in range(total.shape[0])]

    def z_sum(self, near, far, events):
        def sent(value, way="pair"):
            return self.move(value.astype(BF16), "z", way)

        near, far = after((near, far), *events)
        o3, o2 = sent(far[1], "in"), sent(far[0], "in")
        events = yield (o3, o2)
        far, o3, o2 = after((far, o3, o2), *events)
        m3, m2 = sent(far[1] + o3.astype(F32), "mid"), sent(far[0] + o2.astype(F32), "mid")
        events = yield (m3, m2)
        near, m3, m2 = after((near, m3, m2), *events)
        pair = sent(near[1] + m3.astype(F32))
        events = yield (pair,)
        return near[0] + m2.astype(F32) + after(pair, *events).astype(F32)

    def unfold(self, total):
        return total.reshape((self.size["B"], self.size["A"], 2) + total.shape[1:])

    def scatter(self, groups, kind=F32):
        events = yield
        far, near = after((groups[2:], groups[:2]), *events)
        far = self.unfold(self.line_reduce(far, "c").astype(kind))
        near = self.unfold(self.line_reduce(near, "c").astype(kind))
        for axis in "BA":
            events = yield (far, near)
            far, near = after((far, near), *events)
            far = self.line_reduce(self.lines(far), axis).astype(kind)
            near = self.line_reduce(self.lines(near), axis).astype(kind)
        events = yield (far, near)
        return (yield from self.z_sum(near, far, events))

    def scatter_early(self, groups, late):
        yield
        far = self.unfold(self.line_reduce(groups[2:], "c"))
        yield (far,)
        far = self.line_reduce(self.lines(far), "B")
        yield (far,)
        far = self.line_reduce(self.lines(far), "A")
        near = self.unfold(self.line_reduce(late(), "c"))
        events = yield (far, near)
        near = self.line_reduce(self.lines(after(near, *events)), "B")
        o3, o2 = self.move(far[1].astype(BF16), "z", "in"), self.move(far[0].astype(BF16), "z", "in")
        events = yield (near, o3, o2)
        near, o3, o2 = after((near, o3, o2), *events)
        near = self.line_reduce(self.lines(near), "A")
        m3 = self.move((far[1] + o3.astype(F32)).astype(BF16), "z", "mid")
        m2 = self.move((far[0] + o2.astype(F32)).astype(BF16), "z", "mid")
        events = yield (near, m3, m2)
        near, m3, m2 = after((near, m3, m2), *events)
        pair = self.move((near[1] + m3.astype(F32)).astype(BF16), "z")
        events = yield (pair,)
        return near[0] + m2.astype(F32) + after(pair, *events).astype(F32)

    def dp_gather(self, value):
        events = yield
        near, far, o1 = yield from self.z_hops(value, events)
        ny = self.line_gather(near, "y")
        events = yield (o1, *ny[1:])
        fy = self.line_gather(far(after(o1, *events)), "y")
        events = yield (*fy[1:],)
        z, y = self.slots("z"), self.slots("y")
        n = value.shape[0]
        whole = jnp.zeros((n * self.dp,) + value.shape[1:], value.dtype)
        for h, line in enumerate((ny, fy)):
            for j, got in enumerate(line):
                for k in range(2):
                    place = (z[2 * h + k] * self.size["y"] + y[j]) * n
                    whole = lax.dynamic_update_slice_in_dim(whole, got[k], place, 0)
        return whole

    def dp_scatter(self, halves):
        events = yield
        near, far = after(halves, *events)
        far = self.line_reduce(self.lines(far), "y")
        events = yield (far,)
        far, near = after((far, near), *events)
        near = self.line_reduce(self.lines(near), "y")
        return (yield from self.z_sum(near, far, ()))

    def flip(self, value, bit):
        return lax.ppermute(value, AXES, [(i, i ^ bit) for i in range(self.count)])

    def small_gather(self, value):
        held, bit = value[None], 1
        while bit < self.count:
            events = yield (held,)
            held = after(held, *events)
            held = jnp.concatenate([held, self.flip(held, bit)])
            bit *= 2
        return held[self.linear ^ jnp.arange(self.count)]

    def small_scatter(self, value):
        held = value[self.linear ^ jnp.arange(self.count)]
        bit = self.count // 2
        while bit:
            held = held[:bit] + self.flip(held[bit:], bit)
            bit //= 2
        return held[0]

    def group_sum(self, value):
        total = value
        for r in range(1, self.ex):
            total = total + self.flip(value, r)
        return total


def exchange(value):
    return lax.all_to_all(value, "expert", split_axis=0, concat_axis=0, tiled=True)


def moe_kernel(ff, local, x_ref, lift_ref, gate_ref, w_ref, grad_ref, act_ref, sum_ref, back_ref):
    x = x_ref[...]
    per = 128 // ff
    lane = lax.broadcasted_iota(jnp.int32, (x.shape[0], 128), 1)
    for b in range(local // per):
        wide, narrow = pl.ds(256 * b, 256), pl.ds(128 * b, 128)
        pre_act = dot(x, w_ref[:, wide])
        gate_part, up_part = pre_act[:, :128], pre_act[:, 128:]
        spread = jnp.broadcast_to(gate_ref[:, pl.ds(b * per, 1)], lane.shape)
        for k in range(1, per):
            spread = jnp.where(
                lane < k * ff,
                spread,
                jnp.broadcast_to(gate_ref[:, pl.ds(b * per + k, 1)], lane.shape),
            )
        lifted = lift_ref[:, narrow]
        sig = 1.0 / (1.0 + jnp.exp(-gate_part))
        act = (gate_part * sig * up_part).astype(BF16).astype(F32)
        act_ref[:, narrow] = (act * spread).astype(BF16)
        terms = act * lifted
        for k in range(per):
            mine = jnp.where((lane >= k * ff) & (lane < (k + 1) * ff), terms, 0.0)
            sum_ref[:, pl.ds(b * per + k, 1)] = jnp.sum(mine, axis=1, keepdims=True)
        grad_act = lifted * spread
        grad_gate = grad_act * up_part * sig * (1.0 + gate_part * (1.0 - sig))
        grad_ref[:, pl.ds(256 * b, 128)] = grad_gate.astype(BF16)
        grad_ref[:, pl.ds(256 * b + 128, 128)] = (grad_act * gate_part * sig).astype(BF16)
    back_ref[...] = dot(grad_ref[...], w_ref[...], ROWS_BACK).astype(back_ref.dtype)


def moe_rows(x, lifted, gates, weight, ff, start, total, kind):
    width, wide = weight.shape
    local = gates.shape[1]
    tile = 256 if total % 256 == 0 else 128
    skip = start // tile
    row = lambda n: pl.BlockSpec((tile, n), lambda i: (i + skip, 0))
    out = lambda n: pl.BlockSpec((tile, n), lambda i: (i, 0))
    return pl.pallas_call(
        functools.partial(moe_kernel, ff, local),
        grid=(total // tile,),
        in_specs=[
            row(width),
            row(wide // 2),
            row(local),
            pl.BlockSpec((width, wide), lambda i: (0, 0)),
        ],
        out_specs=[out(wide), out(wide // 2), out(local), out(width)],
        out_shape=[
            jax.ShapeDtypeStruct((total, wide), BF16),
            jax.ShapeDtypeStruct((total, wide // 2), BF16),
            jax.ShapeDtypeStruct((total, local), F32),
            jax.ShapeDtypeStruct((total, width), kind),
        ],
        compiler_params=pltpu.CompilerParams(vmem_limit_bytes=56 * 1024 * 1024),
        cost_estimate=pl.CostEstimate(
            flops=4 * total * width * wide, bytes_accessed=total * width * 12, transcendentals=0
        ),
    )(x, lifted, gates, weight)


def deal_kernel(dp, in_ref, out_ref):
    for p in range(dp):
        out_ref[p] = in_ref[0, :, 128 * p : 128 * (p + 1)]


def deal(expert_in, dp):
    local, rows, wide = expert_in.shape
    return pl.pallas_call(
        functools.partial(deal_kernel, dp),
        grid=(local, 2),
        in_specs=[pl.BlockSpec((1, rows, wide // 2), lambda e, g: (e, 0, g))],
        out_specs=pl.BlockSpec((dp, rows, 128), lambda e, g: (0, 0, 2 * e + g)),
        out_shape=jax.ShapeDtypeStruct((dp, rows, local * 256), expert_in.dtype),
        compiler_params=pltpu.CompilerParams(vmem_limit_bytes=32 * 1024 * 1024),
    )(expert_in)


def undeal_kernel(parts, each, *refs):
    out_ref = refs[parts]
    e, g = pl.program_id(0), pl.program_id(1)
    for h in range(parts):

        @pl.when(e // each == h)
        def _():
            column = pl.multiple_of((2 * (e - h * each) + g) * 128, 128)
            for p in range(refs[h].shape[0]):
                piece = refs[h][p, :, pl.ds(column, 128)]
                out_ref[0, :, 128 * p : 128 * (p + 1)] = piece.astype(F32)


def undeal(pieces):
    parts = len(pieces)
    dp, rows, wide = pieces[0].shape
    each = wide // 256
    return pl.pallas_call(
        functools.partial(undeal_kernel, parts, each),
        grid=(parts * each, 2),
        in_specs=[pl.BlockSpec((dp, rows, wide), lambda e, g: (0, 0, 0))] * parts,
        out_specs=pl.BlockSpec((1, rows, dp * 128), lambda e, g: (e, 0, g)),
        out_shape=jax.ShapeDtypeStruct((parts * each, rows, 2 * dp * 128), F32),
        compiler_params=pltpu.CompilerParams(vmem_limit_bytes=48 * 1024 * 1024),
    )(*pieces)


def deal_narrow(expert_in, dp):
    local, rows, wide = expert_in.shape
    ff = wide // 2 // dp
    split = expert_in.reshape(local * ff // 128, 128 // ff, rows, 2, dp, ff)
    return split.transpose(4, 2, 0, 3, 1, 5).reshape(dp, rows, 2 * local * ff)


def undeal_narrow(pieces, ff):
    whole = jnp.concatenate(pieces, axis=2)
    dp, rows, wide = whole.shape
    whole = whole.reshape(dp, rows, wide // 256, 2, 128 // ff, ff).astype(F32)
    return whole.transpose(2, 4, 1, 3, 0, 5).reshape(wide // 2 // ff, rows, 2 * dp * ff)


def swap(value):
    return lax.all_to_all(value, "dp", split_axis=0, concat_axis=0, tiled=True)


def masked(segment):
    length = segment.shape[1]
    row_index = lax.broadcasted_iota(jnp.int32, (length, length), 0)
    col_index = lax.broadcasted_iota(jnp.int32, (length, length), 1)
    return (segment[:, :, None] == segment[:, None, :]) & (col_index <= row_index)[None]


def attend(queries, key_rows, values, allowed):
    raw = jnp.einsum("sqhd,skhd->shqk", queries, key_rows, preferred_element_type=F32)
    scores = jnp.where(allowed[:, None], raw * HEAD_DIM ** (-0.5), MASKED)
    row_max = jnp.max(scores, axis=-1, keepdims=True)
    exp_terms = jnp.exp(scores - row_max)
    weights_f = exp_terms / jnp.sum(exp_terms, axis=-1, keepdims=True)
    attended = jnp.einsum(
        "shqk,skhd->sqhd", weights_f.astype(BF16), values, preferred_element_type=F32
    )
    return (attended.astype(BF16), weights_f)


def attend_back(queries, key_rows, values, weights_f, attended, grad_heads):
    weights_b = weights_f.astype(BF16)
    grad_values = jnp.einsum("shqk,sqhd->skhd", weights_b, grad_heads, preferred_element_type=F32)
    grad_weights = jnp.einsum("sqhd,skhd->shqk", grad_heads, values, preferred_element_type=F32)
    row_delta = jnp.sum(grad_heads.astype(F32) * attended.astype(F32), axis=-1)
    row_delta = jnp.swapaxes(row_delta, 1, 2)[..., None]
    grad_scores = (weights_f * (grad_weights - row_delta) * HEAD_DIM ** (-0.5)).astype(BF16)
    grad_queries = jnp.einsum(
        "shqk,skhd->sqhd", grad_scores, key_rows, preferred_element_type=F32
    )
    grad_keys = jnp.einsum("shqk,sqhd->skhd", grad_scores, queries, preferred_element_type=F32)
    return (grad_queries, grad_keys, grad_values)


def per_device(
    tokens,
    cotangent,
    segments,
    routes,
    slot_index,
    in_projection,
    out_projection,
    router_weight,
    norm_gains,
    expert_in,
    expert_down,
):
    grid = Grid()
    length, width = tokens.shape
    count, dp, ex = grid.count, grid.dp, grid.ex
    local = expert_in.shape[0]
    expert_count = ex * local
    ff = expert_down.shape[1]
    rows = width // count
    block = width // dp
    heads = HEADS // ex
    span = heads * HEAD_DIM
    group = lax.axis_index("expert")
    stage = lax.axis_index("dp")
    cosine, sine_table = rope_tables(length)
    source = grid.sources()
    ids = jnp.arange(count, dtype=source.dtype)
    back = jnp.sum(jnp.where(source[None, :] == ids[:, None], ids[None, :], 0), axis=1)
    dp_source = grid.dp_sources()
    chunks = 1 if length * count <= 4096 else length * count // 4096
    size = length // chunks

    def reorder(tensor, order):
        parts = order.shape[0]
        return jnp.take(
            tensor.reshape(tensor.shape[0], parts, width // parts), order, axis=1
        ).reshape(tensor.shape[0], width)

    small = jnp.concatenate(
        [
            norm_gains.reshape(-1),
            router_weight.reshape(-1),
            segments.astype(BF16).reshape(-1),
        ]
    )
    small = jnp.pad(small, (0, -small.shape[0] % 128)).reshape(-1, 128)
    small_flow = Flow(grid.small_gather(small))
    small_flow.go()

    piece = in_projection.reshape(rows, 3, ex, span).transpose(2, 0, 1, 3)
    piece = exchange(piece.reshape(ex, rows, 3 * span)).reshape(block, 3 * span)
    tokens_g = exchange(
        after(jnp.broadcast_to(tokens[None], (ex, length, width)), piece)
    )
    dense = Flow(grid.dp_gather(piece))
    out_flow = Flow(grid.gather(out_projection))
    cot_flow = Flow(grid.gather(cotangent[:size]))
    dealt = (deal if ff == 128 else deal_narrow)(after(expert_in, piece), dp)
    weight_down = expert_down.reshape(local * ff, width)

    quarter = local * ff // 2
    weights = []

    def fetch(*events):
        columns = slice(len(weights) * quarter, (len(weights) + 1) * quarter)
        weights.append(swap(after(dealt[:, :, columns], *events)).reshape(width, quarter))

    dense.go()
    small_flow.go(piece)
    out_flow.go(*dense.hops[0])
    cot_flow.go(*dense.hops[0])
    small_flow.go(*dense.hops[0])
    dense.go(tokens_g)
    out_flow.go(*dense.hops[1])
    cot_flow.go(*dense.hops[1])
    small_flow.go(*dense.hops[1])
    dense.go(dealt, *out_flow.hops[0], *cot_flow.hops[0])
    fetch(*dense.hops[2])
    out_flow.go(*dense.hops[2])
    small_flow.go(*dense.hops[2])
    dense.go(*out_flow.hops[1], *cot_flow.hops[1])
    cot_flow.go(*dense.hops[3])
    out_flow.go(*dense.hops[3], *out_flow.hops[2])
    proj = after(dense.finish(), weights[0])
    fetch(*dense.hops[3])
    small = small_flow.finish().reshape(count, -1)
    cuts = np.cumsum([4 * rows, rows * expert_count, length])
    all_gains, all_router, all_segments, _ = jnp.split(small, cuts, axis=1)
    gains = jnp.swapaxes(all_gains.reshape(count, 4, rows), 0, 1).reshape(4, width).astype(F32)
    router = all_router.reshape(width, expert_count)
    segment = lax.dynamic_slice_in_dim(
        all_segments.reshape(dp, ex, length), stage, 1, 0
    )[0].astype(jnp.int32)
    allowed = masked(segment)
    gain_q = lax.dynamic_slice_in_dim(gains[2], group * span, span)
    gain_k = lax.dynamic_slice_in_dim(gains[3], group * span, span)

    normed1_g, factor1 = normalize(tokens_g.reshape(ex * length, width).astype(F32))
    hidden1_g = (normed1_g * gains[0]).astype(BF16)
    projected = dot(hidden1_g, proj)
    query_raw, key_raw = projected[:, :span], projected[:, span : 2 * span]
    squares = jnp.stack([jnp.sum(query_raw**2, axis=-1), jnp.sum(key_raw**2, axis=-1)])
    squares = grid.group_sum(squares)
    squares = after(squares, weights[1], *out_flow.hops[3], *cot_flow.hops[2])
    fetch(squares)
    out_flow.go(squares)
    cot_flow.go(squares)
    factors = lax.rsqrt(squares / width + EPSILON)[:, :, None]
    query_factor, key_factor = factors[0], factors[1]
    proj_out = jnp.concatenate(out_flow.finish()).reshape(width, width)
    query_normed, key_normed = query_raw * query_factor, key_raw * key_factor

    def by_heads(tensor):
        return tensor.reshape(ex, length, heads, HEAD_DIM)

    queries = rotate(by_heads(query_normed * gain_q), cosine, sine_table, False).astype(BF16)
    key_rows = rotate(by_heads(key_normed * gain_k), cosine, sine_table, False).astype(BF16)
    values = by_heads(projected[:, 2 * span :].astype(BF16))
    attended_h, weights_f = attend(queries, key_rows, values, allowed)
    cot_flow.go(attended_h, *cot_flow.hops[3])
    attended = exchange(attended_h.reshape(ex, length, span))
    attended = after(attended, weights[2])
    fetch(attended)
    attended_c = jnp.swapaxes(attended, 0, 1).reshape(length, width)
    attended_s = reorder(attended_c, source)
    residual = tokens.astype(F32)
    middle = residual + dot(attended_s, proj_out)
    normed2, factor2 = normalize(middle)
    hidden2 = (normed2 * gains[1]).astype(BF16)
    hidden2 = after(hidden2, weights[3], *cot_flow.hops[4])
    weight_in = jnp.concatenate(weights, axis=1)
    router_probs = jax.nn.softmax(dot(hidden2, router), axis=-1)
    grad_top = cotangent.astype(F32)
    named = jnp.arange(expert_count, dtype=jnp.int32)
    chosen = jnp.any(routes[:, :, None] == named[None, None, :], axis=1)
    gates = jnp.where(chosen, router_probs, 0.0).reshape(-1, 128)

    hid_flow = Flow(grid.gather(hidden2[:size]))
    gate_flow = Flow(grid.small_gather(gates))
    cot_flow.go(hidden2)
    hid_flow.go()
    gate_flow.go()
    hid_flow.go(weight_in, *cot_flow.hops[5])
    cot_flow.go(*hid_flow.hops[0])
    gate_flow.go(*hid_flow.hops[0])
    for k in (1, 2, 3):
        gate_flow.go(*hid_flow.hops[k])
        hid_flow.go(*gate_flow.hops[k])
    gates = gate_flow.finish().reshape(count, length, expert_count)
    gates = lax.dynamic_slice_in_dim(gates[source], group * local, local, 2)
    back_flows, mix_flows, probs_parts = [], [], []
    grad_in_w, grad_down_w = [0.0] * 4, 0.0
    for i in range(chunks):
        if i:
            ready = (back_flows[-1].finish(), mix_flows[-1].finish(), grad_in_w, grad_down_w)
            part = slice(i * size, (i + 1) * size)
            cot_flow = Flow(grid.gather(after(cotangent[part], *ready)))
            hid_flow = Flow(grid.gather(after(hidden2[part], *ready)))
        cot = jnp.concatenate(cot_flow.finish()).reshape(-1, width)
        lifted = dot(cot, weight_down, ROWS_BACK)
        while len(hid_flow.hops) < 5:
            hid_flow.go()
        hid_flow.go(lifted)
        hid = jnp.concatenate(hid_flow.finish()).reshape(-1, width)
        total = hid.shape[0]
        gate_dense = gates[:, i * size : (i + 1) * size].reshape(total, local)
        part = total // 4
        slotted = (count // 4, size, width)
        done = [None] * 4

        def run(j, *events):
            kind = BF16 if j % 2 else F32
            gates = after(gate_dense, *events)
            done[j] = moe_rows(hid, lifted, gates, weight_in, ff, j * part, part, kind)
            return done[j][3].reshape(slotted)

        far = [None, None, None, run(3)]
        far[2] = run(2, done[3][3])
        near = [None, None]
        flow = Flow(grid.scatter_early(far, lambda: near))
        flow.go()
        near[1] = run(1, *flow.hops[0])
        flow.go()
        near[0] = run(0, *flow.hops[1], done[1][3])
        flow.go()
        last = done[0][3]
        acts = [d[1] for d in done]
        grad_pre = jnp.concatenate([d[0] for d in done])
        wide = 2 * local * ff // 4
        columns = [grad_pre[:, q * wide : (q + 1) * wide] for q in range(4)]

        def weigh(q, *events):
            part = dot(after(hid, *events), columns[q], SUM_ROWS)
            grad_in_w[q] += part
            return part

        def mixed(j, *events):
            return dot(after(acts[j], *events), weight_down).astype(BF16).reshape(slotted)

        first = weigh(0, last)
        flow.go(first)
        mix = [None, None, mixed(2, *flow.hops[2]), mixed(3, *flow.hops[2])]
        flow.go(mix[2], mix[3])
        mix[0], mix[1] = mixed(0, *flow.hops[3]), mixed(1, *flow.hops[3])
        second = weigh(1, *flow.hops[3])
        if i == chunks - 1:
            gone = [g.astype(BF16).reshape(dp, block, wide) for g in grad_in_w[:1]]
            home = [swap(gone[0])]
            flow.go(mix[0], mix[1], second, home[0])
        else:
            flow.go()
        third = weigh(2, *flow.hops[4])
        fourth = weigh(3, *flow.hops[4])
        flow.go(third, fourth)
        back_flows.append(flow)
        mix_flow = Flow(grid.scatter(mix, BF16))
        mix_flow.go(*flow.hops[4])
        mix_flows.append(mix_flow)
        probs_part = jnp.concatenate([d[2] for d in done])
        probs_parts.append(probs_part.reshape(count, size, local))
        act_gated = jnp.concatenate(acts)
        if i < chunks - 1:
            grad_down_w += dot(act_gated, cot, SUM_ROWS)

    def send(q, *events):
        home.append(swap(after(grad_in_w[q].astype(BF16).reshape(dp, block, wide), *events)))

    probs_all = jnp.concatenate(probs_parts, axis=1)[back]
    place = (jnp.arange(expert_count) // local == group).astype(F32)
    probs_wide = (jnp.tile(probs_all, (1, 1, ex)) * place).reshape(
        count, length * expert_count // 128, 128
    )
    grad_probs = grid.small_scatter(probs_wide).reshape(length, expert_count)
    grad_probs = jnp.where(chosen, grad_probs, 0.0)

    grad_logits = (
        router_probs * (grad_probs - jnp.sum(router_probs * grad_probs, axis=-1, keepdims=True))
    ).astype(BF16)
    grad_router_part = dot(hidden2, grad_logits, SUM_ROWS)
    grad_hidden2 = jnp.concatenate([f.finish() for f in back_flows]) + dot(grad_logits, router, ROWS_BACK)
    grad_gain_moe = jnp.sum(grad_hidden2 * normed2, axis=0)
    grad_middle = grad_top + normalize_back(grad_hidden2 * gains[1], normed2, factor2)
    grad_mid_b = grad_middle.astype(BF16)
    grad_attended = reorder(dot(grad_mid_b, proj_out, ROWS_BACK).astype(BF16), back)
    grad_heads = by_heads(
        exchange(jnp.swapaxes(grad_attended.reshape(length, ex, span), 0, 1)).reshape(
            ex * length, span
        )
    )
    quarter = width // 4
    out_parts = [
        dot(attended_s[:, j * quarter : (j + 1) * quarter], grad_mid_b, SUM_ROWS).reshape(
            count // 4, rows, width
        )
        for j in range(4)
    ]
    out_flow = Flow(grid.scatter(out_parts))
    send(1, grad_mid_b)
    mix_flow.go(grad_mid_b)
    grad_heads = after(grad_heads, *mix_flow.hops[1])
    send(2, grad_heads)
    mix_flow.go(grad_heads)
    out_flow.go(grad_heads)
    grad_queries, grad_keys, grad_values = attend_back(
        queries, key_rows, values, weights_f, attended_h, grad_heads
    )
    flat = (ex * length, span)
    grad_qscaled = rotate(grad_queries, cosine, sine_table, True).reshape(flat)
    grad_kscaled = rotate(grad_keys, cosine, sine_table, True).reshape(flat)
    up_q, up_k = grad_qscaled * gain_q, grad_kscaled * gain_k
    along = jnp.stack([jnp.sum(up_q * query_normed, axis=-1), jnp.sum(up_k * key_normed, axis=-1)])
    along = (grid.group_sum(along) / width)[:, :, None]
    along = after(along, *mix_flow.hops[2], *out_flow.hops[0])
    mix_flow.go(along)
    out_flow.go(along)
    grad_projected = jnp.concatenate(
        [
            query_factor * (up_q - query_normed * along[0]),
            key_factor * (up_k - key_normed * along[1]),
            grad_values.reshape(flat),
        ],
        axis=1,
    ).astype(BF16)
    mid = width // 2
    hidden1_s = reorder(hidden1_g, dp_source)
    proj_flow = Flow(
        grid.dp_scatter(
            [
                dot(hidden1_s[:, h * mid : (h + 1) * mid], grad_projected, SUM_ROWS).reshape(
                    grid.size["y"], 2, block, 3 * span
                )
                for h in range(2)
            ]
        )
    )
    proj_flow.go(home[1], home[2])
    send(3, grad_projected)
    proj_flow.go(*mix_flow.hops[3], *out_flow.hops[1])
    mix_flow.go(*proj_flow.hops[0])
    out_flow.go(*proj_flow.hops[0])
    proj_flow.go(*mix_flow.hops[4], *out_flow.hops[2])
    mix_flow.go(*proj_flow.hops[1])
    out_flow.go(*proj_flow.hops[1])
    grad_down_w += dot(after(act_gated, *proj_flow.hops[0]), cot, SUM_ROWS)
    proj_flow.go(*mix_flow.hops[5], *out_flow.hops[3])
    out_flow.go(*proj_flow.hops[2])
    grad_proj = proj_flow.finish()
    block_out = middle + jnp.concatenate([f.finish() for f in mix_flows])
    grad_out_projection = out_flow.finish()
    grad_expert_down = grad_down_w.reshape(local, ff, width)
    grad_proj = exchange(grad_proj.astype(BF16).reshape(ex, rows, 3 * span)).astype(F32)
    grad_in_projection = (
        grad_proj.reshape(ex, rows, 3, span).transpose(1, 2, 0, 3).reshape(rows, 3 * width)
    )
    grad_hidden1 = dot(grad_projected, proj, ROWS_BACK).astype(BF16)
    grad_hidden1 = jnp.sum(exchange(grad_hidden1.reshape(ex, length, width)).astype(F32), axis=0)
    own = lax.dynamic_slice_in_dim(normed1_g, group * length, length, 0)
    own_factor = lax.dynamic_slice_in_dim(factor1, group * length, length, 0)
    gain_one = jnp.sum(grad_hidden1 * own, axis=0)
    input_grad = grad_middle + normalize_back(grad_hidden1 * gains[0], own, own_factor)

    home = after(home, grad_proj)
    grad_expert_in = undeal(home) if ff == 128 else undeal_narrow(home, ff)

    def widen(values):
        return lax.dynamic_update_slice_in_dim(jnp.zeros((width,), F32), values, group * span, 0)

    grad_gain_part = jnp.stack(
        [
            gain_one,
            grad_gain_moe,
            widen(jnp.sum(grad_qscaled * query_normed, axis=0)),
            widen(jnp.sum(grad_kscaled * key_normed, axis=0)),
        ]
    )
    last = jnp.concatenate(
        [
            jnp.swapaxes(grad_gain_part.reshape(4, count, rows), 0, 1).reshape(count, -1),
            grad_router_part.reshape(count, -1),
        ],
        axis=1,
    )
    last = grid.small_scatter(last.reshape(count, -1, 128 if last.shape[1] % 128 == 0 else 64))
    last = last.reshape(-1)
    grad_norm_gains = last[: 4 * rows].reshape(4, rows)
    grad_router = last[4 * rows :].reshape(rows, expert_count)
    return (
        block_out,
        input_grad,
        grad_in_projection,
        grad_out_projection,
        grad_router,
        grad_norm_gains,
        grad_expert_in,
        grad_expert_down,
    )


def solution(mesh):
    both = P(AXES, None)
    split = P("expert", "dp", None)
    in_specs = (both,) * 8 + (P(None, AXES), split, split)
    out_specs = (both,) * 5 + (P(None, AXES), split, split)
    return jax.shard_map(
        per_device, mesh=mesh, in_specs=in_specs, out_specs=out_specs, check_vma=False
    )
```

```python
import functools

import jax
import jax.numpy as jnp
import numpy as np
from jax import lax
from jax.experimental import pallas as pl
from jax.experimental.pallas import tpu as pltpu
from jax.sharding import PartitionSpec as P

HEADS = 16
HEAD_DIM = 128
EPSILON = 1e-05
ROPE_BASE = 10000.0
MASKED = -1e30
AXES = ("dp", "expert")
BF16 = jnp.bfloat16
F32 = jnp.float32
ROWS_BACK = (((1,), (1,)), ((), ()))
SUM_ROWS = (((0,), (0,)), ((), ()))


def dot(left, right, dims=(((1,), (0,)), ((), ()))):
    return lax.dot_general(left, right, dims, preferred_element_type=F32)


def after(value, *others):
    return lax.optimization_barrier((value,) + others)[0] if others else value


class Flow:
    def __init__(self, steps):
        self.steps, self.hops, self.result = steps, [], None
        next(steps)

    def go(self, *events):
        if self.result is not None:
            return
        try:
            self.hops.append(self.steps.send(events))
        except StopIteration as stop:
            self.result = stop.value
            assert self.result is not None

    def finish(self):
        while self.result is None:
            self.go()
        return self.result


def normalize(tensor):
    factor = lax.rsqrt(jnp.mean(tensor * tensor, axis=-1, keepdims=True) + EPSILON)
    return (tensor * factor, factor)


def normalize_back(upstream, normed, factor):
    return factor * (upstream - normed * jnp.mean(upstream * normed, axis=-1, keepdims=True))


def rope_tables(length):
    half_dim = HEAD_DIM // 2
    position = jnp.arange(length).astype(F32)
    frequency = ROPE_BASE ** (-2.0 * jnp.arange(half_dim).astype(F32) / HEAD_DIM)
    angles = position[:, None] * frequency[None, :]
    return (jnp.cos(angles), jnp.sin(angles))


def rotate(tensor, cosine, sine_table, inverse):
    half = HEAD_DIM // 2
    first_half, second_half = tensor[..., :half], tensor[..., half:]
    cosine, sine_table = cosine[None, :, None, :], sine_table[None, :, None, :]
    if inverse:
        sine_table = -sine_table
    return jnp.concatenate(
        [
            first_half * cosine - second_half * sine_table,
            second_half * cosine + first_half * sine_table,
        ],
        axis=-1,
    )


class Grid:
    def __init__(self):
        self.dp = lax.axis_size("dp")
        self.ex = lax.axis_size("expert")
        self.count = self.dp * self.ex
        self.size = {"z": 4, "y": self.dp // 4, "x": self.ex // 2, "c": 2}
        self.size["A"], self.size["B"] = self.size["y"], self.size["x"]
        self.swap = self.size["x"] == self.size["y"]
        d, e = lax.axis_index("dp"), lax.axis_index("expert")
        self.linear = d * self.ex + e
        ny = self.size["y"]
        self.at = {"z": d // ny, "y": d % ny, "x": e // 2, "c": e % 2}

    def real(self, axis, core):
        if axis in "AB":
            return "yx"[(axis == "B") != (core == 1 and self.swap)]
        return axis

    def index(self, p):
        return (p["z"] * self.size["y"] + p["y"]) * self.ex + p["x"] * 2 + p["c"]

    def move(self, value, axis, kind="pair"):
        s = self.size
        if s[axis] == 2:
            moves = {0: 1, 1: 0}
        else:
            moves = {
                "pair": {0: 1, 1: 0, 2: 3, 3: 2},
                "mid": {1: 2, 2: 1},
                "out": {1: 0, 2: 3},
                "in": {0: 1, 3: 2},
            }[kind]
        pairs = []
        for i in range(self.count):
            d, e = divmod(i, self.ex)
            here = {"z": d // s["y"], "y": d % s["y"], "x": e // 2, "c": e % 2}
            line = self.real(axis, here["c"])
            if here[line] in moves:
                pairs.append((i, self.index({**here, line: moves[here[line]]})))
        return lax.ppermute(value, AXES, pairs)

    def middle(self, axis):
        at = self.at[self.real(axis, 0)]
        if axis in "AB" and self.swap:
            at = jnp.where(self.at["c"] == 0, at, self.at[self.real(axis, 1)])
        return (at == 1) | (at == 2)

    def slots(self, axis):
        n = self.size[axis]
        table = {
            1: [[0]],
            2: [[0, 1], [1, 0]],
            4: [[0, 1, 2, 3], [1, 0, 2, 3], [2, 3, 1, 0], [3, 2, 1, 0]],
        }[n]
        return jnp.asarray(np.array(table, np.int32))[self.at[axis]]

    def sources(self):
        c, y, x, z = [self.slots(a) for a in "cyxz"]
        z, c = z.reshape(2, 1, 1, 1, 2), c.reshape(1, -1, 1, 1, 1)
        along_b, along_a = (1, 1, -1, 1, 1), (1, 1, 1, -1, 1)
        xs, ys = x.reshape(along_b), y.reshape(along_a)
        if self.swap:
            xs = jnp.where(c == 0, xs, x.reshape(along_a))
            ys = jnp.where(c == 0, ys, y.reshape(along_b))
        return ((z * self.size["y"] + ys) * self.ex + xs * 2 + c).reshape(-1)

    def dp_sources(self):
        z = self.slots("z").reshape(2, 1, 2)
        return (z * self.size["y"] + self.slots("y").reshape(1, -1, 1)).reshape(-1)

    def line_gather(self, value, axis):
        n = self.size[axis]
        if n == 1:
            return [value]
        pair = self.move(value, axis)
        if n == 2:
            return [value, pair]
        m0, m1 = self.move(value, axis, "mid"), self.move(pair, axis, "mid")
        o0, o1 = self.move(m0, axis, "out"), self.move(m1, axis, "out")
        mid = self.middle(axis)
        return [value, pair, jnp.where(mid, m0, o0), jnp.where(mid, m1, o1)]

    def line_reduce(self, slots, axis, kind=BF16):
        n = self.size[axis]
        slots = [slots[0].astype(F32)] + list(slots[1:])

        def sent(value, *way):
            return self.move(value.astype(kind), axis, *way).astype(F32)

        if n == 1:
            return slots[0]
        if n == 2:
            return slots[0] + sent(slots[1])
        m3 = sent(slots[3] + sent(slots[3], "in"), "mid")
        m2 = sent(slots[2] + sent(slots[2], "in"), "mid")
        return slots[0] + m2 + sent(slots[1] + m3)

    def z_hops(self, value, events):
        value = after(value, *events)
        pair, m0 = self.move(value, "z"), self.move(value, "z", "mid")
        events = yield (pair, m0)
        pair, m0 = after((pair, m0), *events)
        m1, o0 = self.move(pair, "z", "mid"), self.move(m0, "z", "out")
        events = yield (m1, o0)
        mid = self.middle("z")
        near = jnp.stack([value, pair])
        m1, near = after((m1, near), *events)
        o1 = self.move(m1, "z", "out")
        return near, lambda o1: jnp.stack([jnp.where(mid, m0, o0), jnp.where(mid, m1, o1)]), o1

    def gather(self, value):
        events = yield
        near, far, o1 = yield from self.z_hops(value, events)
        na = self.line_gather(near, "A")
        events = yield (o1, *na[1:])
        o1, na = after((o1, na), *events)
        fa, nb = self.line_gather(far(o1), "A"), [self.line_gather(na[0], "B")]
        events = yield (*fa[1:], *nb[0][1:])
        na, fa = after((na, fa), *events)
        nb += [self.line_gather(v, "B") for v in na[1:]]
        fb = [self.line_gather(fa[0], "B")]
        events = yield (*nb[1][1:], *fb[0][1:])
        nb, fa = after((nb, fa), *events)
        fb += [self.line_gather(v, "B") for v in fa[1:]]
        count = self.size["B"]
        block = jnp.concatenate([row[i] for i in range(count) for row in nb])
        nc = self.line_gather(block, "c")
        events = yield (*fb[1][1:], *nc[1:])
        fb = after(fb, *events)
        block = jnp.concatenate([row[i] for i in range(count) for row in fb])
        return nc + self.line_gather(block, "c")

    def lines(self, total):
        return [total[i] for i in range(total.shape[0])]

    def z_sum(self, near, far, events):
        def sent(value, way="pair"):
            return self.move(value.astype(BF16), "z", way)

        near, far = after((near, far), *events)
        o3, o2 = sent(far[1], "in"), sent(far[0], "in")
        events = yield (o3, o2)
        far, o3, o2 = after((far, o3, o2), *events)
        m3, m2 = sent(far[1] + o3.astype(F32), "mid"), sent(far[0] + o2.astype(F32), "mid")
        events = yield (m3, m2)
        near, m3, m2 = after((near, m3, m2), *events)
        pair = sent(near[1] + m3.astype(F32))
        events = yield (pair,)
        return near[0] + m2.astype(F32) + after(pair, *events).astype(F32)

    def unfold(self, total):
        return total.reshape((self.size["B"], self.size["A"], 2) + total.shape[1:])

    def scatter(self, groups, kind=F32):
        events = yield
        far, near = after((groups[2:], groups[:2]), *events)
        far = self.unfold(self.line_reduce(far, "c").astype(kind))
        near = self.unfold(self.line_reduce(near, "c").astype(kind))
        for axis in "BA":
            events = yield (far, near)
            far, near = after((far, near), *events)
            far = self.line_reduce(self.lines(far), axis).astype(kind)
            near = self.line_reduce(self.lines(near), axis).astype(kind)
        events = yield (far, near)
        return (yield from self.z_sum(near, far, events))

    def scatter_early(self, groups, late):
        yield
        far = self.unfold(self.line_reduce(groups[2:], "c"))
        yield (far,)
        far = self.line_reduce(self.lines(far), "B")
        yield (far,)
        far = self.line_reduce(self.lines(far), "A")
        near = self.unfold(self.line_reduce(late(), "c"))
        events = yield (far, near)
        near = self.line_reduce(self.lines(after(near, *events)), "B")
        o3, o2 = self.move(far[1].astype(BF16), "z", "in"), self.move(far[0].astype(BF16), "z", "in")
        events = yield (near, o3, o2)
        near, o3, o2 = after((near, o3, o2), *events)
        near = self.line_reduce(self.lines(near), "A")
        m3 = self.move((far[1] + o3.astype(F32)).astype(BF16), "z", "mid")
        m2 = self.move((far[0] + o2.astype(F32)).astype(BF16), "z", "mid")
        events = yield (near, m3, m2)
        near, m3, m2 = after((near, m3, m2), *events)
        pair = self.move((near[1] + m3.astype(F32)).astype(BF16), "z")
        events = yield (pair,)
        return near[0] + m2.astype(F32) + after(pair, *events).astype(F32)

    def dp_gather(self, value):
        events = yield
        near, far, o1 = yield from self.z_hops(value, events)
        ny = self.line_gather(near, "y")
        events = yield (o1, *ny[1:])
        fy = self.line_gather(far(after(o1, *events)), "y")
        events = yield (*fy[1:],)
        z, y = self.slots("z"), self.slots("y")
        n = value.shape[0]
        whole = jnp.zeros((n * self.dp,) + value.shape[1:], value.dtype)
        for h, line in enumerate((ny, fy)):
            for j, got in enumerate(line):
                for k in range(2):
                    place = (z[2 * h + k] * self.size["y"] + y[j]) * n
                    whole = lax.dynamic_update_slice_in_dim(whole, got[k], place, 0)
        return whole

    def dp_scatter(self, halves):
        events = yield
        near, far = after(halves, *events)
        far = self.line_reduce(self.lines(far), "y")
        events = yield (far,)
        far, near = after((far, near), *events)
        near = self.line_reduce(self.lines(near), "y")
        return (yield from self.z_sum(near, far, ()))

    def flip(self, value, bit):
        return lax.ppermute(value, AXES, [(i, i ^ bit) for i in range(self.count)])

    def small_gather(self, value):
        held, bit = value[None], 1
        while bit < self.count:
            events = yield (held,)
            held = after(held, *events)
            held = jnp.concatenate([held, self.flip(held, bit)])
            bit *= 2
        return held[self.linear ^ jnp.arange(self.count)]

    def small_scatter(self, value):
        held = value[self.linear ^ jnp.arange(self.count)]
        bit = self.count // 2
        while bit:
            held = held[:bit] + self.flip(held[bit:], bit)
            bit //= 2
        return held[0]

    def group_sum(self, value):
        total = value
        for r in range(1, self.ex):
            total = total + self.flip(value, r)
        return total


def exchange(value):
    return lax.all_to_all(value, "expert", split_axis=0, concat_axis=0, tiled=True)


def moe_kernel(ff, local, x_ref, lift_ref, gate_ref, w_ref, grad_ref, act_ref, sum_ref, back_ref):
    x = x_ref[...]
    per = 128 // ff
    lane = lax.broadcasted_iota(jnp.int32, (x.shape[0], 128), 1)
    for b in range(local // per):
        wide, narrow = pl.ds(256 * b, 256), pl.ds(128 * b, 128)
        pre_act = dot(x, w_ref[:, wide])
        gate_part, up_part = pre_act[:, :128], pre_act[:, 128:]
        spread = jnp.broadcast_to(gate_ref[:, pl.ds(b * per, 1)], lane.shape)
        for k in range(1, per):
            spread = jnp.where(
                lane < k * ff,
                spread,
                jnp.broadcast_to(gate_ref[:, pl.ds(b * per + k, 1)], lane.shape),
            )
        lifted = lift_ref[:, narrow]
        sig = 1.0 / (1.0 + jnp.exp(-gate_part))
        act = (gate_part * sig * up_part).astype(BF16).astype(F32)
        act_ref[:, narrow] = (act * spread).astype(BF16)
        terms = act * lifted
        for k in range(per):
            mine = jnp.where((lane >= k * ff) & (lane < (k + 1) * ff), terms, 0.0)
            sum_ref[:, pl.ds(b * per + k, 1)] = jnp.sum(mine, axis=1, keepdims=True)
        grad_act = lifted * spread
        grad_gate = grad_act * up_part * sig * (1.0 + gate_part * (1.0 - sig))
        grad_ref[:, pl.ds(256 * b, 128)] = grad_gate.astype(BF16)
        grad_ref[:, pl.ds(256 * b + 128, 128)] = (grad_act * gate_part * sig).astype(BF16)
    back_ref[...] = dot(grad_ref[...], w_ref[...], ROWS_BACK).astype(back_ref.dtype)


def moe_rows(x, lifted, gates, weight, ff, start, total, kind):
    width, wide = weight.shape
    local = gates.shape[1]
    tile = 256 if total % 256 == 0 else 128
    skip = start // tile
    row = lambda n: pl.BlockSpec((tile, n), lambda i: (i + skip, 0))
    out = lambda n: pl.BlockSpec((tile, n), lambda i: (i, 0))
    return pl.pallas_call(
        functools.partial(moe_kernel, ff, local),
        grid=(total // tile,),
        in_specs=[
            row(width),
            row(wide // 2),
            row(local),
            pl.BlockSpec((width, wide), lambda i: (0, 0)),
        ],
        out_specs=[out(wide), out(wide // 2), out(local), out(width)],
        out_shape=[
            jax.ShapeDtypeStruct((total, wide), BF16),
            jax.ShapeDtypeStruct((total, wide // 2), BF16),
            jax.ShapeDtypeStruct((total, local), F32),
            jax.ShapeDtypeStruct((total, width), kind),
        ],
        compiler_params=pltpu.CompilerParams(vmem_limit_bytes=56 * 1024 * 1024),
        cost_estimate=pl.CostEstimate(
            flops=4 * total * width * wide, bytes_accessed=total * width * 12, transcendentals=0
        ),
    )(x, lifted, gates, weight)


def deal_kernel(dp, in_ref, out_ref):
    for p in range(dp):
        out_ref[p] = in_ref[0, :, 128 * p : 128 * (p + 1)]


def deal(expert_in, dp):
    local, rows, wide = expert_in.shape
    return pl.pallas_call(
        functools.partial(deal_kernel, dp),
        grid=(local, 2),
        in_specs=[pl.BlockSpec((1, rows, wide // 2), lambda e, g: (e, 0, g))],
        out_specs=pl.BlockSpec((dp, rows, 128), lambda e, g: (0, 0, 2 * e + g)),
        out_shape=jax.ShapeDtypeStruct((dp, rows, local * 256), expert_in.dtype),
        compiler_params=pltpu.CompilerParams(vmem_limit_bytes=32 * 1024 * 1024),
    )(expert_in)


def undeal_kernel(parts, each, *refs):
    out_ref = refs[parts]
    e, g = pl.program_id(0), pl.program_id(1)
    for h in range(parts):

        @pl.when(e // each == h)
        def _():
            column = pl.multiple_of((2 * (e - h * each) + g) * 128, 128)
            for p in range(refs[h].shape[0]):
                piece = refs[h][p, :, pl.ds(column, 128)]
                out_ref[0, :, 128 * p : 128 * (p + 1)] = piece.astype(F32)


def undeal(pieces):
    parts = len(pieces)
    dp, rows, wide = pieces[0].shape
    each = wide // 256
    return pl.pallas_call(
        functools.partial(undeal_kernel, parts, each),
        grid=(parts * each, 2),
        in_specs=[pl.BlockSpec((dp, rows, wide), lambda e, g: (0, 0, 0))] * parts,
        out_specs=pl.BlockSpec((1, rows, dp * 128), lambda e, g: (e, 0, g)),
        out_shape=jax.ShapeDtypeStruct((parts * each, rows, 2 * dp * 128), F32),
        compiler_params=pltpu.CompilerParams(vmem_limit_bytes=48 * 1024 * 1024),
    )(*pieces)


def deal_narrow(expert_in, dp):
    local, rows, wide = expert_in.shape
    ff = wide // 2 // dp
    split = expert_in.reshape(local * ff // 128, 128 // ff, rows, 2, dp, ff)
    return split.transpose(4, 2, 0, 3, 1, 5).reshape(dp, rows, 2 * local * ff)


def undeal_narrow(pieces, ff):
    whole = jnp.concatenate(pieces, axis=2)
    dp, rows, wide = whole.shape
    whole = whole.reshape(dp, rows, wide // 256, 2, 128 // ff, ff).astype(F32)
    return whole.transpose(2, 4, 1, 3, 0, 5).reshape(wide // 2 // ff, rows, 2 * dp * ff)


def swap(value):
    return lax.all_to_all(value, "dp", split_axis=0, concat_axis=0, tiled=True)


def masked(segment):
    length = segment.shape[1]
    row_index = lax.broadcasted_iota(jnp.int32, (length, length), 0)
    col_index = lax.broadcasted_iota(jnp.int32, (length, length), 1)
    return (segment[:, :, None] == segment[:, None, :]) & (col_index <= row_index)[None]


def attend(queries, key_rows, values, allowed):
    raw = jnp.einsum("sqhd,skhd->shqk", queries, key_rows, preferred_element_type=F32)
    scores = jnp.where(allowed[:, None], raw * HEAD_DIM ** (-0.5), MASKED)
    row_max = jnp.max(scores, axis=-1, keepdims=True)
    exp_terms = jnp.exp(scores - row_max)
    weights_f = exp_terms / jnp.sum(exp_terms, axis=-1, keepdims=True)
    attended = jnp.einsum(
        "shqk,skhd->sqhd", weights_f.astype(BF16), values, preferred_element_type=F32
    )
    return (attended.astype(BF16), weights_f)


def attend_back(queries, key_rows, values, weights_f, attended, grad_heads):
    weights_b = weights_f.astype(BF16)
    grad_values = jnp.einsum("shqk,sqhd->skhd", weights_b, grad_heads, preferred_element_type=F32)
    grad_weights = jnp.einsum("sqhd,skhd->shqk", grad_heads, values, preferred_element_type=F32)
    row_delta = jnp.sum(grad_heads.astype(F32) * attended.astype(F32), axis=-1)
    row_delta = jnp.swapaxes(row_delta, 1, 2)[..., None]
    grad_scores = (weights_f * (grad_weights - row_delta) * HEAD_DIM ** (-0.5)).astype(BF16)
    grad_queries = jnp.einsum(
        "shqk,skhd->sqhd", grad_scores, key_rows, preferred_element_type=F32
    )
    grad_keys = jnp.einsum("shqk,sqhd->skhd", grad_scores, queries, preferred_element_type=F32)
    return (grad_queries, grad_keys, grad_values)


def per_device(
    tokens,
    cotangent,
    segments,
    routes,
    slot_index,
    in_projection,
    out_projection,
    router_weight,
    norm_gains,
    expert_in,
    expert_down,
):
    grid = Grid()
    length, width = tokens.shape
    count, dp, ex = grid.count, grid.dp, grid.ex
    local = expert_in.shape[0]
    expert_count = ex * local
    ff = expert_down.shape[1]
    rows = width // count
    block = width // dp
    heads = HEADS // ex
    span = heads * HEAD_DIM
    group = lax.axis_index("expert")
    stage = lax.axis_index("dp")
    cosine, sine_table = rope_tables(length)
    source = grid.sources()
    ids = jnp.arange(count, dtype=source.dtype)
    back = jnp.sum(jnp.where(source[None, :] == ids[:, None], ids[None, :], 0), axis=1)
    dp_source = grid.dp_sources()
    chunks = 1 if length * count <= 4096 else length * count // 4096
    size = length // chunks

    def reorder(tensor, order):
        parts = order.shape[0]
        return jnp.take(
            tensor.reshape(tensor.shape[0], parts, width // parts), order, axis=1
        ).reshape(tensor.shape[0], width)

    small = jnp.concatenate(
        [
            norm_gains.reshape(-1),
            router_weight.reshape(-1),
            segments.astype(BF16).reshape(-1),
        ]
    )
    small = jnp.pad(small, (0, -small.shape[0] % 128)).reshape(-1, 128)
    small_flow = Flow(grid.small_gather(small))
    small_flow.go()

    piece = in_projection.reshape(rows, 3, ex, span).transpose(2, 0, 1, 3)
    piece = exchange(piece.reshape(ex, rows, 3 * span)).reshape(block, 3 * span)
    tokens_g = exchange(
        after(jnp.broadcast_to(tokens[None], (ex, length, width)), piece)
    )
    dense = Flow(grid.dp_gather(piece))
    out_flow = Flow(grid.gather(out_projection))
    cot_flow = Flow(grid.gather(cotangent[:size]))
    dealt = (deal if ff == 128 else deal_narrow)(after(expert_in, piece), dp)
    weight_down = expert_down.reshape(local * ff, width)

    quarter = local * ff // 2
    weights = []

    def fetch(*events):
        columns = slice(len(weights) * quarter, (len(weights) + 1) * quarter)
        weights.append(swap(after(dealt[:, :, columns], *events)).reshape(width, quarter))

    dense.go()
    small_flow.go(piece)
    out_flow.go(*dense.hops[0])
    cot_flow.go(*dense.hops[0])
    small_flow.go(*dense.hops[0])
    dense.go(tokens_g)
    out_flow.go(*dense.hops[1])
    cot_flow.go(*dense.hops[1])
    small_flow.go(*dense.hops[1])
    dense.go(dealt, *out_flow.hops[0], *cot_flow.hops[0])
    fetch(*dense.hops[2])
    out_flow.go(*dense.hops[2])
    small_flow.go(*dense.hops[2])
    dense.go(*out_flow.hops[1], *cot_flow.hops[1])
    cot_flow.go(*dense.hops[3])
    out_flow.go(*dense.hops[3], *out_flow.hops[2])
    proj = after(dense.finish(), weights[0])
    fetch(*dense.hops[3])
    small = small_flow.finish().reshape(count, -1)
    cuts = np.cumsum([4 * rows, rows * expert_count, length])
    all_gains, all_router, all_segments, _ = jnp.split(small, cuts, axis=1)
    gains = jnp.swapaxes(all_gains.reshape(count, 4, rows), 0, 1).reshape(4, width).astype(F32)
    router = all_router.reshape(width, expert_count)
    segment = lax.dynamic_slice_in_dim(
        all_segments.reshape(dp, ex, length), stage, 1, 0
    )[0].astype(jnp.int32)
    allowed = masked(segment)
    gain_q = lax.dynamic_slice_in_dim(gains[2], group * span, span)
    gain_k = lax.dynamic_slice_in_dim(gains[3], group * span, span)

    normed1_g, factor1 = normalize(tokens_g.reshape(ex * length, width).astype(F32))
    hidden1_g = (normed1_g * gains[0]).astype(BF16)
    projected = dot(hidden1_g, proj)
    query_raw, key_raw = projected[:, :span], projected[:, span : 2 * span]
    squares = jnp.stack([jnp.sum(query_raw**2, axis=-1), jnp.sum(key_raw**2, axis=-1)])
    squares = grid.group_sum(squares)
    squares = after(squares, weights[1], *out_flow.hops[3], *cot_flow.hops[2])
    fetch(squares)
    out_flow.go(squares)
    cot_flow.go(squares)
    factors = lax.rsqrt(squares / width + EPSILON)[:, :, None]
    query_factor, key_factor = factors[0], factors[1]
    proj_out = jnp.concatenate(out_flow.finish()).reshape(width, width)
    query_normed, key_normed = query_raw * query_factor, key_raw * key_factor

    def by_heads(tensor):
        return tensor.reshape(ex, length, heads, HEAD_DIM)

    queries = rotate(by_heads(query_normed * gain_q), cosine, sine_table, False).astype(BF16)
    key_rows = rotate(by_heads(key_normed * gain_k), cosine, sine_table, False).astype(BF16)
    values = by_heads(projected[:, 2 * span :].astype(BF16))
    attended_h, weights_f = attend(queries, key_rows, values, allowed)
    cot_flow.go(attended_h, *cot_flow.hops[3])
    attended = exchange(attended_h.reshape(ex, length, span))
    attended = after(attended, weights[2])
    fetch(attended)
    attended_c = jnp.swapaxes(attended, 0, 1).reshape(length, width)
    attended_s = reorder(attended_c, source)
    residual = tokens.astype(F32)
    middle = residual + dot(attended_s, proj_out)
    normed2, factor2 = normalize(middle)
    hidden2 = (normed2 * gains[1]).astype(BF16)
    hidden2 = after(hidden2, weights[3], *cot_flow.hops[4])
    weight_in = jnp.concatenate(weights, axis=1)
    router_probs = jax.nn.softmax(dot(hidden2, router), axis=-1)
    grad_top = cotangent.astype(F32)
    named = jnp.arange(expert_count, dtype=jnp.int32)
    chosen = jnp.any(routes[:, :, None] == named[None, None, :], axis=1)
    gates = jnp.where(chosen, router_probs, 0.0).reshape(-1, 128)

    hid_flow = Flow(grid.gather(hidden2[:size]))
    gate_flow = Flow(grid.small_gather(gates))
    cot_flow.go(hidden2)
    hid_flow.go()
    gate_flow.go()
    hid_flow.go(weight_in, *cot_flow.hops[5])
    cot_flow.go(*hid_flow.hops[0])
    gate_flow.go(*hid_flow.hops[0])
    for k in (1, 2, 3):
        gate_flow.go(*hid_flow.hops[k])
        hid_flow.go(*gate_flow.hops[k])
    gates = gate_flow.finish().reshape(count, length, expert_count)
    gates = lax.dynamic_slice_in_dim(gates[source], group * local, local, 2)
    back_flows, mix_flows, probs_parts = [], [], []
    grad_in_w, grad_down_w = [0.0] * 4, 0.0
    for i in range(chunks):
        if i:
            ready = (back_flows[-1].finish(), mix_flows[-1].finish(), grad_in_w, grad_down_w)
            part = slice(i * size, (i + 1) * size)
            cot_flow = Flow(grid.gather(after(cotangent[part], *ready)))
            hid_flow = Flow(grid.gather(after(hidden2[part], *ready)))
        cot = jnp.concatenate(cot_flow.finish()).reshape(-1, width)
        lifted = dot(cot, weight_down, ROWS_BACK)
        while len(hid_flow.hops) < 5:
            hid_flow.go()
        total = size * count
        gate_dense = gates[:, i * size : (i + 1) * size].reshape(total, local)
        hid_flow.go(lifted, gate_dense)
        hid = jnp.concatenate(hid_flow.finish()).reshape(-1, width)
        part = total // 4
        slotted = (count // 4, size, width)
        done = [None] * 4

        def run(j, *events):
            kind = BF16 if j % 2 else F32
            gates = after(gate_dense, *events)
            done[j] = moe_rows(hid, lifted, gates, weight_in, ff, j * part, part, kind)
            return done[j][3].reshape(slotted)

        far = [None, None, None, run(3)]
        far[2] = run(2, done[3][3])
        near = [None, None]
        flow = Flow(grid.scatter_early(far, lambda: near))
        flow.go()
        near[1] = run(1, *flow.hops[0])
        flow.go()
        near[0] = run(0, *flow.hops[1], done[1][3])
        flow.go()
        last = done[0][3]
        acts = [d[1] for d in done]
        grad_pre = jnp.concatenate([d[0] for d in done])
        wide = 2 * local * ff // 4
        columns = [grad_pre[:, q * wide : (q + 1) * wide] for q in range(4)]

        def weigh(q, *events):
            part = dot(after(hid, *events), columns[q], SUM_ROWS)
            grad_in_w[q] += part
            return part

        def mixed(j, *events):
            return dot(after(acts[j], *events), weight_down).astype(BF16).reshape(slotted)

        first = weigh(0, last)
        flow.go(first)
        mix = [None, None, mixed(2, *flow.hops[2]), mixed(3, *flow.hops[2])]
        flow.go(mix[2], mix[3])
        mix[0], mix[1] = mixed(0, *flow.hops[3]), mixed(1, *flow.hops[3])
        second = weigh(1, *flow.hops[3])
        if i == chunks - 1:
            gone = [g.astype(BF16).reshape(dp, block, wide) for g in grad_in_w[:1]]
            home = [swap(gone[0])]
            flow.go(mix[0], mix[1], second, home[0])
        else:
            flow.go()
        third = weigh(2, *flow.hops[4])
        flow.go(third)
        if i < chunks - 1:
            weigh(3)
        back_flows.append(flow)
        mix_flow = Flow(grid.scatter(mix, BF16))
        mix_flow.go(*flow.hops[4])
        mix_flows.append(mix_flow)
        probs_part = jnp.concatenate([d[2] for d in done])
        probs_parts.append(probs_part.reshape(count, size, local))
        act_gated = jnp.concatenate(acts)
        if i < chunks - 1:
            grad_down_w += dot(act_gated, cot, SUM_ROWS)

    def send(q, *events):
        home.append(swap(after(grad_in_w[q].astype(BF16).reshape(dp, block, wide), *events)))

    probs_all = jnp.concatenate(probs_parts, axis=1)[back]
    place = (jnp.arange(expert_count) // local == group).astype(F32)
    probs_wide = (jnp.tile(probs_all, (1, 1, ex)) * place).reshape(
        count, length * expert_count // 128, 128
    )
    grad_probs = grid.small_scatter(probs_wide).reshape(length, expert_count)
    grad_probs = jnp.where(chosen, grad_probs, 0.0)

    grad_logits = (
        router_probs * (grad_probs - jnp.sum(router_probs * grad_probs, axis=-1, keepdims=True))
    ).astype(BF16)
    grad_router_part = dot(hidden2, grad_logits, SUM_ROWS)
    grad_hidden2 = jnp.concatenate([f.finish() for f in back_flows]) + dot(grad_logits, router, ROWS_BACK)
    grad_gain_moe = jnp.sum(grad_hidden2 * normed2, axis=0)
    grad_middle = grad_top + normalize_back(grad_hidden2 * gains[1], normed2, factor2)
    grad_mid_b = grad_middle.astype(BF16)
    grad_attended = reorder(dot(grad_mid_b, proj_out, ROWS_BACK).astype(BF16), back)
    grad_heads = by_heads(
        exchange(jnp.swapaxes(grad_attended.reshape(length, ex, span), 0, 1)).reshape(
            ex * length, span
        )
    )
    quarter = width // 4
    out_parts = [
        dot(attended_s[:, j * quarter : (j + 1) * quarter], grad_mid_b, SUM_ROWS).reshape(
            count // 4, rows, width
        )
        for j in range(4)
    ]
    out_flow = Flow(grid.scatter(out_parts))
    send(1, grad_mid_b)
    mix_flow.go(grad_mid_b)
    fourth = weigh(3, grad_attended)
    grad_heads = after(grad_heads, fourth, *mix_flow.hops[1])
    send(2, grad_heads)
    mix_flow.go(grad_heads)
    out_flow.go(grad_heads)
    grad_queries, grad_keys, grad_values = attend_back(
        queries, key_rows, values, weights_f, attended_h, grad_heads
    )
    flat = (ex * length, span)
    grad_qscaled = rotate(grad_queries, cosine, sine_table, True).reshape(flat)
    grad_kscaled = rotate(grad_keys, cosine, sine_table, True).reshape(flat)
    up_q, up_k = grad_qscaled * gain_q, grad_kscaled * gain_k
    along = jnp.stack([jnp.sum(up_q * query_normed, axis=-1), jnp.sum(up_k * key_normed, axis=-1)])
    along = (grid.group_sum(along) / width)[:, :, None]
    along = after(along, *mix_flow.hops[2], *out_flow.hops[0])
    mix_flow.go(along)
    out_flow.go(along)
    grad_projected = jnp.concatenate(
        [
            query_factor * (up_q - query_normed * along[0]),
            key_factor * (up_k - key_normed * along[1]),
            grad_values.reshape(flat),
        ],
        axis=1,
    ).astype(BF16)
    mid = width // 2
    hidden1_s = reorder(hidden1_g, dp_source)
    proj_flow = Flow(
        grid.dp_scatter(
            [
                dot(hidden1_s[:, h * mid : (h + 1) * mid], grad_projected, SUM_ROWS).reshape(
                    grid.size["y"], 2, block, 3 * span
                )
                for h in range(2)
            ]
        )
    )
    proj_flow.go(home[1], home[2])
    send(3, grad_projected)
    proj_flow.go(home[3], *mix_flow.hops[3], *out_flow.hops[1])
    mix_flow.go(*proj_flow.hops[0])
    out_flow.go(*proj_flow.hops[0])
    grad_down_w += dot(after(act_gated, *proj_flow.hops[0]), cot, SUM_ROWS)
    proj_flow.go(grad_down_w, *mix_flow.hops[4], *out_flow.hops[2])
    mix_flow.go(*proj_flow.hops[1])
    out_flow.go(*proj_flow.hops[1])
    home = after(home, *proj_flow.hops[1])
    grad_expert_in = undeal(home) if ff == 128 else undeal_narrow(home, ff)
    proj_flow.go(grad_expert_in, *mix_flow.hops[5], *out_flow.hops[3])
    out_flow.go(*proj_flow.hops[2])
    grad_proj = proj_flow.finish()
    block_out = middle + jnp.concatenate([f.finish() for f in mix_flows])
    grad_out_projection = out_flow.finish()
    grad_expert_down = grad_down_w.reshape(local, ff, width)
    grad_proj = exchange(grad_proj.astype(BF16).reshape(ex, rows, 3 * span)).astype(F32)
    grad_in_projection = (
        grad_proj.reshape(ex, rows, 3, span).transpose(1, 2, 0, 3).reshape(rows, 3 * width)
    )
    grad_hidden1 = dot(grad_projected, proj, ROWS_BACK).astype(BF16)
    grad_hidden1 = jnp.sum(exchange(grad_hidden1.reshape(ex, length, width)).astype(F32), axis=0)
    own = lax.dynamic_slice_in_dim(normed1_g, group * length, length, 0)
    own_factor = lax.dynamic_slice_in_dim(factor1, group * length, length, 0)
    gain_one = jnp.sum(grad_hidden1 * own, axis=0)
    input_grad = grad_middle + normalize_back(grad_hidden1 * gains[0], own, own_factor)


    def widen(values):
        return lax.dynamic_update_slice_in_dim(jnp.zeros((width,), F32), values, group * span, 0)

    grad_gain_part = jnp.stack(
        [
            gain_one,
            grad_gain_moe,
            widen(jnp.sum(grad_qscaled * query_normed, axis=0)),
            widen(jnp.sum(grad_kscaled * key_normed, axis=0)),
        ]
    )
    last = jnp.concatenate(
        [
            jnp.swapaxes(grad_gain_part.reshape(4, count, rows), 0, 1).reshape(count, -1),
            grad_router_part.reshape(count, -1),
        ],
        axis=1,
    )
    last = after(last, *proj_flow.hops[2])
    last = grid.small_scatter(last.reshape(count, -1, 128 if last.shape[1] % 128 == 0 else 64))
    last = last.reshape(-1)
    grad_norm_gains = last[: 4 * rows].reshape(4, rows)
    grad_router = last[4 * rows :].reshape(rows, expert_count)
    return (
        block_out,
        input_grad,
        grad_in_projection,
        grad_out_projection,
        grad_router,
        grad_norm_gains,
        grad_expert_in,
        grad_expert_down,
    )


def solution(mesh):
    both = P(AXES, None)
    split = P("expert", "dp", None)
    in_specs = (both,) * 8 + (P(None, AXES), split, split)
    out_specs = (both,) * 5 + (P(None, AXES), split, split)
    return jax.shard_map(
        per_device, mesh=mesh, in_specs=in_specs, out_specs=out_specs, check_vma=False
    )
```

```python
import functools

import jax
import jax.numpy as jnp
import numpy as np
from jax import lax
from jax.experimental import pallas as pl
from jax.experimental.pallas import tpu as pltpu
from jax.sharding import PartitionSpec as P

HEADS = 16
HEAD_DIM = 128
EPSILON = 1e-05
ROPE_BASE = 10000.0
MASKED = -1e30
AXES = ("dp", "expert")
BF16 = jnp.bfloat16
F32 = jnp.float32
ROWS_BACK = (((1,), (1,)), ((), ()))
SUM_ROWS = (((0,), (0,)), ((), ()))


def dot(left, right, dims=(((1,), (0,)), ((), ()))):
    return lax.dot_general(left, right, dims, preferred_element_type=F32)


def after(value, *others):
    return lax.optimization_barrier((value,) + others)[0] if others else value


class Flow:
    def __init__(self, steps):
        self.steps, self.hops, self.result = steps, [], None
        next(steps)

    def go(self, *events):
        if self.result is not None:
            return
        try:
            self.hops.append(self.steps.send(events))
        except StopIteration as stop:
            self.result = stop.value
            assert self.result is not None

    def finish(self):
        while self.result is None:
            self.go()
        return self.result


def normalize(tensor):
    factor = lax.rsqrt(jnp.mean(tensor * tensor, axis=-1, keepdims=True) + EPSILON)
    return (tensor * factor, factor)


def normalize_back(upstream, normed, factor):
    return factor * (upstream - normed * jnp.mean(upstream * normed, axis=-1, keepdims=True))


def rope_tables(length):
    half_dim = HEAD_DIM // 2
    position = jnp.arange(length).astype(F32)
    frequency = ROPE_BASE ** (-2.0 * jnp.arange(half_dim).astype(F32) / HEAD_DIM)
    angles = position[:, None] * frequency[None, :]
    return (jnp.cos(angles), jnp.sin(angles))


def rotate(tensor, cosine, sine_table, inverse):
    half = HEAD_DIM // 2
    first_half, second_half = tensor[..., :half], tensor[..., half:]
    cosine, sine_table = cosine[None, :, None, :], sine_table[None, :, None, :]
    if inverse:
        sine_table = -sine_table
    return jnp.concatenate(
        [
            first_half * cosine - second_half * sine_table,
            second_half * cosine + first_half * sine_table,
        ],
        axis=-1,
    )


class Grid:
    def __init__(self):
        self.dp = lax.axis_size("dp")
        self.ex = lax.axis_size("expert")
        self.count = self.dp * self.ex
        self.size = {"z": 4, "y": self.dp // 4, "x": self.ex // 2, "c": 2}
        self.size["A"], self.size["B"] = self.size["y"], self.size["x"]
        self.swap = self.size["x"] == self.size["y"]
        d, e = lax.axis_index("dp"), lax.axis_index("expert")
        self.linear = d * self.ex + e
        ny = self.size["y"]
        self.at = {"z": d // ny, "y": d % ny, "x": e // 2, "c": e % 2}

    def real(self, axis, core):
        if axis in "AB":
            return "yx"[(axis == "B") != (core == 1 and self.swap)]
        return axis

    def index(self, p):
        return (p["z"] * self.size["y"] + p["y"]) * self.ex + p["x"] * 2 + p["c"]

    def move(self, value, axis, kind="pair"):
        s = self.size
        if s[axis] == 2:
            moves = {0: 1, 1: 0}
        else:
            moves = {
                "pair": {0: 1, 1: 0, 2: 3, 3: 2},
                "mid": {1: 2, 2: 1},
                "out": {1: 0, 2: 3},
                "in": {0: 1, 3: 2},
            }[kind]
        pairs = []
        for i in range(self.count):
            d, e = divmod(i, self.ex)
            here = {"z": d // s["y"], "y": d % s["y"], "x": e // 2, "c": e % 2}
            line = self.real(axis, here["c"])
            if here[line] in moves:
                pairs.append((i, self.index({**here, line: moves[here[line]]})))
        return lax.ppermute(value, AXES, pairs)

    def middle(self, axis):
        at = self.at[self.real(axis, 0)]
        if axis in "AB" and self.swap:
            at = jnp.where(self.at["c"] == 0, at, self.at[self.real(axis, 1)])
        return (at == 1) | (at == 2)

    def slots(self, axis):
        n = self.size[axis]
        table = {
            1: [[0]],
            2: [[0, 1], [1, 0]],
            4: [[0, 1, 2, 3], [1, 0, 2, 3], [2, 3, 1, 0], [3, 2, 1, 0]],
        }[n]
        return jnp.asarray(np.array(table, np.int32))[self.at[axis]]

    def sources(self):
        c, y, x, z = [self.slots(a) for a in "cyxz"]
        z, c = z.reshape(2, 1, 1, 1, 2), c.reshape(1, -1, 1, 1, 1)
        along_b, along_a = (1, 1, -1, 1, 1), (1, 1, 1, -1, 1)
        xs, ys = x.reshape(along_b), y.reshape(along_a)
        if self.swap:
            xs = jnp.where(c == 0, xs, x.reshape(along_a))
            ys = jnp.where(c == 0, ys, y.reshape(along_b))
        return ((z * self.size["y"] + ys) * self.ex + xs * 2 + c).reshape(-1)

    def dp_sources(self):
        z = self.slots("z").reshape(2, 1, 2)
        return (z * self.size["y"] + self.slots("y").reshape(1, -1, 1)).reshape(-1)

    def line_gather(self, value, axis):
        n = self.size[axis]
        if n == 1:
            return [value]
        pair = self.move(value, axis)
        if n == 2:
            return [value, pair]
        m0, m1 = self.move(value, axis, "mid"), self.move(pair, axis, "mid")
        o0, o1 = self.move(m0, axis, "out"), self.move(m1, axis, "out")
        mid = self.middle(axis)
        return [value, pair, jnp.where(mid, m0, o0), jnp.where(mid, m1, o1)]

    def line_reduce(self, slots, axis, kind=BF16):
        n = self.size[axis]
        slots = [slots[0].astype(F32)] + list(slots[1:])

        def sent(value, *way):
            return self.move(value.astype(kind), axis, *way).astype(F32)

        if n == 1:
            return slots[0]
        if n == 2:
            return slots[0] + sent(slots[1])
        m3 = sent(slots[3] + sent(slots[3], "in"), "mid")
        m2 = sent(slots[2] + sent(slots[2], "in"), "mid")
        return slots[0] + m2 + sent(slots[1] + m3)

    def z_hops(self, value, events):
        value = after(value, *events)
        pair, m0 = self.move(value, "z"), self.move(value, "z", "mid")
        events = yield (pair, m0)
        pair, m0 = after((pair, m0), *events)
        m1, o0 = self.move(pair, "z", "mid"), self.move(m0, "z", "out")
        events = yield (m1, o0)
        mid = self.middle("z")
        near = jnp.stack([value, pair])
        m1, near = after((m1, near), *events)
        o1 = self.move(m1, "z", "out")
        return near, lambda o1: jnp.stack([jnp.where(mid, m0, o0), jnp.where(mid, m1, o1)]), o1

    def gather(self, value):
        events = yield
        near, far, o1 = yield from self.z_hops(value, events)
        na = self.line_gather(near, "A")
        events = yield (o1, *na[1:])
        o1, na = after((o1, na), *events)
        fa, nb = self.line_gather(far(o1), "A"), [self.line_gather(na[0], "B")]
        events = yield (*fa[1:], *nb[0][1:])
        na, fa = after((na, fa), *events)
        nb += [self.line_gather(v, "B") for v in na[1:]]
        fb = [self.line_gather(fa[0], "B")]
        events = yield (*nb[1][1:], *fb[0][1:])
        nb, fa = after((nb, fa), *events)
        fb += [self.line_gather(v, "B") for v in fa[1:]]
        count = self.size["B"]
        block = jnp.concatenate([row[i] for i in range(count) for row in nb])
        nc = self.line_gather(block, "c")
        events = yield (*fb[1][1:], *nc[1:])
        fb = after(fb, *events)
        block = jnp.concatenate([row[i] for i in range(count) for row in fb])
        return nc + self.line_gather(block, "c")

    def lines(self, total):
        return [total[i] for i in range(total.shape[0])]

    def z_sum(self, near, far, events):
        def sent(value, way="pair"):
            return self.move(value.astype(BF16), "z", way)

        near, far = after((near, far), *events)
        o3, o2 = sent(far[1], "in"), sent(far[0], "in")
        events = yield (o3, o2)
        far, o3, o2 = after((far, o3, o2), *events)
        m3, m2 = sent(far[1] + o3.astype(F32), "mid"), sent(far[0] + o2.astype(F32), "mid")
        events = yield (m3, m2)
        near, m3, m2 = after((near, m3, m2), *events)
        pair = sent(near[1] + m3.astype(F32))
        events = yield (pair,)
        return near[0] + m2.astype(F32) + after(pair, *events).astype(F32)

    def unfold(self, total):
        return total.reshape((self.size["B"], self.size["A"], 2) + total.shape[1:])

    def scatter(self, groups, kind=F32):
        events = yield
        far, near = after((groups[2:], groups[:2]), *events)
        far = self.unfold(self.line_reduce(far, "c").astype(kind))
        near = self.unfold(self.line_reduce(near, "c").astype(kind))
        for axis in "BA":
            events = yield (far, near)
            far, near = after((far, near), *events)
            far = self.line_reduce(self.lines(far), axis).astype(kind)
            near = self.line_reduce(self.lines(near), axis).astype(kind)
        events = yield (far, near)
        return (yield from self.z_sum(near, far, events))

    def scatter_early(self, groups, late):
        yield
        far = self.unfold(self.line_reduce(groups[2:], "c"))
        yield (far,)
        far = self.line_reduce(self.lines(far), "B")
        yield (far,)
        far = self.line_reduce(self.lines(far), "A")
        near = self.unfold(self.line_reduce(late(), "c"))
        events = yield (far, near)
        near = self.line_reduce(self.lines(after(near, *events)), "B")
        o3, o2 = self.move(far[1].astype(BF16), "z", "in"), self.move(far[0].astype(BF16), "z", "in")
        events = yield (near, o3, o2)
        near, o3, o2 = after((near, o3, o2), *events)
        near = self.line_reduce(self.lines(near), "A")
        m3 = self.move((far[1] + o3.astype(F32)).astype(BF16), "z", "mid")
        m2 = self.move((far[0] + o2.astype(F32)).astype(BF16), "z", "mid")
        events = yield (near, m3, m2)
        near, m3, m2 = after((near, m3, m2), *events)
        pair = self.move((near[1] + m3.astype(F32)).astype(BF16), "z")
        events = yield (pair,)
        return near[0] + m2.astype(F32) + after(pair, *events).astype(F32)

    def dp_gather(self, value):
        events = yield
        near, far, o1 = yield from self.z_hops(value, events)
        ny = self.line_gather(near, "y")
        events = yield (o1, *ny[1:])
        fy = self.line_gather(far(after(o1, *events)), "y")
        events = yield (*fy[1:],)
        z, y = self.slots("z"), self.slots("y")
        n = value.shape[0]
        whole = jnp.zeros((n * self.dp,) + value.shape[1:], value.dtype)
        for h, line in enumerate((ny, fy)):
            for j, got in enumerate(line):
                for k in range(2):
                    place = (z[2 * h + k] * self.size["y"] + y[j]) * n
                    whole = lax.dynamic_update_slice_in_dim(whole, got[k], place, 0)
        return whole

    def dp_scatter(self, halves):
        events = yield
        near, far = after(halves, *events)
        far = self.line_reduce(self.lines(far), "y")
        events = yield (far,)
        far, near = after((far, near), *events)
        near = self.line_reduce(self.lines(near), "y")
        return (yield from self.z_sum(near, far, ()))

    def flip(self, value, bit):
        return lax.ppermute(value, AXES, [(i, i ^ bit) for i in range(self.count)])

    def small_gather(self, value):
        held, bit = value[None], 1
        while bit < self.count:
            events = yield (held,)
            held = after(held, *events)
            held = jnp.concatenate([held, self.flip(held, bit)])
            bit *= 2
        return held[self.linear ^ jnp.arange(self.count)]

    def small_scatter(self, value):
        held = value[self.linear ^ jnp.arange(self.count)]
        bit = self.count // 2
        while bit:
            held = held[:bit] + self.flip(held[bit:], bit)
            bit //= 2
        return held[0]

    def small_sum(self, value):
        held, bit = value[self.linear ^ jnp.arange(self.count)], 1
        while bit < self.count:
            events = yield (held,)
            held = after(held, *events)
            held = held.reshape((held.shape[0] // 2, 2) + held.shape[1:])
            held = held[:, 0] + self.flip(held[:, 1], bit)
            bit *= 2
        return held[0]

    def group_sum(self, value):
        total = value
        for r in range(1, self.ex):
            total = total + self.flip(value, r)
        return total


def exchange(value):
    return lax.all_to_all(value, "expert", split_axis=0, concat_axis=0, tiled=True)


def moe_kernel(ff, local, x_ref, lift_ref, gate_ref, w_ref, grad_ref, act_ref, sum_ref, back_ref):
    x = x_ref[...]
    per = 128 // ff
    lane = lax.broadcasted_iota(jnp.int32, (x.shape[0], 128), 1)
    for b in range(local // per):
        wide, narrow = pl.ds(256 * b, 256), pl.ds(128 * b, 128)
        pre_act = dot(x, w_ref[:, wide])
        gate_part, up_part = pre_act[:, :128], pre_act[:, 128:]
        spread = jnp.broadcast_to(gate_ref[:, pl.ds(b * per, 1)], lane.shape)
        for k in range(1, per):
            spread = jnp.where(
                lane < k * ff,
                spread,
                jnp.broadcast_to(gate_ref[:, pl.ds(b * per + k, 1)], lane.shape),
            )
        lifted = lift_ref[:, narrow]
        sig = 1.0 / (1.0 + jnp.exp(-gate_part))
        act = (gate_part * sig * up_part).astype(BF16).astype(F32)
        act_ref[:, narrow] = (act * spread).astype(BF16)
        terms = act * lifted
        for k in range(per):
            mine = jnp.where((lane >= k * ff) & (lane < (k + 1) * ff), terms, 0.0)
            sum_ref[:, pl.ds(b * per + k, 1)] = jnp.sum(mine, axis=1, keepdims=True)
        grad_act = lifted * spread
        grad_gate = grad_act * up_part * sig * (1.0 + gate_part * (1.0 - sig))
        grad_ref[:, pl.ds(256 * b, 128)] = grad_gate.astype(BF16)
        grad_ref[:, pl.ds(256 * b + 128, 128)] = (grad_act * gate_part * sig).astype(BF16)
    back_ref[...] = dot(grad_ref[...], w_ref[...], ROWS_BACK).astype(back_ref.dtype)


def moe_rows(x, lifted, gates, weight, ff, start, total, kind):
    width, wide = weight.shape
    local = gates.shape[1]
    tile = 256 if total % 256 == 0 else 128
    skip = start // tile
    row = lambda n: pl.BlockSpec((tile, n), lambda i: (i + skip, 0))
    out = lambda n: pl.BlockSpec((tile, n), lambda i: (i, 0))
    return pl.pallas_call(
        functools.partial(moe_kernel, ff, local),
        grid=(total // tile,),
        in_specs=[
            row(width),
            row(wide // 2),
            row(local),
            pl.BlockSpec((width, wide), lambda i: (0, 0)),
        ],
        out_specs=[out(wide), out(wide // 2), out(local), out(width)],
        out_shape=[
            jax.ShapeDtypeStruct((total, wide), BF16),
            jax.ShapeDtypeStruct((total, wide // 2), BF16),
            jax.ShapeDtypeStruct((total, local), F32),
            jax.ShapeDtypeStruct((total, width), kind),
        ],
        compiler_params=pltpu.CompilerParams(vmem_limit_bytes=56 * 1024 * 1024),
        cost_estimate=pl.CostEstimate(
            flops=4 * total * width * wide, bytes_accessed=total * width * 12, transcendentals=0
        ),
    )(x, lifted, gates, weight)


def deal_kernel(dp, in_ref, out_ref):
    for p in range(dp):
        out_ref[p] = in_ref[0, :, 128 * p : 128 * (p + 1)]


def deal(expert_in, dp):
    local, rows, wide = expert_in.shape
    return pl.pallas_call(
        functools.partial(deal_kernel, dp),
        grid=(local, 2),
        in_specs=[pl.BlockSpec((1, rows, wide // 2), lambda e, g: (e, 0, g))],
        out_specs=pl.BlockSpec((dp, rows, 128), lambda e, g: (0, 0, 2 * e + g)),
        out_shape=jax.ShapeDtypeStruct((dp, rows, local * 256), expert_in.dtype),
        compiler_params=pltpu.CompilerParams(vmem_limit_bytes=32 * 1024 * 1024),
    )(expert_in)


def undeal_kernel(parts, each, *refs):
    out_ref = refs[parts]
    e, g = pl.program_id(0), pl.program_id(1)
    for h in range(parts):

        @pl.when(e // each == h)
        def _():
            column = pl.multiple_of((2 * (e - h * each) + g) * 128, 128)
            for p in range(refs[h].shape[0]):
                piece = refs[h][p, :, pl.ds(column, 128)]
                out_ref[0, :, 128 * p : 128 * (p + 1)] = piece.astype(F32)


def undeal(pieces):
    parts = len(pieces)
    dp, rows, wide = pieces[0].shape
    each = wide // 256
    return pl.pallas_call(
        functools.partial(undeal_kernel, parts, each),
        grid=(parts * each, 2),
        in_specs=[pl.BlockSpec((dp, rows, wide), lambda e, g: (0, 0, 0))] * parts,
        out_specs=pl.BlockSpec((1, rows, dp * 128), lambda e, g: (e, 0, g)),
        out_shape=jax.ShapeDtypeStruct((parts * each, rows, 2 * dp * 128), F32),
        compiler_params=pltpu.CompilerParams(vmem_limit_bytes=48 * 1024 * 1024),
    )(*pieces)


def deal_narrow(expert_in, dp):
    local, rows, wide = expert_in.shape
    ff = wide // 2 // dp
    split = expert_in.reshape(local * ff // 128, 128 // ff, rows, 2, dp, ff)
    return split.transpose(4, 2, 0, 3, 1, 5).reshape(dp, rows, 2 * local * ff)


def undeal_narrow(pieces, ff):
    whole = jnp.concatenate(pieces, axis=2)
    dp, rows, wide = whole.shape
    whole = whole.reshape(dp, rows, wide // 256, 2, 128 // ff, ff).astype(F32)
    return whole.transpose(2, 4, 1, 3, 0, 5).reshape(wide // 2 // ff, rows, 2 * dp * ff)


def swap(value):
    return lax.all_to_all(value, "dp", split_axis=0, concat_axis=0, tiled=True)


def masked(segment):
    length = segment.shape[1]
    row_index = lax.broadcasted_iota(jnp.int32, (length, length), 0)
    col_index = lax.broadcasted_iota(jnp.int32, (length, length), 1)
    return (segment[:, :, None] == segment[:, None, :]) & (col_index <= row_index)[None]


def attend(queries, key_rows, values, allowed):
    raw = jnp.einsum("sqhd,skhd->shqk", queries, key_rows, preferred_element_type=F32)
    scores = jnp.where(allowed[:, None], raw * HEAD_DIM ** (-0.5), MASKED)
    row_max = jnp.max(scores, axis=-1, keepdims=True)
    exp_terms = jnp.exp(scores - row_max)
    weights_f = exp_terms / jnp.sum(exp_terms, axis=-1, keepdims=True)
    attended = jnp.einsum(
        "shqk,skhd->sqhd", weights_f.astype(BF16), values, preferred_element_type=F32
    )
    return (attended.astype(BF16), weights_f)


def attend_back(queries, key_rows, values, weights_f, attended, grad_heads):
    weights_b = weights_f.astype(BF16)
    grad_values = jnp.einsum("shqk,sqhd->skhd", weights_b, grad_heads, preferred_element_type=F32)
    grad_weights = jnp.einsum("sqhd,skhd->shqk", grad_heads, values, preferred_element_type=F32)
    row_delta = jnp.sum(grad_heads.astype(F32) * attended.astype(F32), axis=-1)
    row_delta = jnp.swapaxes(row_delta, 1, 2)[..., None]
    grad_scores = (weights_f * (grad_weights - row_delta) * HEAD_DIM ** (-0.5)).astype(BF16)
    grad_queries = jnp.einsum(
        "shqk,skhd->sqhd", grad_scores, key_rows, preferred_element_type=F32
    )
    grad_keys = jnp.einsum("shqk,sqhd->skhd", grad_scores, queries, preferred_element_type=F32)
    return (grad_queries, grad_keys, grad_values)


def per_device(
    tokens,
    cotangent,
    segments,
    routes,
    slot_index,
    in_projection,
    out_projection,
    router_weight,
    norm_gains,
    expert_in,
    expert_down,
):
    grid = Grid()
    length, width = tokens.shape
    count, dp, ex = grid.count, grid.dp, grid.ex
    local = expert_in.shape[0]
    expert_count = ex * local
    ff = expert_down.shape[1]
    rows = width // count
    block = width // dp
    heads = HEADS // ex
    span = heads * HEAD_DIM
    group = lax.axis_index("expert")
    stage = lax.axis_index("dp")
    cosine, sine_table = rope_tables(length)
    source = grid.sources()
    ids = jnp.arange(count, dtype=source.dtype)
    back = jnp.sum(jnp.where(source[None, :] == ids[:, None], ids[None, :], 0), axis=1)
    dp_source = grid.dp_sources()
    chunks = 1 if length * count <= 4096 else length * count // 4096
    size = length // chunks

    def reorder(tensor, order):
        parts = order.shape[0]
        return jnp.take(
            tensor.reshape(tensor.shape[0], parts, width // parts), order, axis=1
        ).reshape(tensor.shape[0], width)

    small = jnp.concatenate(
        [
            norm_gains.reshape(-1),
            router_weight.reshape(-1),
            segments.astype(BF16).reshape(-1),
        ]
    )
    small = jnp.pad(small, (0, -small.shape[0] % 128)).reshape(-1, 128)
    small_flow = Flow(grid.small_gather(small))
    small_flow.go()

    piece = in_projection.reshape(rows, 3, ex, span).transpose(2, 0, 1, 3)
    piece = exchange(piece.reshape(ex, rows, 3 * span)).reshape(block, 3 * span)
    tokens_g = exchange(
        after(jnp.broadcast_to(tokens[None], (ex, length, width)), piece)
    )
    dense = Flow(grid.dp_gather(piece))
    out_flow = Flow(grid.gather(out_projection))
    cot_flow = Flow(grid.gather(cotangent[:size]))
    dealt = (deal if ff == 128 else deal_narrow)(after(expert_in, piece), dp)
    weight_down = expert_down.reshape(local * ff, width)

    quarter = local * ff // 2
    weights = []

    def fetch(*events):
        columns = slice(len(weights) * quarter, (len(weights) + 1) * quarter)
        weights.append(swap(after(dealt[:, :, columns], *events)).reshape(width, quarter))

    dense.go()
    small_flow.go(piece)
    out_flow.go(*dense.hops[0])
    cot_flow.go(*dense.hops[0])
    small_flow.go(*dense.hops[0])
    dense.go(tokens_g)
    out_flow.go(*dense.hops[1])
    cot_flow.go(*dense.hops[1])
    small_flow.go(*dense.hops[1])
    dense.go(dealt, *out_flow.hops[0], *cot_flow.hops[0])
    fetch(*dense.hops[2])
    out_flow.go(*dense.hops[2])
    small_flow.go(*dense.hops[2])
    dense.go(*out_flow.hops[1], *cot_flow.hops[1])
    cot_flow.go(*dense.hops[3])
    out_flow.go(*dense.hops[3], *out_flow.hops[2])
    proj = after(dense.finish(), weights[0])
    fetch(*dense.hops[3])
    small = small_flow.finish().reshape(count, -1)
    cuts = np.cumsum([4 * rows, rows * expert_count, length])
    all_gains, all_router, all_segments, _ = jnp.split(small, cuts, axis=1)
    gains = jnp.swapaxes(all_gains.reshape(count, 4, rows), 0, 1).reshape(4, width).astype(F32)
    router = all_router.reshape(width, expert_count)
    segment = lax.dynamic_slice_in_dim(
        all_segments.reshape(dp, ex, length), stage, 1, 0
    )[0].astype(jnp.int32)
    allowed = masked(segment)
    gain_q = lax.dynamic_slice_in_dim(gains[2], group * span, span)
    gain_k = lax.dynamic_slice_in_dim(gains[3], group * span, span)

    normed1_g, factor1 = normalize(tokens_g.reshape(ex * length, width).astype(F32))
    hidden1_g = (normed1_g * gains[0]).astype(BF16)
    projected = dot(hidden1_g, proj)
    query_raw, key_raw = projected[:, :span], projected[:, span : 2 * span]
    squares = jnp.stack([jnp.sum(query_raw**2, axis=-1), jnp.sum(key_raw**2, axis=-1)])
    squares = grid.group_sum(squares)
    squares = after(squares, weights[1], *out_flow.hops[3], *cot_flow.hops[2])
    fetch(squares)
    out_flow.go(squares)
    cot_flow.go(squares)
    factors = lax.rsqrt(squares / width + EPSILON)[:, :, None]
    query_factor, key_factor = factors[0], factors[1]
    proj_out = jnp.concatenate(out_flow.finish()).reshape(width, width)
    query_normed, key_normed = query_raw * query_factor, key_raw * key_factor

    def by_heads(tensor):
        return tensor.reshape(ex, length, heads, HEAD_DIM)

    queries = rotate(by_heads(query_normed * gain_q), cosine, sine_table, False).astype(BF16)
    key_rows = rotate(by_heads(key_normed * gain_k), cosine, sine_table, False).astype(BF16)
    values = by_heads(projected[:, 2 * span :].astype(BF16))
    attended_h, weights_f = attend(queries, key_rows, values, allowed)
    cot_flow.go(attended_h, *cot_flow.hops[3])
    attended = exchange(attended_h.reshape(ex, length, span))
    attended = after(attended, weights[2])
    fetch(attended)
    attended_c = jnp.swapaxes(attended, 0, 1).reshape(length, width)
    attended_s = reorder(attended_c, source)
    residual = tokens.astype(F32)
    middle = residual + dot(attended_s, proj_out)
    normed2, factor2 = normalize(middle)
    hidden2 = (normed2 * gains[1]).astype(BF16)
    hidden2 = after(hidden2, weights[3], *cot_flow.hops[4])
    weight_in = jnp.concatenate(weights, axis=1)
    router_probs = jax.nn.softmax(dot(hidden2, router), axis=-1)
    grad_top = cotangent.astype(F32)
    named = jnp.arange(expert_count, dtype=jnp.int32)
    chosen = jnp.any(routes[:, :, None] == named[None, None, :], axis=1)
    gates = jnp.where(chosen, router_probs, 0.0).reshape(-1, 128)

    hid_flow = Flow(grid.gather(hidden2[:size]))
    gate_flow = Flow(grid.small_gather(gates))
    cot_flow.go(hidden2)
    hid_flow.go()
    gate_flow.go()
    hid_flow.go(weight_in, *cot_flow.hops[5])
    cot_flow.go(*hid_flow.hops[0])
    gate_flow.go(*hid_flow.hops[0])
    for k in (1, 2, 3):
        gate_flow.go(*hid_flow.hops[k])
        hid_flow.go(*gate_flow.hops[k])
    gates = gate_flow.finish().reshape(count, length, expert_count)
    gates = lax.dynamic_slice_in_dim(gates[source], group * local, local, 2)
    back_flows, mix_flows, probs_parts = [], [], []
    grad_in_w, grad_down_w = [0.0] * 4, 0.0
    for i in range(chunks):
        if i:
            ready = (back_flows[-1].finish(), mix_flows[-1].finish(), grad_in_w, grad_down_w)
            part = slice(i * size, (i + 1) * size)
            cot_flow = Flow(grid.gather(after(cotangent[part], *ready)))
            hid_flow = Flow(grid.gather(after(hidden2[part], *ready)))
        cot = jnp.concatenate(cot_flow.finish()).reshape(-1, width)
        lifted = dot(cot, weight_down, ROWS_BACK)
        while len(hid_flow.hops) < 5:
            hid_flow.go()
        total = size * count
        gate_dense = gates[:, i * size : (i + 1) * size].reshape(total, local)
        hid_flow.go(lifted, gate_dense)
        hid = jnp.concatenate(hid_flow.finish()).reshape(-1, width)
        part = total // 4
        slotted = (count // 4, size, width)
        done = [None] * 4

        def run(j, *events):
            kind = BF16 if j % 2 else F32
            gates = after(gate_dense, *events)
            done[j] = moe_rows(hid, lifted, gates, weight_in, ff, j * part, part, kind)
            return done[j][3].reshape(slotted)

        far = [None, None, None, run(3)]
        far[2] = run(2, done[3][3])
        near = [None, None]
        flow = Flow(grid.scatter_early(far, lambda: near))
        flow.go()
        near[1] = run(1, *flow.hops[0])
        flow.go()
        near[0] = run(0, *flow.hops[1], done[1][3])
        flow.go()
        last = done[0][3]
        acts = [d[1] for d in done]
        grad_pre = jnp.concatenate([d[0] for d in done])
        wide = 2 * local * ff // 4
        columns = [grad_pre[:, q * wide : (q + 1) * wide] for q in range(4)]

        def weigh(q, *events):
            part = dot(after(hid, *events), columns[q], SUM_ROWS)
            grad_in_w[q] += part
            return part

        def mixed(j, *events):
            return dot(after(acts[j], *events), weight_down).astype(BF16).reshape(slotted)

        first = weigh(0, last)
        flow.go(first)
        mix = [None, None, mixed(2, *flow.hops[2]), mixed(3, *flow.hops[2])]
        flow.go(mix[2], mix[3])
        mix[0], mix[1] = mixed(0, *flow.hops[3]), mixed(1, *flow.hops[3])
        second = weigh(1, *flow.hops[3])
        if i == chunks - 1:
            gone = [g.astype(BF16).reshape(dp, block, wide) for g in grad_in_w[:1]]
            home = [swap(gone[0])]
            flow.go(mix[0], mix[1], second, home[0])
        else:
            flow.go()
        third = weigh(2, *flow.hops[4])
        flow.go(third)
        if i < chunks - 1:
            weigh(3)
        back_flows.append(flow)
        mix_flow = Flow(grid.scatter(mix, BF16))
        mix_flow.go(*flow.hops[4])
        mix_flows.append(mix_flow)
        probs_part = jnp.concatenate([d[2] for d in done])
        probs_parts.append(probs_part.reshape(count, size, local))
        act_gated = jnp.concatenate(acts)
        if i < chunks - 1:
            grad_down_w += dot(act_gated, cot, SUM_ROWS)

    def send(q, *events):
        home.append(swap(after(grad_in_w[q].astype(BF16).reshape(dp, block, wide), *events)))

    probs_all = jnp.concatenate(probs_parts, axis=1)[back]
    place = (jnp.arange(expert_count) // local == group).astype(F32)
    probs_wide = (jnp.tile(probs_all, (1, 1, ex)) * place).reshape(
        count, length * expert_count // 128, 128
    )
    grad_probs = grid.small_scatter(probs_wide).reshape(length, expert_count)
    grad_probs = jnp.where(chosen, grad_probs, 0.0)

    grad_logits = (
        router_probs * (grad_probs - jnp.sum(router_probs * grad_probs, axis=-1, keepdims=True))
    ).astype(BF16)
    grad_router_part = dot(hidden2, grad_logits, SUM_ROWS)
    grad_hidden2 = jnp.concatenate([f.finish() for f in back_flows]) + dot(grad_logits, router, ROWS_BACK)
    grad_gain_moe = jnp.sum(grad_hidden2 * normed2, axis=0)
    grad_middle = grad_top + normalize_back(grad_hidden2 * gains[1], normed2, factor2)
    grad_mid_b = grad_middle.astype(BF16)
    grad_attended = reorder(dot(grad_mid_b, proj_out, ROWS_BACK).astype(BF16), back)
    grad_heads = by_heads(
        exchange(jnp.swapaxes(grad_attended.reshape(length, ex, span), 0, 1)).reshape(
            ex * length, span
        )
    )
    quarter = width // 4
    out_parts = [
        dot(attended_s[:, j * quarter : (j + 1) * quarter], grad_mid_b, SUM_ROWS).reshape(
            count // 4, rows, width
        )
        for j in range(4)
    ]
    out_flow = Flow(grid.scatter(out_parts))
    send(1, grad_mid_b)
    out_flow.go(grad_mid_b)
    mix_flow.go(grad_mid_b)
    fourth = weigh(3, grad_attended)
    grad_heads = after(grad_heads, fourth, *mix_flow.hops[1])
    send(2, grad_heads)
    mix_flow.go(grad_heads)
    out_flow.go(grad_heads)
    grad_queries, grad_keys, grad_values = attend_back(
        queries, key_rows, values, weights_f, attended_h, grad_heads
    )
    flat = (ex * length, span)
    grad_qscaled = rotate(grad_queries, cosine, sine_table, True).reshape(flat)
    grad_kscaled = rotate(grad_keys, cosine, sine_table, True).reshape(flat)
    up_q, up_k = grad_qscaled * gain_q, grad_kscaled * gain_k
    along = jnp.stack([jnp.sum(up_q * query_normed, axis=-1), jnp.sum(up_k * key_normed, axis=-1)])
    along = (grid.group_sum(along) / width)[:, :, None]
    along = after(along, *mix_flow.hops[2], *out_flow.hops[1])
    mix_flow.go(along)
    out_flow.go(along)
    grad_projected = jnp.concatenate(
        [
            query_factor * (up_q - query_normed * along[0]),
            key_factor * (up_k - key_normed * along[1]),
            grad_values.reshape(flat),
        ],
        axis=1,
    ).astype(BF16)
    mid = width // 2
    hidden1_s = reorder(hidden1_g, dp_source)
    proj_flow = Flow(
        grid.dp_scatter(
            [
                dot(hidden1_s[:, h * mid : (h + 1) * mid], grad_projected, SUM_ROWS).reshape(
                    grid.size["y"], 2, block, 3 * span
                )
                for h in range(2)
            ]
        )
    )
    proj_flow.go(home[1], home[2])
    send(3, grad_projected)
    proj_flow.go(home[3], *mix_flow.hops[3], *out_flow.hops[2])
    mix_flow.go(*proj_flow.hops[0])
    out_flow.go(*proj_flow.hops[0])
    grad_down_w += dot(after(act_gated, *proj_flow.hops[0]), cot, SUM_ROWS)
    proj_flow.go(grad_down_w, *mix_flow.hops[4], *out_flow.hops[3])
    mix_flow.go(*proj_flow.hops[1])
    out_flow.go(*proj_flow.hops[1])
    home = after(home, *proj_flow.hops[1])
    grad_expert_in = undeal(home) if ff == 128 else undeal_narrow(home, ff)
    proj_flow.go(grad_expert_in, *mix_flow.hops[5], *out_flow.hops[4])
    out_flow.go(*proj_flow.hops[2])
    grad_proj = proj_flow.finish()
    block_out = middle + jnp.concatenate([f.finish() for f in mix_flows])
    grad_out_projection = out_flow.finish()
    grad_expert_down = grad_down_w.reshape(local, ff, width)
    grad_proj = exchange(grad_proj.astype(BF16).reshape(ex, rows, 3 * span)).astype(F32)
    grad_in_projection = (
        grad_proj.reshape(ex, rows, 3, span).transpose(1, 2, 0, 3).reshape(rows, 3 * width)
    )
    grad_hidden1 = dot(grad_projected, proj, ROWS_BACK).astype(BF16)
    grad_hidden1 = jnp.sum(exchange(grad_hidden1.reshape(ex, length, width)).astype(F32), axis=0)
    own = lax.dynamic_slice_in_dim(normed1_g, group * length, length, 0)
    own_factor = lax.dynamic_slice_in_dim(factor1, group * length, length, 0)
    gain_one = jnp.sum(grad_hidden1 * own, axis=0)
    input_grad = grad_middle + normalize_back(grad_hidden1 * gains[0], own, own_factor)


    def widen(values):
        return lax.dynamic_update_slice_in_dim(jnp.zeros((width,), F32), values, group * span, 0)

    grad_gain_part = jnp.stack(
        [
            gain_one,
            grad_gain_moe,
            widen(jnp.sum(grad_qscaled * query_normed, axis=0)),
            widen(jnp.sum(grad_kscaled * key_normed, axis=0)),
        ]
    )
    last = jnp.concatenate(
        [
            jnp.swapaxes(grad_gain_part.reshape(4, count, rows), 0, 1).reshape(count, -1),
            grad_router_part.reshape(count, -1),
        ],
        axis=1,
    )
    last = last.reshape(count, -1, 128 if last.shape[1] % 128 == 0 else 64)
    last_flow = Flow(grid.small_sum(last))
    last_flow.go(*proj_flow.hops[0])
    last_flow.go(*proj_flow.hops[1])
    last_flow.go(*proj_flow.hops[1])
    last_flow.go(grad_proj)
    last = last_flow.finish()
    last = last.reshape(-1)
    grad_norm_gains = last[: 4 * rows].reshape(4, rows)
    grad_router = last[4 * rows :].reshape(rows, expert_count)
    return (
        block_out,
        input_grad,
        grad_in_projection,
        grad_out_projection,
        grad_router,
        grad_norm_gains,
        grad_expert_in,
        grad_expert_down,
    )


def solution(mesh):
    both = P(AXES, None)
    split = P("expert", "dp", None)
    in_specs = (both,) * 8 + (P(None, AXES), split, split)
    out_specs = (both,) * 5 + (P(None, AXES), split, split)
    return jax.shard_map(
        per_device, mesh=mesh, in_specs=in_specs, out_specs=out_specs, check_vma=False
    )
```

```python
import functools

import jax
import jax.numpy as jnp
import numpy as np
from jax import lax
from jax.experimental import pallas as pl
from jax.experimental.pallas import tpu as pltpu
from jax.sharding import PartitionSpec as P

HEADS = 16
HEAD_DIM = 128
EPSILON = 1e-05
ROPE_BASE = 10000.0
MASKED = -1e30
AXES = ("dp", "expert")
BF16 = jnp.bfloat16
F32 = jnp.float32
ROWS_BACK = (((1,), (1,)), ((), ()))
SUM_ROWS = (((0,), (0,)), ((), ()))


def dot(left, right, dims=(((1,), (0,)), ((), ()))):
    return lax.dot_general(left, right, dims, preferred_element_type=F32)


def after(value, *others):
    return lax.optimization_barrier((value,) + others)[0] if others else value


class Flow:
    def __init__(self, steps):
        self.steps, self.hops, self.result = steps, [], None
        next(steps)

    def go(self, *events):
        if self.result is not None:
            return
        try:
            self.hops.append(self.steps.send(events))
        except StopIteration as stop:
            self.result = stop.value
            assert self.result is not None

    def finish(self):
        while self.result is None:
            self.go()
        return self.result


def normalize(tensor):
    factor = lax.rsqrt(jnp.mean(tensor * tensor, axis=-1, keepdims=True) + EPSILON)
    return (tensor * factor, factor)


def normalize_back(upstream, normed, factor):
    return factor * (upstream - normed * jnp.mean(upstream * normed, axis=-1, keepdims=True))


def rope_tables(length):
    half_dim = HEAD_DIM // 2
    position = jnp.arange(length).astype(F32)
    frequency = ROPE_BASE ** (-2.0 * jnp.arange(half_dim).astype(F32) / HEAD_DIM)
    angles = position[:, None] * frequency[None, :]
    return (jnp.cos(angles), jnp.sin(angles))


def rotate(tensor, cosine, sine_table, inverse):
    half = HEAD_DIM // 2
    first_half, second_half = tensor[..., :half], tensor[..., half:]
    cosine, sine_table = cosine[None, :, None, :], sine_table[None, :, None, :]
    if inverse:
        sine_table = -sine_table
    return jnp.concatenate(
        [
            first_half * cosine - second_half * sine_table,
            second_half * cosine + first_half * sine_table,
        ],
        axis=-1,
    )


class Grid:
    def __init__(self):
        self.dp = lax.axis_size("dp")
        self.ex = lax.axis_size("expert")
        self.count = self.dp * self.ex
        self.size = {"z": 4, "y": self.dp // 4, "x": self.ex // 2, "c": 2}
        self.size["A"], self.size["B"] = self.size["y"], self.size["x"]
        self.swap = self.size["x"] == self.size["y"]
        d, e = lax.axis_index("dp"), lax.axis_index("expert")
        self.linear = d * self.ex + e
        ny = self.size["y"]
        self.at = {"z": d // ny, "y": d % ny, "x": e // 2, "c": e % 2}

    def real(self, axis, core):
        if axis in "AB":
            return "yx"[(axis == "B") != (core == 1 and self.swap)]
        return axis

    def index(self, p):
        return (p["z"] * self.size["y"] + p["y"]) * self.ex + p["x"] * 2 + p["c"]

    def move(self, value, axis, kind="pair"):
        s = self.size
        if s[axis] == 2:
            moves = {0: 1, 1: 0}
        else:
            moves = {
                "pair": {0: 1, 1: 0, 2: 3, 3: 2},
                "mid": {1: 2, 2: 1},
                "out": {1: 0, 2: 3},
                "in": {0: 1, 3: 2},
            }[kind]
        pairs = []
        for i in range(self.count):
            d, e = divmod(i, self.ex)
            here = {"z": d // s["y"], "y": d % s["y"], "x": e // 2, "c": e % 2}
            line = self.real(axis, here["c"])
            if here[line] in moves:
                pairs.append((i, self.index({**here, line: moves[here[line]]})))
        return lax.ppermute(value, AXES, pairs)

    def middle(self, axis):
        at = self.at[self.real(axis, 0)]
        if axis in "AB" and self.swap:
            at = jnp.where(self.at["c"] == 0, at, self.at[self.real(axis, 1)])
        return (at == 1) | (at == 2)

    def slots(self, axis):
        n = self.size[axis]
        table = {
            1: [[0]],
            2: [[0, 1], [1, 0]],
            4: [[0, 1, 2, 3], [1, 0, 2, 3], [2, 3, 1, 0], [3, 2, 1, 0]],
        }[n]
        return jnp.asarray(np.array(table, np.int32))[self.at[axis]]

    def sources(self):
        c, y, x, z = [self.slots(a) for a in "cyxz"]
        z, c = z.reshape(2, 1, 1, 1, 2), c.reshape(1, -1, 1, 1, 1)
        along_b, along_a = (1, 1, -1, 1, 1), (1, 1, 1, -1, 1)
        xs, ys = x.reshape(along_b), y.reshape(along_a)
        if self.swap:
            xs = jnp.where(c == 0, xs, x.reshape(along_a))
            ys = jnp.where(c == 0, ys, y.reshape(along_b))
        return ((z * self.size["y"] + ys) * self.ex + xs * 2 + c).reshape(-1)

    def dp_sources(self):
        z = self.slots("z").reshape(2, 1, 2)
        return (z * self.size["y"] + self.slots("y").reshape(1, -1, 1)).reshape(-1)

    def line_gather(self, value, axis):
        n = self.size[axis]
        if n == 1:
            return [value]
        pair = self.move(value, axis)
        if n == 2:
            return [value, pair]
        m0, m1 = self.move(value, axis, "mid"), self.move(pair, axis, "mid")
        o0, o1 = self.move(m0, axis, "out"), self.move(m1, axis, "out")
        mid = self.middle(axis)
        return [value, pair, jnp.where(mid, m0, o0), jnp.where(mid, m1, o1)]

    def line_reduce(self, slots, axis, kind=BF16):
        n = self.size[axis]
        slots = [slots[0].astype(F32)] + list(slots[1:])

        def sent(value, *way):
            return self.move(value.astype(kind), axis, *way).astype(F32)

        if n == 1:
            return slots[0]
        if n == 2:
            return slots[0] + sent(slots[1])
        m3 = sent(slots[3] + sent(slots[3], "in"), "mid")
        m2 = sent(slots[2] + sent(slots[2], "in"), "mid")
        return slots[0] + m2 + sent(slots[1] + m3)

    def z_hops(self, value, events):
        value = after(value, *events)
        pair, m0 = self.move(value, "z"), self.move(value, "z", "mid")
        events = yield (pair, m0)
        pair, m0 = after((pair, m0), *events)
        m1, o0 = self.move(pair, "z", "mid"), self.move(m0, "z", "out")
        events = yield (m1, o0)
        mid = self.middle("z")
        near = jnp.stack([value, pair])
        m1, near = after((m1, near), *events)
        o1 = self.move(m1, "z", "out")
        return near, lambda o1: jnp.stack([jnp.where(mid, m0, o0), jnp.where(mid, m1, o1)]), o1

    def gather(self, value):
        events = yield
        near, far, o1 = yield from self.z_hops(value, events)
        na = self.line_gather(near, "A")
        events = yield (o1, *na[1:])
        o1, na = after((o1, na), *events)
        fa, nb = self.line_gather(far(o1), "A"), [self.line_gather(na[0], "B")]
        events = yield (*fa[1:], *nb[0][1:])
        na, fa = after((na, fa), *events)
        nb += [self.line_gather(v, "B") for v in na[1:]]
        fb = [self.line_gather(fa[0], "B")]
        events = yield (*nb[1][1:], *fb[0][1:])
        nb, fa = after((nb, fa), *events)
        fb += [self.line_gather(v, "B") for v in fa[1:]]
        count = self.size["B"]
        block = jnp.concatenate([row[i] for i in range(count) for row in nb])
        nc = self.line_gather(block, "c")
        events = yield (*fb[1][1:], *nc[1:])
        fb = after(fb, *events)
        block = jnp.concatenate([row[i] for i in range(count) for row in fb])
        return nc + self.line_gather(block, "c")

    def lines(self, total):
        return [total[i] for i in range(total.shape[0])]

    def z_sum(self, near, far, events):
        def sent(value, way="pair"):
            return self.move(value.astype(BF16), "z", way)

        near, far = after((near, far), *events)
        o3, o2 = sent(far[1], "in"), sent(far[0], "in")
        events = yield (o3, o2)
        far, o3, o2 = after((far, o3, o2), *events)
        m3, m2 = sent(far[1] + o3.astype(F32), "mid"), sent(far[0] + o2.astype(F32), "mid")
        events = yield (m3, m2)
        near, m3, m2 = after((near, m3, m2), *events)
        pair = sent(near[1] + m3.astype(F32))
        events = yield (pair,)
        return near[0] + m2.astype(F32) + after(pair, *events).astype(F32)

    def unfold(self, total):
        return total.reshape((self.size["B"], self.size["A"], 2) + total.shape[1:])

    def scatter(self, groups, kind=F32):
        events = yield
        far, near = after((groups[2:], groups[:2]), *events)
        far = self.unfold(self.line_reduce(far, "c").astype(kind))
        near = self.unfold(self.line_reduce(near, "c").astype(kind))
        for axis in "BA":
            events = yield (far, near)
            far, near = after((far, near), *events)
            far = self.line_reduce(self.lines(far), axis).astype(kind)
            near = self.line_reduce(self.lines(near), axis).astype(kind)
        events = yield (far, near)
        return (yield from self.z_sum(near, far, events))

    def scatter_early(self, groups, late):
        yield
        far = self.unfold(self.line_reduce(groups[2:], "c"))
        yield (far,)
        far = self.line_reduce(self.lines(far), "B")
        yield (far,)
        far = self.line_reduce(self.lines(far), "A")
        near = self.unfold(self.line_reduce(late(), "c"))
        events = yield (far, near)
        near = self.line_reduce(self.lines(after(near, *events)), "B")
        o3, o2 = self.move(far[1].astype(BF16), "z", "in"), self.move(far[0].astype(BF16), "z", "in")
        events = yield (near, o3, o2)
        near, o3, o2 = after((near, o3, o2), *events)
        near = self.line_reduce(self.lines(near), "A")
        m3 = self.move((far[1] + o3.astype(F32)).astype(BF16), "z", "mid")
        m2 = self.move((far[0] + o2.astype(F32)).astype(BF16), "z", "mid")
        events = yield (near, m3, m2)
        near, m3, m2 = after((near, m3, m2), *events)
        pair = self.move((near[1] + m3.astype(F32)).astype(BF16), "z")
        events = yield (pair,)
        return near[0] + m2.astype(F32) + after(pair, *events).astype(F32)

    def dp_gather(self, value):
        events = yield
        near, far, o1 = yield from self.z_hops(value, events)
        ny = self.line_gather(near, "y")
        events = yield (o1, *ny[1:])
        fy = self.line_gather(far(after(o1, *events)), "y")
        events = yield (*fy[1:],)
        z, y = self.slots("z"), self.slots("y")
        n = value.shape[0]
        whole = jnp.zeros((n * self.dp,) + value.shape[1:], value.dtype)
        for h, line in enumerate((ny, fy)):
            for j, got in enumerate(line):
                for k in range(2):
                    place = (z[2 * h + k] * self.size["y"] + y[j]) * n
                    whole = lax.dynamic_update_slice_in_dim(whole, got[k], place, 0)
        return whole

    def dp_scatter(self, halves):
        events = yield
        near, far = after(halves, *events)
        far = self.line_reduce(self.lines(far), "y")
        events = yield (far,)
        far, near = after((far, near), *events)
        near = self.line_reduce(self.lines(near), "y")
        return (yield from self.z_sum(near, far, ()))

    def flip(self, value, bit):
        return lax.ppermute(value, AXES, [(i, i ^ bit) for i in range(self.count)])

    def small_gather(self, value):
        held, bit = value[None], 1
        while bit < self.count:
            events = yield (held,)
            held = after(held, *events)
            held = jnp.concatenate([held, self.flip(held, bit)])
            bit *= 2
        return held[self.linear ^ jnp.arange(self.count)]

    def small_scatter(self, value):
        held = value[self.linear ^ jnp.arange(self.count)]
        bit = self.count // 2
        while bit:
            held = held[:bit] + self.flip(held[bit:], bit)
            bit //= 2
        return held[0]

    def small_sum(self, value):
        held, bit = value[self.linear ^ jnp.arange(self.count)], 1
        while bit < self.count:
            events = yield (held,)
            held = after(held, *events)
            held = held.reshape((held.shape[0] // 2, 2) + held.shape[1:])
            held = held[:, 0] + self.flip(held[:, 1], bit)
            bit *= 2
        return held[0]

    def group_sum(self, value):
        total = value
        for r in range(1, self.ex):
            total = total + self.flip(value, r)
        return total


def exchange(value):
    return lax.all_to_all(value, "expert", split_axis=0, concat_axis=0, tiled=True)


def moe_kernel(ff, local, x_ref, lift_ref, gate_ref, w_ref, grad_ref, act_ref, sum_ref, back_ref):
    x = x_ref[...]
    per = 128 // ff
    lane = lax.broadcasted_iota(jnp.int32, (x.shape[0], 128), 1)
    for b in range(local // per):
        wide, narrow = pl.ds(256 * b, 256), pl.ds(128 * b, 128)
        pre_act = dot(x, w_ref[:, wide])
        gate_part, up_part = pre_act[:, :128], pre_act[:, 128:]
        spread = jnp.broadcast_to(gate_ref[:, pl.ds(b * per, 1)], lane.shape)
        for k in range(1, per):
            spread = jnp.where(
                lane < k * ff,
                spread,
                jnp.broadcast_to(gate_ref[:, pl.ds(b * per + k, 1)], lane.shape),
            )
        lifted = lift_ref[:, narrow]
        sig = 1.0 / (1.0 + jnp.exp(-gate_part))
        act = (gate_part * sig * up_part).astype(BF16).astype(F32)
        act_ref[:, narrow] = (act * spread).astype(BF16)
        terms = act * lifted
        for k in range(per):
            mine = jnp.where((lane >= k * ff) & (lane < (k + 1) * ff), terms, 0.0)
            sum_ref[:, pl.ds(b * per + k, 1)] = jnp.sum(mine, axis=1, keepdims=True)
        grad_act = lifted * spread
        grad_gate = grad_act * up_part * sig * (1.0 + gate_part * (1.0 - sig))
        grad_ref[:, pl.ds(256 * b, 128)] = grad_gate.astype(BF16)
        grad_ref[:, pl.ds(256 * b + 128, 128)] = (grad_act * gate_part * sig).astype(BF16)
    back_ref[...] = dot(grad_ref[...], w_ref[...], ROWS_BACK).astype(back_ref.dtype)


def moe_rows(x, lifted, gates, weight, ff, start, total, kind):
    width, wide = weight.shape
    local = gates.shape[1]
    tile = 256 if total % 256 == 0 else 128
    skip = start // tile
    row = lambda n: pl.BlockSpec((tile, n), lambda i: (i + skip, 0))
    out = lambda n: pl.BlockSpec((tile, n), lambda i: (i, 0))
    return pl.pallas_call(
        functools.partial(moe_kernel, ff, local),
        grid=(total // tile,),
        in_specs=[
            row(width),
            row(wide // 2),
            row(local),
            pl.BlockSpec((width, wide), lambda i: (0, 0)),
        ],
        out_specs=[out(wide), out(wide // 2), out(local), out(width)],
        out_shape=[
            jax.ShapeDtypeStruct((total, wide), BF16),
            jax.ShapeDtypeStruct((total, wide // 2), BF16),
            jax.ShapeDtypeStruct((total, local), F32),
            jax.ShapeDtypeStruct((total, width), kind),
        ],
        compiler_params=pltpu.CompilerParams(vmem_limit_bytes=56 * 1024 * 1024),
        cost_estimate=pl.CostEstimate(
            flops=4 * total * width * wide, bytes_accessed=total * width * 12, transcendentals=0
        ),
    )(x, lifted, gates, weight)


def deal_kernel(dp, in_ref, out_ref):
    for p in range(dp):
        out_ref[p] = in_ref[0, :, 128 * p : 128 * (p + 1)]


def deal(expert_in, dp):
    local, rows, wide = expert_in.shape
    return pl.pallas_call(
        functools.partial(deal_kernel, dp),
        grid=(local, 2),
        in_specs=[pl.BlockSpec((1, rows, wide // 2), lambda e, g: (e, 0, g))],
        out_specs=pl.BlockSpec((dp, rows, 128), lambda e, g: (0, 0, 2 * e + g)),
        out_shape=jax.ShapeDtypeStruct((dp, rows, local * 256), expert_in.dtype),
        compiler_params=pltpu.CompilerParams(vmem_limit_bytes=32 * 1024 * 1024),
    )(expert_in)


def undeal_kernel(parts, each, *refs):
    out_ref = refs[parts]
    e, g = pl.program_id(0), pl.program_id(1)
    for h in range(parts):

        @pl.when(e // each == h)
        def _():
            column = pl.multiple_of((2 * (e - h * each) + g) * 128, 128)
            for p in range(refs[h].shape[0]):
                piece = refs[h][p, :, pl.ds(column, 128)]
                out_ref[0, :, 128 * p : 128 * (p + 1)] = piece.astype(F32)


def undeal(pieces):
    parts = len(pieces)
    dp, rows, wide = pieces[0].shape
    each = wide // 256
    return pl.pallas_call(
        functools.partial(undeal_kernel, parts, each),
        grid=(parts * each, 2),
        in_specs=[pl.BlockSpec((dp, rows, wide), lambda e, g: (0, 0, 0))] * parts,
        out_specs=pl.BlockSpec((1, rows, dp * 128), lambda e, g: (e, 0, g)),
        out_shape=jax.ShapeDtypeStruct((parts * each, rows, 2 * dp * 128), F32),
        compiler_params=pltpu.CompilerParams(vmem_limit_bytes=48 * 1024 * 1024),
    )(*pieces)


def deal_narrow(expert_in, dp):
    local, rows, wide = expert_in.shape
    ff = wide // 2 // dp
    split = expert_in.reshape(local * ff // 128, 128 // ff, rows, 2, dp, ff)
    return split.transpose(4, 2, 0, 3, 1, 5).reshape(dp, rows, 2 * local * ff)


def undeal_narrow(pieces, ff):
    whole = jnp.concatenate(pieces, axis=2)
    dp, rows, wide = whole.shape
    whole = whole.reshape(dp, rows, wide // 256, 2, 128 // ff, ff).astype(F32)
    return whole.transpose(2, 4, 1, 3, 0, 5).reshape(wide // 2 // ff, rows, 2 * dp * ff)


def swap(value):
    return lax.all_to_all(value, "dp", split_axis=0, concat_axis=0, tiled=True)


def masked(segment):
    length = segment.shape[1]
    row_index = lax.broadcasted_iota(jnp.int32, (length, length), 0)
    col_index = lax.broadcasted_iota(jnp.int32, (length, length), 1)
    return (segment[:, :, None] == segment[:, None, :]) & (col_index <= row_index)[None]


def attend(queries, key_rows, values, allowed):
    raw = jnp.einsum("sqhd,skhd->shqk", queries, key_rows, preferred_element_type=F32)
    scores = jnp.where(allowed[:, None], raw * HEAD_DIM ** (-0.5), MASKED)
    row_max = jnp.max(scores, axis=-1, keepdims=True)
    exp_terms = jnp.exp(scores - row_max)
    weights_f = exp_terms / jnp.sum(exp_terms, axis=-1, keepdims=True)
    attended = jnp.einsum(
        "shqk,skhd->sqhd", weights_f.astype(BF16), values, preferred_element_type=F32
    )
    return (attended.astype(BF16), weights_f)


def attend_back(queries, key_rows, values, weights_f, attended, grad_heads):
    weights_b = weights_f.astype(BF16)
    grad_values = jnp.einsum("shqk,sqhd->skhd", weights_b, grad_heads, preferred_element_type=F32)
    grad_weights = jnp.einsum("sqhd,skhd->shqk", grad_heads, values, preferred_element_type=F32)
    row_delta = jnp.sum(grad_heads.astype(F32) * attended.astype(F32), axis=-1)
    row_delta = jnp.swapaxes(row_delta, 1, 2)[..., None]
    grad_scores = (weights_f * (grad_weights - row_delta) * HEAD_DIM ** (-0.5)).astype(BF16)
    grad_queries = jnp.einsum(
        "shqk,skhd->sqhd", grad_scores, key_rows, preferred_element_type=F32
    )
    grad_keys = jnp.einsum("shqk,sqhd->skhd", grad_scores, queries, preferred_element_type=F32)
    return (grad_queries, grad_keys, grad_values)


def per_device(
    tokens,
    cotangent,
    segments,
    routes,
    slot_index,
    in_projection,
    out_projection,
    router_weight,
    norm_gains,
    expert_in,
    expert_down,
):
    grid = Grid()
    length, width = tokens.shape
    count, dp, ex = grid.count, grid.dp, grid.ex
    local = expert_in.shape[0]
    expert_count = ex * local
    ff = expert_down.shape[1]
    rows = width // count
    block = width // dp
    heads = HEADS // ex
    span = heads * HEAD_DIM
    group = lax.axis_index("expert")
    stage = lax.axis_index("dp")
    cosine, sine_table = rope_tables(length)
    source = grid.sources()
    ids = jnp.arange(count, dtype=source.dtype)
    back = jnp.sum(jnp.where(source[None, :] == ids[:, None], ids[None, :], 0), axis=1)
    dp_source = grid.dp_sources()
    chunks = 1 if length * count <= 4096 else length * count // 4096
    size = length // chunks

    def reorder(tensor, order):
        parts = order.shape[0]
        return jnp.take(
            tensor.reshape(tensor.shape[0], parts, width // parts), order, axis=1
        ).reshape(tensor.shape[0], width)

    small = jnp.concatenate(
        [
            norm_gains.reshape(-1),
            router_weight.reshape(-1),
            segments.astype(BF16).reshape(-1),
        ]
    )
    small = jnp.pad(small, (0, -small.shape[0] % 128)).reshape(-1, 128)
    small_flow = Flow(grid.small_gather(small))
    small_flow.go()

    piece = in_projection.reshape(rows, 3, ex, span).transpose(2, 0, 1, 3)
    piece = exchange(piece.reshape(ex, rows, 3 * span)).reshape(block, 3 * span)
    tokens_g = exchange(
        after(jnp.broadcast_to(tokens[None], (ex, length, width)), piece)
    )
    dense = Flow(grid.dp_gather(piece))
    out_flow = Flow(grid.gather(out_projection))
    cot_flow = Flow(grid.gather(cotangent[:size]))
    dealt = (deal if ff == 128 else deal_narrow)(after(expert_in, piece), dp)
    weight_down = expert_down.reshape(local * ff, width)

    quarter = local * ff // 2
    weights = []

    def fetch(*events):
        columns = slice(len(weights) * quarter, (len(weights) + 1) * quarter)
        weights.append(swap(after(dealt[:, :, columns], *events)).reshape(width, quarter))

    dense.go()
    small_flow.go(piece)
    out_flow.go(*dense.hops[0])
    cot_flow.go(*dense.hops[0])
    small_flow.go(*dense.hops[0])
    dense.go(tokens_g)
    out_flow.go(*dense.hops[1])
    cot_flow.go(*dense.hops[1])
    small_flow.go(*dense.hops[1])
    dense.go(dealt, *out_flow.hops[0], *cot_flow.hops[0])
    fetch(*dense.hops[2])
    out_flow.go(*dense.hops[2])
    small_flow.go(*dense.hops[2])
    dense.go(*out_flow.hops[1], *cot_flow.hops[1])
    cot_flow.go(*dense.hops[3])
    out_flow.go(*dense.hops[3], *out_flow.hops[2])
    proj = after(dense.finish(), weights[0])
    fetch(*dense.hops[3])
    small = small_flow.finish().reshape(count, -1)
    cuts = np.cumsum([4 * rows, rows * expert_count, length])
    all_gains, all_router, all_segments, _ = jnp.split(small, cuts, axis=1)
    gains = jnp.swapaxes(all_gains.reshape(count, 4, rows), 0, 1).reshape(4, width).astype(F32)
    router = all_router.reshape(width, expert_count)
    segment = lax.dynamic_slice_in_dim(
        all_segments.reshape(dp, ex, length), stage, 1, 0
    )[0].astype(jnp.int32)
    allowed = masked(segment)
    gain_q = lax.dynamic_slice_in_dim(gains[2], group * span, span)
    gain_k = lax.dynamic_slice_in_dim(gains[3], group * span, span)

    normed1_g, factor1 = normalize(tokens_g.reshape(ex * length, width).astype(F32))
    hidden1_g = (normed1_g * gains[0]).astype(BF16)
    projected = dot(hidden1_g, proj)
    query_raw, key_raw = projected[:, :span], projected[:, span : 2 * span]
    squares = jnp.stack([jnp.sum(query_raw**2, axis=-1), jnp.sum(key_raw**2, axis=-1)])
    squares = grid.group_sum(squares)
    squares = after(squares, weights[1], *out_flow.hops[3], *cot_flow.hops[2])
    fetch(squares)
    out_flow.go(squares)
    cot_flow.go(squares)
    factors = lax.rsqrt(squares / width + EPSILON)[:, :, None]
    query_factor, key_factor = factors[0], factors[1]
    proj_out = jnp.concatenate(out_flow.finish()).reshape(width, width)
    query_normed, key_normed = query_raw * query_factor, key_raw * key_factor

    def by_heads(tensor):
        return tensor.reshape(ex, length, heads, HEAD_DIM)

    queries = rotate(by_heads(query_normed * gain_q), cosine, sine_table, False).astype(BF16)
    key_rows = rotate(by_heads(key_normed * gain_k), cosine, sine_table, False).astype(BF16)
    values = by_heads(projected[:, 2 * span :].astype(BF16))
    attended_h, weights_f = attend(queries, key_rows, values, allowed)
    cot_flow.go(attended_h, *cot_flow.hops[3])
    attended = exchange(attended_h.reshape(ex, length, span))
    attended = after(attended, weights[2])
    fetch(attended)
    attended_c = jnp.swapaxes(attended, 0, 1).reshape(length, width)
    attended_s = reorder(attended_c, source)
    residual = tokens.astype(F32)
    middle = residual + dot(attended_s, proj_out)
    normed2, factor2 = normalize(middle)
    hidden2 = (normed2 * gains[1]).astype(BF16)
    hidden2 = after(hidden2, weights[3], *cot_flow.hops[4])
    weight_in = jnp.concatenate(weights, axis=1)
    router_probs = jax.nn.softmax(dot(hidden2, router), axis=-1)
    grad_top = cotangent.astype(F32)
    named = jnp.arange(expert_count, dtype=jnp.int32)
    chosen = jnp.any(routes[:, :, None] == named[None, None, :], axis=1)
    gates = jnp.where(chosen, router_probs, 0.0).reshape(-1, 128)

    hid_flow = Flow(grid.gather(hidden2[:size]))
    gate_flow = Flow(grid.small_gather(gates))
    cot_flow.go(hidden2)
    hid_flow.go()
    gate_flow.go()
    hid_flow.go(weight_in, *cot_flow.hops[5])
    cot_flow.go(*hid_flow.hops[0])
    gate_flow.go(*hid_flow.hops[0])
    for k in (1, 2, 3):
        gate_flow.go(*hid_flow.hops[k])
        hid_flow.go(*gate_flow.hops[k])
    gates = gate_flow.finish().reshape(count, length, expert_count)
    gates = lax.dynamic_slice_in_dim(gates[source], group * local, local, 2)
    back_flows, mix_flows, probs_parts = [], [], []
    grad_in_w, grad_down_w = [0.0] * 4, 0.0
    for i in range(chunks):
        if i:
            ready = (back_flows[-1].finish(), mix_flows[-1].finish(), grad_in_w, grad_down_w)
            part = slice(i * size, (i + 1) * size)
            cot_flow = Flow(grid.gather(after(cotangent[part], *ready)))
            hid_flow = Flow(grid.gather(after(hidden2[part], *ready)))
        cot = jnp.concatenate(cot_flow.finish()).reshape(-1, width)
        lifted = dot(cot, weight_down, ROWS_BACK)
        while len(hid_flow.hops) < 5:
            hid_flow.go()
        total = size * count
        gate_dense = gates[:, i * size : (i + 1) * size].reshape(total, local)
        hid_flow.go(lifted, gate_dense)
        hid = jnp.concatenate(hid_flow.finish()).reshape(-1, width)
        part = total // 4
        slotted = (count // 4, size, width)
        done = [None] * 4

        def run(j, *events):
            kind = BF16 if j % 2 else F32
            gates = after(gate_dense, *events)
            done[j] = moe_rows(hid, lifted, gates, weight_in, ff, j * part, part, kind)
            return done[j][3].reshape(slotted)

        far = [None, None, None, run(3)]
        far[2] = run(2, done[3][3])
        near = [None, None]
        flow = Flow(grid.scatter_early(far, lambda: near))
        flow.go()
        near[1] = run(1, *flow.hops[0])
        flow.go()
        near[0] = run(0, *flow.hops[1], done[1][3])
        flow.go()
        last = done[0][3]
        acts = [d[1] for d in done]
        grad_pre = jnp.concatenate([d[0] for d in done])
        wide = 2 * local * ff // 4
        columns = [grad_pre[:, q * wide : (q + 1) * wide] for q in range(4)]

        def weigh(q, *events):
            part = dot(after(hid, *events), columns[q], SUM_ROWS)
            grad_in_w[q] += part
            return part

        def mixed(j, *events):
            return dot(after(acts[j], *events), weight_down).astype(BF16).reshape(slotted)

        first = weigh(0, last)
        flow.go(first)
        mix = [None, None, mixed(2, *flow.hops[2]), mixed(3, *flow.hops[2])]
        flow.go(mix[2], mix[3])
        mix[0], mix[1] = mixed(0, *flow.hops[3]), mixed(1, *flow.hops[3])
        second = weigh(1, *flow.hops[3])
        if i == chunks - 1:
            gone = [g.astype(BF16).reshape(dp, block, wide) for g in grad_in_w[:1]]
            home = [swap(gone[0])]
            flow.go(mix[0], mix[1], second, home[0])
        else:
            flow.go()
        third = weigh(2, *flow.hops[4])
        flow.go(third)
        if i < chunks - 1:
            weigh(3)
        back_flows.append(flow)
        mix_flow = Flow(grid.scatter(mix, BF16))
        mix_flow.go(*flow.hops[4])
        mix_flows.append(mix_flow)
        probs_part = jnp.concatenate([d[2] for d in done])
        probs_parts.append(probs_part.reshape(count, size, local))
        act_gated = jnp.concatenate(acts)
        if i < chunks - 1:
            grad_down_w += dot(act_gated, cot, SUM_ROWS)

    def send(q, *events):
        home.append(swap(after(grad_in_w[q].astype(BF16).reshape(dp, block, wide), *events)))

    probs_all = jnp.concatenate(probs_parts, axis=1)[back]
    place = (jnp.arange(expert_count) // local == group).astype(F32)
    probs_wide = (jnp.tile(probs_all, (1, 1, ex)) * place).reshape(
        count, length * expert_count // 128, 128
    )
    grad_probs = grid.small_scatter(probs_wide).reshape(length, expert_count)
    grad_probs = jnp.where(chosen, grad_probs, 0.0)

    grad_logits = (
        router_probs * (grad_probs - jnp.sum(router_probs * grad_probs, axis=-1, keepdims=True))
    ).astype(BF16)
    grad_router_part = dot(hidden2, grad_logits, SUM_ROWS)
    grad_hidden2 = jnp.concatenate([f.finish() for f in back_flows]) + dot(grad_logits, router, ROWS_BACK)
    grad_gain_moe = jnp.sum(grad_hidden2 * normed2, axis=0)
    grad_middle = grad_top + normalize_back(grad_hidden2 * gains[1], normed2, factor2)
    grad_mid_b = grad_middle.astype(BF16)
    grad_attended = reorder(dot(grad_mid_b, proj_out, ROWS_BACK).astype(BF16), back)
    grad_heads = by_heads(
        exchange(jnp.swapaxes(grad_attended.reshape(length, ex, span), 0, 1)).reshape(
            ex * length, span
        )
    )
    quarter = width // 4
    out_parts = [
        dot(attended_s[:, j * quarter : (j + 1) * quarter], grad_mid_b, SUM_ROWS).reshape(
            count // 4, rows, width
        )
        for j in range(4)
    ]
    out_flow = Flow(grid.scatter(out_parts))
    send(1, grad_mid_b)
    mix_flow.go(grad_mid_b)
    fourth = weigh(3, grad_attended)
    grad_heads = after(grad_heads, fourth, *mix_flow.hops[1])
    send(2, grad_heads)
    mix_flow.go(grad_heads)
    out_flow.go(grad_heads)
    grad_queries, grad_keys, grad_values = attend_back(
        queries, key_rows, values, weights_f, attended_h, grad_heads
    )
    flat = (ex * length, span)
    grad_qscaled = rotate(grad_queries, cosine, sine_table, True).reshape(flat)
    grad_kscaled = rotate(grad_keys, cosine, sine_table, True).reshape(flat)
    up_q, up_k = grad_qscaled * gain_q, grad_kscaled * gain_k
    along = jnp.stack([jnp.sum(up_q * query_normed, axis=-1), jnp.sum(up_k * key_normed, axis=-1)])
    along = (grid.group_sum(along) / width)[:, :, None]
    along = after(along, *mix_flow.hops[2], *out_flow.hops[0])
    mix_flow.go(along)
    out_flow.go(along)
    grad_projected = jnp.concatenate(
        [
            query_factor * (up_q - query_normed * along[0]),
            key_factor * (up_k - key_normed * along[1]),
            grad_values.reshape(flat),
        ],
        axis=1,
    ).astype(BF16)
    mid = width // 2
    hidden1_s = reorder(hidden1_g, dp_source)
    proj_flow = Flow(
        grid.dp_scatter(
            [
                dot(hidden1_s[:, h * mid : (h + 1) * mid], grad_projected, SUM_ROWS).reshape(
                    grid.size["y"], 2, block, 3 * span
                )
                for h in range(2)
            ]
        )
    )
    proj_flow.go(home[1], home[2])
    send(3, grad_projected)
    proj_flow.go(home[3], *mix_flow.hops[3], *out_flow.hops[1])
    mix_flow.go(*proj_flow.hops[0])
    out_flow.go(*proj_flow.hops[0])
    grad_down_w += dot(after(act_gated, *proj_flow.hops[0]), cot, SUM_ROWS)
    proj_flow.go(grad_down_w, *mix_flow.hops[4], *out_flow.hops[2])
    mix_flow.go(*proj_flow.hops[1])
    out_flow.go(*proj_flow.hops[1])
    home = after(home, *proj_flow.hops[1])
    grad_expert_in = undeal(home) if ff == 128 else undeal_narrow(home, ff)
    proj_flow.go(grad_expert_in, *mix_flow.hops[5], *out_flow.hops[3])
    out_flow.go(*proj_flow.hops[2])
    grad_proj = proj_flow.finish()
    block_out = middle + jnp.concatenate([f.finish() for f in mix_flows])
    grad_out_projection = out_flow.finish()
    grad_expert_down = grad_down_w.reshape(local, ff, width)
    grad_proj = exchange(grad_proj.astype(BF16).reshape(ex, rows, 3 * span)).astype(F32)
    grad_in_projection = (
        grad_proj.reshape(ex, rows, 3, span).transpose(1, 2, 0, 3).reshape(rows, 3 * width)
    )
    grad_hidden1 = dot(grad_projected, proj, ROWS_BACK).astype(BF16)
    grad_hidden1 = jnp.sum(exchange(grad_hidden1.reshape(ex, length, width)).astype(F32), axis=0)
    own = lax.dynamic_slice_in_dim(normed1_g, group * length, length, 0)
    own_factor = lax.dynamic_slice_in_dim(factor1, group * length, length, 0)
    gain_one = jnp.sum(grad_hidden1 * own, axis=0)
    input_grad = grad_middle + normalize_back(grad_hidden1 * gains[0], own, own_factor)


    def widen(values):
        return lax.dynamic_update_slice_in_dim(jnp.zeros((width,), F32), values, group * span, 0)

    grad_gain_part = jnp.stack(
        [
            gain_one,
            grad_gain_moe,
            widen(jnp.sum(grad_qscaled * query_normed, axis=0)),
            widen(jnp.sum(grad_kscaled * key_normed, axis=0)),
        ]
    )
    last = jnp.concatenate(
        [
            jnp.swapaxes(grad_gain_part.reshape(4, count, rows), 0, 1).reshape(count, -1),
            grad_router_part.reshape(count, -1),
        ],
        axis=1,
    )
    last = last.reshape(count, -1, 128 if last.shape[1] % 128 == 0 else 64)
    last_flow = Flow(grid.small_sum(last))
    last_flow.go(*proj_flow.hops[1])
    last_flow.go(*proj_flow.hops[1])
    last_flow.go(*proj_flow.hops[2])
    last_flow.go(grad_proj)
    last = last_flow.finish()
    last = last.reshape(-1)
    grad_norm_gains = last[: 4 * rows].reshape(4, rows)
    grad_router = last[4 * rows :].reshape(rows, expert_count)
    return (
        block_out,
        input_grad,
        grad_in_projection,
        grad_out_projection,
        grad_router,
        grad_norm_gains,
        grad_expert_in,
        grad_expert_down,
    )


def solution(mesh):
    both = P(AXES, None)
    split = P("expert", "dp", None)
    in_specs = (both,) * 8 + (P(None, AXES), split, split)
    out_specs = (both,) * 5 + (P(None, AXES), split, split)
    return jax.shard_map(
        per_device, mesh=mesh, in_specs=in_specs, out_specs=out_specs, check_vma=False
    )
```

```python
import functools

import jax
import jax.numpy as jnp
import numpy as np
from jax import lax
from jax.experimental import pallas as pl
from jax.experimental.pallas import tpu as pltpu
from jax.sharding import PartitionSpec as P

HEADS = 16
HEAD_DIM = 128
EPSILON = 1e-05
ROPE_BASE = 10000.0
MASKED = -1e30
AXES = ("dp", "expert")
BF16 = jnp.bfloat16
F32 = jnp.float32
ROWS_BACK = (((1,), (1,)), ((), ()))
SUM_ROWS = (((0,), (0,)), ((), ()))


def dot(left, right, dims=(((1,), (0,)), ((), ()))):
    return lax.dot_general(left, right, dims, preferred_element_type=F32)


def after(value, *others):
    return lax.optimization_barrier((value,) + others)[0] if others else value


class Flow:
    def __init__(self, steps):
        self.steps, self.hops, self.result = steps, [], None
        next(steps)

    def go(self, *events):
        if self.result is not None:
            return
        try:
            self.hops.append(self.steps.send(events))
        except StopIteration as stop:
            self.result = stop.value
            assert self.result is not None

    def finish(self):
        while self.result is None:
            self.go()
        return self.result


def normalize(tensor):
    factor = lax.rsqrt(jnp.mean(tensor * tensor, axis=-1, keepdims=True) + EPSILON)
    return (tensor * factor, factor)


def normalize_back(upstream, normed, factor):
    return factor * (upstream - normed * jnp.mean(upstream * normed, axis=-1, keepdims=True))


def rope_tables(length):
    half_dim = HEAD_DIM // 2
    position = jnp.arange(length).astype(F32)
    frequency = ROPE_BASE ** (-2.0 * jnp.arange(half_dim).astype(F32) / HEAD_DIM)
    angles = position[:, None] * frequency[None, :]
    return (jnp.cos(angles), jnp.sin(angles))


def rotate(tensor, cosine, sine_table, inverse):
    half = HEAD_DIM // 2
    first_half, second_half = tensor[..., :half], tensor[..., half:]
    cosine, sine_table = cosine[None, :, None, :], sine_table[None, :, None, :]
    if inverse:
        sine_table = -sine_table
    return jnp.concatenate(
        [
            first_half * cosine - second_half * sine_table,
            second_half * cosine + first_half * sine_table,
        ],
        axis=-1,
    )


class Grid:
    def __init__(self):
        self.dp = lax.axis_size("dp")
        self.ex = lax.axis_size("expert")
        self.count = self.dp * self.ex
        self.size = {"z": 4, "y": self.dp // 4, "x": self.ex // 2, "c": 2}
        self.size["A"], self.size["B"] = self.size["y"], self.size["x"]
        self.swap = self.size["x"] == self.size["y"]
        d, e = lax.axis_index("dp"), lax.axis_index("expert")
        self.linear = d * self.ex + e
        ny = self.size["y"]
        self.at = {"z": d // ny, "y": d % ny, "x": e // 2, "c": e % 2}

    def real(self, axis, core):
        if axis in "AB":
            return "yx"[(axis == "B") != (core == 1 and self.swap)]
        return axis

    def index(self, p):
        return (p["z"] * self.size["y"] + p["y"]) * self.ex + p["x"] * 2 + p["c"]

    def move(self, value, axis, kind="pair"):
        s = self.size
        if s[axis] == 2:
            moves = {0: 1, 1: 0}
        else:
            moves = {
                "pair": {0: 1, 1: 0, 2: 3, 3: 2},
                "mid": {1: 2, 2: 1},
                "out": {1: 0, 2: 3},
                "in": {0: 1, 3: 2},
            }[kind]
        pairs = []
        for i in range(self.count):
            d, e = divmod(i, self.ex)
            here = {"z": d // s["y"], "y": d % s["y"], "x": e // 2, "c": e % 2}
            line = self.real(axis, here["c"])
            if here[line] in moves:
                pairs.append((i, self.index({**here, line: moves[here[line]]})))
        return lax.ppermute(value, AXES, pairs)

    def middle(self, axis):
        at = self.at[self.real(axis, 0)]
        if axis in "AB" and self.swap:
            at = jnp.where(self.at["c"] == 0, at, self.at[self.real(axis, 1)])
        return (at == 1) | (at == 2)

    def slots(self, axis):
        n = self.size[axis]
        table = {
            1: [[0]],
            2: [[0, 1], [1, 0]],
            4: [[0, 1, 2, 3], [1, 0, 2, 3], [2, 3, 1, 0], [3, 2, 1, 0]],
        }[n]
        return jnp.asarray(np.array(table, np.int32))[self.at[axis]]

    def sources(self):
        c, y, x, z = [self.slots(a) for a in "cyxz"]
        z, c = z.reshape(2, 1, 1, 1, 2), c.reshape(1, -1, 1, 1, 1)
        along_b, along_a = (1, 1, -1, 1, 1), (1, 1, 1, -1, 1)
        xs, ys = x.reshape(along_b), y.reshape(along_a)
        if self.swap:
            xs = jnp.where(c == 0, xs, x.reshape(along_a))
            ys = jnp.where(c == 0, ys, y.reshape(along_b))
        return ((z * self.size["y"] + ys) * self.ex + xs * 2 + c).reshape(-1)

    def dp_sources(self):
        z = self.slots("z").reshape(2, 1, 2)
        return (z * self.size["y"] + self.slots("y").reshape(1, -1, 1)).reshape(-1)

    def line_gather(self, value, axis):
        n = self.size[axis]
        if n == 1:
            return [value]
        pair = self.move(value, axis)
        if n == 2:
            return [value, pair]
        m0, m1 = self.move(value, axis, "mid"), self.move(pair, axis, "mid")
        o0, o1 = self.move(m0, axis, "out"), self.move(m1, axis, "out")
        mid = self.middle(axis)
        return [value, pair, jnp.where(mid, m0, o0), jnp.where(mid, m1, o1)]

    def line_reduce(self, slots, axis, kind=BF16):
        n = self.size[axis]
        slots = [slots[0].astype(F32)] + list(slots[1:])

        def sent(value, *way):
            return self.move(value.astype(kind), axis, *way).astype(F32)

        if n == 1:
            return slots[0]
        if n == 2:
            return slots[0] + sent(slots[1])
        m3 = sent(slots[3] + sent(slots[3], "in"), "mid")
        m2 = sent(slots[2] + sent(slots[2], "in"), "mid")
        return slots[0] + m2 + sent(slots[1] + m3)

    def z_hops(self, value, events):
        value = after(value, *events)
        pair, m0 = self.move(value, "z"), self.move(value, "z", "mid")
        events = yield (pair, m0)
        pair, m0 = after((pair, m0), *events)
        m1, o0 = self.move(pair, "z", "mid"), self.move(m0, "z", "out")
        events = yield (m1, o0)
        mid = self.middle("z")
        near = jnp.stack([value, pair])
        m1, near = after((m1, near), *events)
        o1 = self.move(m1, "z", "out")
        return near, lambda o1: jnp.stack([jnp.where(mid, m0, o0), jnp.where(mid, m1, o1)]), o1

    def gather(self, value):
        events = yield
        near, far, o1 = yield from self.z_hops(value, events)
        na = self.line_gather(near, "A")
        events = yield (o1, *na[1:])
        o1, na = after((o1, na), *events)
        fa, nb = self.line_gather(far(o1), "A"), [self.line_gather(na[0], "B")]
        events = yield (*fa[1:], *nb[0][1:])
        na, fa = after((na, fa), *events)
        nb += [self.line_gather(v, "B") for v in na[1:]]
        fb = [self.line_gather(fa[0], "B")]
        events = yield (*nb[1][1:], *fb[0][1:])
        nb, fa = after((nb, fa), *events)
        fb += [self.line_gather(v, "B") for v in fa[1:]]
        count = self.size["B"]
        block = jnp.concatenate([row[i] for i in range(count) for row in nb])
        nc = self.line_gather(block, "c")
        events = yield (*fb[1][1:], *nc[1:])
        fb = after(fb, *events)
        block = jnp.concatenate([row[i] for i in range(count) for row in fb])
        return nc + self.line_gather(block, "c")

    def lines(self, total):
        return [total[i] for i in range(total.shape[0])]

    def z_sum(self, near, far, events):
        def sent(value, way="pair"):
            return self.move(value.astype(BF16), "z", way)

        near, far = after((near, far), *events)
        o3, o2 = sent(far[1], "in"), sent(far[0], "in")
        events = yield (o3, o2)
        far, o3, o2 = after((far, o3, o2), *events)
        m3, m2 = sent(far[1] + o3.astype(F32), "mid"), sent(far[0] + o2.astype(F32), "mid")
        events = yield (m3, m2)
        near, m3, m2 = after((near, m3, m2), *events)
        pair = sent(near[1] + m3.astype(F32))
        events = yield (pair,)
        return near[0] + m2.astype(F32) + after(pair, *events).astype(F32)

    def unfold(self, total):
        return total.reshape((self.size["B"], self.size["A"], 2) + total.shape[1:])

    def scatter(self, groups, kind=F32):
        events = yield
        far, near = after((groups[2:], groups[:2]), *events)
        far = self.unfold(self.line_reduce(far, "c").astype(kind))
        near = self.unfold(self.line_reduce(near, "c").astype(kind))
        for axis in "BA":
            events = yield (far, near)
            far, near = after((far, near), *events)
            far = self.line_reduce(self.lines(far), axis).astype(kind)
            near = self.line_reduce(self.lines(near), axis).astype(kind)
        events = yield (far, near)
        return (yield from self.z_sum(near, far, events))

    def scatter_early(self, groups, late):
        yield
        far = self.unfold(self.line_reduce(groups[2:], "c"))
        yield (far,)
        far = self.line_reduce(self.lines(far), "B")
        yield (far,)
        far = self.line_reduce(self.lines(far), "A")
        near = self.unfold(self.line_reduce(late(), "c"))
        events = yield (far, near)
        near = self.line_reduce(self.lines(after(near, *events)), "B")
        o3, o2 = self.move(far[1].astype(BF16), "z", "in"), self.move(far[0].astype(BF16), "z", "in")
        events = yield (near, o3, o2)
        near, o3, o2 = after((near, o3, o2), *events)
        near = self.line_reduce(self.lines(near), "A")
        m3 = self.move((far[1] + o3.astype(F32)).astype(BF16), "z", "mid")
        m2 = self.move((far[0] + o2.astype(F32)).astype(BF16), "z", "mid")
        events = yield (near, m3, m2)
        near, m3, m2 = after((near, m3, m2), *events)
        pair = self.move((near[1] + m3.astype(F32)).astype(BF16), "z")
        events = yield (pair,)
        return near[0] + m2.astype(F32) + after(pair, *events).astype(F32)

    def dp_gather(self, value):
        events = yield
        near, far, o1 = yield from self.z_hops(value, events)
        ny = self.line_gather(near, "y")
        events = yield (o1, *ny[1:])
        fy = self.line_gather(far(after(o1, *events)), "y")
        events = yield (*fy[1:],)
        z, y = self.slots("z"), self.slots("y")
        n = value.shape[0]
        whole = jnp.zeros((n * self.dp,) + value.shape[1:], value.dtype)
        for h, line in enumerate((ny, fy)):
            for j, got in enumerate(line):
                for k in range(2):
                    place = (z[2 * h + k] * self.size["y"] + y[j]) * n
                    whole = lax.dynamic_update_slice_in_dim(whole, got[k], place, 0)
        return whole

    def dp_scatter(self, halves):
        events = yield
        near, far = after(halves, *events)
        far = self.line_reduce(self.lines(far), "y")
        events = yield (far,)
        far, near = after((far, near), *events)
        near = self.line_reduce(self.lines(near), "y")
        return (yield from self.z_sum(near, far, ()))

    def flip(self, value, bit):
        return lax.ppermute(value, AXES, [(i, i ^ bit) for i in range(self.count)])

    def small_gather(self, value):
        held, bit = value[None], 1
        while bit < self.count:
            events = yield (held,)
            held = after(held, *events)
            held = jnp.concatenate([held, self.flip(held, bit)])
            bit *= 2
        return held[self.linear ^ jnp.arange(self.count)]

    def small_scatter(self, value):
        held = value[self.linear ^ jnp.arange(self.count)]
        bit = self.count // 2
        while bit:
            held = held[:bit] + self.flip(held[bit:], bit)
            bit //= 2
        return held[0]

    def group_sum(self, value):
        total = value
        for r in range(1, self.ex):
            total = total + self.flip(value, r)
        return total


def exchange(value):
    return lax.all_to_all(value, "expert", split_axis=0, concat_axis=0, tiled=True)


def moe_kernel(ff, local, x_ref, lift_ref, gate_ref, w_ref, grad_ref, act_ref, sum_ref, back_ref):
    x = x_ref[...]
    per = 128 // ff
    lane = lax.broadcasted_iota(jnp.int32, (x.shape[0], 128), 1)
    for b in range(local // per):
        wide, narrow = pl.ds(256 * b, 256), pl.ds(128 * b, 128)
        pre_act = dot(x, w_ref[:, wide])
        gate_part, up_part = pre_act[:, :128], pre_act[:, 128:]
        spread = jnp.broadcast_to(gate_ref[:, pl.ds(b * per, 1)], lane.shape)
        for k in range(1, per):
            spread = jnp.where(
                lane < k * ff,
                spread,
                jnp.broadcast_to(gate_ref[:, pl.ds(b * per + k, 1)], lane.shape),
            )
        lifted = lift_ref[:, narrow]
        sig = 1.0 / (1.0 + jnp.exp(-gate_part))
        act = (gate_part * sig * up_part).astype(BF16).astype(F32)
        act_ref[:, narrow] = (act * spread).astype(BF16)
        terms = act * lifted
        for k in range(per):
            mine = jnp.where((lane >= k * ff) & (lane < (k + 1) * ff), terms, 0.0)
            sum_ref[:, pl.ds(b * per + k, 1)] = jnp.sum(mine, axis=1, keepdims=True)
        grad_act = lifted * spread
        grad_gate = grad_act * up_part * sig * (1.0 + gate_part * (1.0 - sig))
        grad_ref[:, pl.ds(256 * b, 128)] = grad_gate.astype(BF16)
        grad_ref[:, pl.ds(256 * b + 128, 128)] = (grad_act * gate_part * sig).astype(BF16)
    back_ref[...] = dot(grad_ref[...], w_ref[...], ROWS_BACK).astype(back_ref.dtype)


def moe_rows(x, lifted, gates, weight, ff, start, total, kind):
    width, wide = weight.shape
    local = gates.shape[1]
    tile = 256 if total % 256 == 0 else 128
    skip = start // tile
    row = lambda n: pl.BlockSpec((tile, n), lambda i: (i + skip, 0))
    out = lambda n: pl.BlockSpec((tile, n), lambda i: (i, 0))
    return pl.pallas_call(
        functools.partial(moe_kernel, ff, local),
        grid=(total // tile,),
        in_specs=[
            row(width),
            row(wide // 2),
            row(local),
            pl.BlockSpec((width, wide), lambda i: (0, 0)),
        ],
        out_specs=[out(wide), out(wide // 2), out(local), out(width)],
        out_shape=[
            jax.ShapeDtypeStruct((total, wide), BF16),
            jax.ShapeDtypeStruct((total, wide // 2), BF16),
            jax.ShapeDtypeStruct((total, local), F32),
            jax.ShapeDtypeStruct((total, width), kind),
        ],
        compiler_params=pltpu.CompilerParams(vmem_limit_bytes=56 * 1024 * 1024),
        cost_estimate=pl.CostEstimate(
            flops=4 * total * width * wide, bytes_accessed=total * width * 12, transcendentals=0
        ),
    )(x, lifted, gates, weight)


def deal_kernel(dp, in_ref, out_ref):
    for p in range(dp):
        out_ref[p] = in_ref[0, :, 128 * p : 128 * (p + 1)]


def deal(expert_in, dp):
    local, rows, wide = expert_in.shape
    return pl.pallas_call(
        functools.partial(deal_kernel, dp),
        grid=(local, 2),
        in_specs=[pl.BlockSpec((1, rows, wide // 2), lambda e, g: (e, 0, g))],
        out_specs=pl.BlockSpec((dp, rows, 128), lambda e, g: (0, 0, 2 * e + g)),
        out_shape=jax.ShapeDtypeStruct((dp, rows, local * 256), expert_in.dtype),
        compiler_params=pltpu.CompilerParams(vmem_limit_bytes=32 * 1024 * 1024),
    )(expert_in)


def undeal_kernel(parts, each, *refs):
    out_ref = refs[parts]
    e, g = pl.program_id(0), pl.program_id(1)
    for h in range(parts):

        @pl.when(e // each == h)
        def _():
            column = pl.multiple_of((2 * (e - h * each) + g) * 128, 128)
            for p in range(refs[h].shape[0]):
                piece = refs[h][p, :, pl.ds(column, 128)]
                out_ref[0, :, 128 * p : 128 * (p + 1)] = piece.astype(F32)


def undeal(pieces):
    parts = len(pieces)
    dp, rows, wide = pieces[0].shape
    each = wide // 256
    return pl.pallas_call(
        functools.partial(undeal_kernel, parts, each),
        grid=(parts * each, 2),
        in_specs=[pl.BlockSpec((dp, rows, wide), lambda e, g: (0, 0, 0))] * parts,
        out_specs=pl.BlockSpec((1, rows, dp * 128), lambda e, g: (e, 0, g)),
        out_shape=jax.ShapeDtypeStruct((parts * each, rows, 2 * dp * 128), F32),
        compiler_params=pltpu.CompilerParams(vmem_limit_bytes=48 * 1024 * 1024),
    )(*pieces)


def deal_narrow(expert_in, dp):
    local, rows, wide = expert_in.shape
    ff = wide // 2 // dp
    split = expert_in.reshape(local * ff // 128, 128 // ff, rows, 2, dp, ff)
    return split.transpose(4, 2, 0, 3, 1, 5).reshape(dp, rows, 2 * local * ff)


def undeal_narrow(pieces, ff):
    whole = jnp.concatenate(pieces, axis=2)
    dp, rows, wide = whole.shape
    whole = whole.reshape(dp, rows, wide // 256, 2, 128 // ff, ff).astype(F32)
    return whole.transpose(2, 4, 1, 3, 0, 5).reshape(wide // 2 // ff, rows, 2 * dp * ff)


def swap(value):
    return lax.all_to_all(value, "dp", split_axis=0, concat_axis=0, tiled=True)


def masked(segment):
    length = segment.shape[1]
    row_index = lax.broadcasted_iota(jnp.int32, (length, length), 0)
    col_index = lax.broadcasted_iota(jnp.int32, (length, length), 1)
    return (segment[:, :, None] == segment[:, None, :]) & (col_index <= row_index)[None]


def attend(queries, key_rows, values, allowed):
    raw = jnp.einsum("sqhd,skhd->shqk", queries, key_rows, preferred_element_type=F32)
    scores = jnp.where(allowed[:, None], raw * HEAD_DIM ** (-0.5), MASKED)
    row_max = jnp.max(scores, axis=-1, keepdims=True)
    exp_terms = jnp.exp(scores - row_max)
    weights_f = exp_terms / jnp.sum(exp_terms, axis=-1, keepdims=True)
    attended = jnp.einsum(
        "shqk,skhd->sqhd", weights_f.astype(BF16), values, preferred_element_type=F32
    )
    return (attended.astype(BF16), weights_f)


def attend_back(queries, key_rows, values, weights_f, attended, grad_heads):
    weights_b = weights_f.astype(BF16)
    grad_values = jnp.einsum("shqk,sqhd->skhd", weights_b, grad_heads, preferred_element_type=F32)
    grad_weights = jnp.einsum("sqhd,skhd->shqk", grad_heads, values, preferred_element_type=F32)
    row_delta = jnp.sum(grad_heads.astype(F32) * attended.astype(F32), axis=-1)
    row_delta = jnp.swapaxes(row_delta, 1, 2)[..., None]
    grad_scores = (weights_f * (grad_weights - row_delta) * HEAD_DIM ** (-0.5)).astype(BF16)
    grad_queries = jnp.einsum(
        "shqk,skhd->sqhd", grad_scores, key_rows, preferred_element_type=F32
    )
    grad_keys = jnp.einsum("shqk,sqhd->skhd", grad_scores, queries, preferred_element_type=F32)
    return (grad_queries, grad_keys, grad_values)


def per_device(
    tokens,
    cotangent,
    segments,
    routes,
    slot_index,
    in_projection,
    out_projection,
    router_weight,
    norm_gains,
    expert_in,
    expert_down,
):
    grid = Grid()
    length, width = tokens.shape
    count, dp, ex = grid.count, grid.dp, grid.ex
    local = expert_in.shape[0]
    expert_count = ex * local
    ff = expert_down.shape[1]
    rows = width // count
    block = width // dp
    heads = HEADS // ex
    span = heads * HEAD_DIM
    group = lax.axis_index("expert")
    stage = lax.axis_index("dp")
    cosine, sine_table = rope_tables(length)
    source = grid.sources()
    ids = jnp.arange(count, dtype=source.dtype)
    back = jnp.sum(jnp.where(source[None, :] == ids[:, None], ids[None, :], 0), axis=1)
    dp_source = grid.dp_sources()
    chunks = 1 if length * count <= 4096 else length * count // 4096
    size = length // chunks

    def reorder(tensor, order):
        parts = order.shape[0]
        return jnp.take(
            tensor.reshape(tensor.shape[0], parts, width // parts), order, axis=1
        ).reshape(tensor.shape[0], width)

    small = jnp.concatenate(
        [
            norm_gains.reshape(-1),
            router_weight.reshape(-1),
            segments.astype(BF16).reshape(-1),
        ]
    )
    small = jnp.pad(small, (0, -small.shape[0] % 128)).reshape(-1, 128)
    small_flow = Flow(grid.small_gather(small))
    small_flow.go()

    piece = in_projection.reshape(rows, 3, ex, span).transpose(2, 0, 1, 3)
    piece = exchange(piece.reshape(ex, rows, 3 * span)).reshape(block, 3 * span)
    tokens_g = exchange(
        after(jnp.broadcast_to(tokens[None], (ex, length, width)), piece)
    )
    dense = Flow(grid.dp_gather(piece))
    out_flow = Flow(grid.gather(out_projection))
    cot_flow = Flow(grid.gather(cotangent[:size]))
    dealt = (deal if ff == 128 else deal_narrow)(after(expert_in, piece), dp)
    weight_down = expert_down.reshape(local * ff, width)

    quarter = local * ff // 2
    weights = []

    def fetch(*events):
        columns = slice(len(weights) * quarter, (len(weights) + 1) * quarter)
        weights.append(swap(after(dealt[:, :, columns], *events)).reshape(width, quarter))

    dense.go()
    small_flow.go(piece)
    out_flow.go(*dense.hops[0])
    cot_flow.go(*dense.hops[0])
    small_flow.go(*dense.hops[0])
    dense.go(tokens_g)
    out_flow.go(*dense.hops[1])
    cot_flow.go(*dense.hops[1])
    small_flow.go(*dense.hops[1])
    dense.go(dealt, *out_flow.hops[0], *cot_flow.hops[0])
    fetch(*dense.hops[2])
    out_flow.go(*dense.hops[2])
    small_flow.go(*dense.hops[2])
    dense.go(*out_flow.hops[1], *cot_flow.hops[1])
    cot_flow.go(*dense.hops[3])
    out_flow.go(*dense.hops[3], *out_flow.hops[2])
    proj = after(dense.finish(), weights[0])
    fetch(*dense.hops[3])
    small = small_flow.finish().reshape(count, -1)
    cuts = np.cumsum([4 * rows, rows * expert_count, length])
    all_gains, all_router, all_segments, _ = jnp.split(small, cuts, axis=1)
    gains = jnp.swapaxes(all_gains.reshape(count, 4, rows), 0, 1).reshape(4, width).astype(F32)
    router = all_router.reshape(width, expert_count)
    segment = lax.dynamic_slice_in_dim(
        all_segments.reshape(dp, ex, length), stage, 1, 0
    )[0].astype(jnp.int32)
    allowed = masked(segment)
    gain_q = lax.dynamic_slice_in_dim(gains[2], group * span, span)
    gain_k = lax.dynamic_slice_in_dim(gains[3], group * span, span)

    normed1_g, factor1 = normalize(tokens_g.reshape(ex * length, width).astype(F32))
    hidden1_g = (normed1_g * gains[0]).astype(BF16)
    projected = dot(hidden1_g, proj)
    query_raw, key_raw = projected[:, :span], projected[:, span : 2 * span]
    squares = jnp.stack([jnp.sum(query_raw**2, axis=-1), jnp.sum(key_raw**2, axis=-1)])
    squares = grid.group_sum(squares)
    squares = after(squares, weights[1], *out_flow.hops[3], *cot_flow.hops[2])
    fetch(squares)
    out_flow.go(squares)
    cot_flow.go(squares)
    factors = lax.rsqrt(squares / width + EPSILON)[:, :, None]
    query_factor, key_factor = factors[0], factors[1]
    proj_out = jnp.concatenate(out_flow.finish()).reshape(width, width)
    query_normed, key_normed = query_raw * query_factor, key_raw * key_factor

    def by_heads(tensor):
        return tensor.reshape(ex, length, heads, HEAD_DIM)

    queries = rotate(by_heads(query_normed * gain_q), cosine, sine_table, False).astype(BF16)
    key_rows = rotate(by_heads(key_normed * gain_k), cosine, sine_table, False).astype(BF16)
    values = by_heads(projected[:, 2 * span :].astype(BF16))
    attended_h, weights_f = attend(queries, key_rows, values, allowed)
    cot_flow.go(attended_h, *cot_flow.hops[3])
    attended = exchange(attended_h.reshape(ex, length, span))
    attended = after(attended, weights[2])
    fetch(attended)
    attended_c = jnp.swapaxes(attended, 0, 1).reshape(length, width)
    attended_s = reorder(attended_c, source)
    residual = tokens.astype(F32)
    middle = residual + dot(attended_s, proj_out)
    normed2, factor2 = normalize(middle)
    hidden2 = (normed2 * gains[1]).astype(BF16)
    hidden2 = after(hidden2, weights[3], *cot_flow.hops[4])
    weight_in = jnp.concatenate(weights, axis=1)
    router_probs = jax.nn.softmax(dot(hidden2, router), axis=-1)
    grad_top = cotangent.astype(F32)
    named = jnp.arange(expert_count, dtype=jnp.int32)
    chosen = jnp.any(routes[:, :, None] == named[None, None, :], axis=1)
    gates = jnp.where(chosen, router_probs, 0.0).reshape(-1, 128)

    hid_flow = Flow(grid.gather(hidden2[:size]))
    gate_flow = Flow(grid.small_gather(gates))
    cot_flow.go(hidden2)
    hid_flow.go()
    gate_flow.go()
    hid_flow.go(weight_in, *cot_flow.hops[5])
    cot_flow.go(*hid_flow.hops[0])
    gate_flow.go(*hid_flow.hops[0])
    for k in (1, 2, 3):
        gate_flow.go(*hid_flow.hops[k])
        hid_flow.go(*gate_flow.hops[k])
    gates = gate_flow.finish().reshape(count, length, expert_count)
    gates = lax.dynamic_slice_in_dim(gates[source], group * local, local, 2)
    back_flows, mix_flows, probs_parts = [], [], []
    grad_in_w, grad_down_w = [0.0] * 4, 0.0
    for i in range(chunks):
        if i:
            ready = (back_flows[-1].finish(), mix_flows[-1].finish(), grad_in_w, grad_down_w)
            part = slice(i * size, (i + 1) * size)
            cot_flow = Flow(grid.gather(after(cotangent[part], *ready)))
            hid_flow = Flow(grid.gather(after(hidden2[part], *ready)))
        cot = jnp.concatenate(cot_flow.finish()).reshape(-1, width)
        lifted = dot(cot, weight_down, ROWS_BACK)
        while len(hid_flow.hops) < 5:
            hid_flow.go()
        total = size * count
        gate_dense = gates[:, i * size : (i + 1) * size].reshape(total, local)
        hid_flow.go(lifted, gate_dense)
        hid = jnp.concatenate(hid_flow.finish()).reshape(-1, width)
        part = total // 4
        slotted = (count // 4, size, width)
        done = [None] * 4

        def run(j, *events):
            kind = BF16 if j % 2 else F32
            gates = after(gate_dense, *events)
            done[j] = moe_rows(hid, lifted, gates, weight_in, ff, j * part, part, kind)
            return done[j][3].reshape(slotted)

        far = [None, None, None, run(3)]
        far[2] = run(2, done[3][3])
        near = [None, None]
        flow = Flow(grid.scatter_early(far, lambda: near))
        flow.go()
        near[1] = run(1, *flow.hops[0])
        flow.go()
        near[0] = run(0, *flow.hops[1], done[1][3])
        flow.go()
        last = done[0][3]
        acts = [d[1] for d in done]
        grad_pre = jnp.concatenate([d[0] for d in done])
        wide = 2 * local * ff // 4
        columns = [grad_pre[:, q * wide : (q + 1) * wide] for q in range(4)]

        def weigh(q, *events):
            part = dot(after(hid, *events), columns[q], SUM_ROWS)
            grad_in_w[q] += part
            return part

        def mixed(j, *events):
            return dot(after(acts[j], *events), weight_down).astype(BF16).reshape(slotted)

        first = weigh(0, last)
        flow.go(first)
        mix = [None, None, mixed(2, *flow.hops[2]), mixed(3, *flow.hops[2])]
        flow.go(mix[2], mix[3])
        mix[0], mix[1] = mixed(0, *flow.hops[3]), mixed(1, *flow.hops[3])
        second = weigh(1, *flow.hops[3])
        if i == chunks - 1:
            gone = [g.astype(BF16).reshape(dp, block, wide) for g in grad_in_w[:1]]
            home = [swap(gone[0])]
            flow.go(mix[0], mix[1], second, home[0])
        else:
            flow.go()
        third = weigh(2, *flow.hops[4])
        flow.go(third)
        if i < chunks - 1:
            weigh(3)
        back_flows.append(flow)
        mix_flow = Flow(grid.scatter(mix, BF16))
        mix_flow.go(*flow.hops[4])
        mix_flows.append(mix_flow)
        probs_part = jnp.concatenate([d[2] for d in done])
        probs_parts.append(probs_part.reshape(count, size, local))
        act_gated = jnp.concatenate(acts)
        if i < chunks - 1:
            grad_down_w += dot(act_gated, cot, SUM_ROWS)

    def send(q, *events):
        home.append(swap(after(grad_in_w[q].astype(BF16).reshape(dp, block, wide), *events)))

    probs_all = jnp.concatenate(probs_parts, axis=1)[back]
    place = (jnp.arange(expert_count) // local == group).astype(F32)
    probs_wide = (jnp.tile(probs_all, (1, 1, ex)) * place).reshape(
        count, length * expert_count // 128, 128
    )
    grad_probs = grid.small_scatter(probs_wide).reshape(length, expert_count)
    grad_probs = jnp.where(chosen, grad_probs, 0.0)

    grad_logits = (
        router_probs * (grad_probs - jnp.sum(router_probs * grad_probs, axis=-1, keepdims=True))
    ).astype(BF16)
    grad_router_part = dot(hidden2, grad_logits, SUM_ROWS)
    grad_hidden2 = jnp.concatenate([f.finish() for f in back_flows]) + dot(grad_logits, router, ROWS_BACK)
    grad_gain_moe = jnp.sum(grad_hidden2 * normed2, axis=0)
    grad_middle = grad_top + normalize_back(grad_hidden2 * gains[1], normed2, factor2)
    grad_mid_b = grad_middle.astype(BF16)
    grad_attended = reorder(dot(grad_mid_b, proj_out, ROWS_BACK).astype(BF16), back)
    grad_heads = by_heads(
        exchange(jnp.swapaxes(grad_attended.reshape(length, ex, span), 0, 1)).reshape(
            ex * length, span
        )
    )
    quarter = width // 4
    out_parts = [
        dot(attended_s[:, j * quarter : (j + 1) * quarter], grad_mid_b, SUM_ROWS).reshape(
            count // 4, rows, width
        )
        for j in range(4)
    ]
    out_flow = Flow(grid.scatter(out_parts))
    send(1, grad_mid_b)
    mix_flow.go(grad_mid_b)
    fourth = weigh(3, grad_attended)
    grad_heads = after(grad_heads, fourth, *mix_flow.hops[1])
    send(2, grad_heads)
    mix_flow.go(grad_heads)
    out_flow.go(grad_heads)
    grad_queries, grad_keys, grad_values = attend_back(
        queries, key_rows, values, weights_f, attended_h, grad_heads
    )
    flat = (ex * length, span)
    grad_qscaled = rotate(grad_queries, cosine, sine_table, True).reshape(flat)
    grad_kscaled = rotate(grad_keys, cosine, sine_table, True).reshape(flat)
    up_q, up_k = grad_qscaled * gain_q, grad_kscaled * gain_k
    along = jnp.stack([jnp.sum(up_q * query_normed, axis=-1), jnp.sum(up_k * key_normed, axis=-1)])
    along = (grid.group_sum(along) / width)[:, :, None]
    along = after(along, *mix_flow.hops[2], *out_flow.hops[0])
    mix_flow.go(along)
    out_flow.go(along)
    grad_projected = jnp.concatenate(
        [
            query_factor * (up_q - query_normed * along[0]),
            key_factor * (up_k - key_normed * along[1]),
            grad_values.reshape(flat),
        ],
        axis=1,
    ).astype(BF16)
    mid = width // 2
    hidden1_s = reorder(hidden1_g, dp_source)
    proj_flow = Flow(
        grid.dp_scatter(
            [
                dot(hidden1_s[:, h * mid : (h + 1) * mid], grad_projected, SUM_ROWS).reshape(
                    grid.size["y"], 2, block, 3 * span
                )
                for h in range(2)
            ]
        )
    )
    proj_flow.go(home[1], home[2])
    send(3, grad_projected)
    proj_flow.go(home[3], *mix_flow.hops[3], *out_flow.hops[1])
    mix_flow.go(*proj_flow.hops[0])
    out_flow.go(*proj_flow.hops[0])
    grad_down_w += dot(after(act_gated, *proj_flow.hops[0]), cot, SUM_ROWS)
    proj_flow.go(grad_down_w, *mix_flow.hops[4], *out_flow.hops[2])
    mix_flow.go(*proj_flow.hops[1])
    out_flow.go(*proj_flow.hops[1])
    home = after(home, *proj_flow.hops[1])
    grad_expert_in = undeal(home) if ff == 128 else undeal_narrow(home, ff)
    proj_flow.go(grad_expert_in, *mix_flow.hops[5], *out_flow.hops[3])
    out_flow.go(*proj_flow.hops[2])
    grad_proj = proj_flow.finish()
    block_out = middle + jnp.concatenate([f.finish() for f in mix_flows])
    grad_out_projection = out_flow.finish()
    grad_expert_down = grad_down_w.reshape(local, ff, width)
    grad_proj = exchange(grad_proj.astype(BF16).reshape(ex, rows, 3 * span)).astype(F32)
    grad_in_projection = (
        grad_proj.reshape(ex, rows, 3, span).transpose(1, 2, 0, 3).reshape(rows, 3 * width)
    )
    grad_hidden1 = dot(grad_projected, proj, ROWS_BACK).astype(BF16)
    grad_hidden1 = jnp.sum(exchange(grad_hidden1.reshape(ex, length, width)).astype(F32), axis=0)
    own = lax.dynamic_slice_in_dim(normed1_g, group * length, length, 0)
    own_factor = lax.dynamic_slice_in_dim(factor1, group * length, length, 0)
    gain_one = jnp.sum(grad_hidden1 * own, axis=0)
    input_grad = grad_middle + normalize_back(grad_hidden1 * gains[0], own, own_factor)


    def widen(values):
        return lax.dynamic_update_slice_in_dim(jnp.zeros((width,), F32), values, group * span, 0)

    grad_gain_part = jnp.stack(
        [
            gain_one,
            grad_gain_moe,
            widen(jnp.sum(grad_qscaled * query_normed, axis=0)),
            widen(jnp.sum(grad_kscaled * key_normed, axis=0)),
        ]
    )
    last = jnp.concatenate(
        [
            jnp.swapaxes(grad_gain_part.reshape(4, count, rows), 0, 1).reshape(count, -1),
            grad_router_part.reshape(count, -1),
        ],
        axis=1,
    )
    last = after(last, grad_proj)
    last = grid.small_scatter(last.reshape(count, -1, 128 if last.shape[1] % 128 == 0 else 64))
    last = last.reshape(-1)
    grad_norm_gains = last[: 4 * rows].reshape(4, rows)
    grad_router = last[4 * rows :].reshape(rows, expert_count)
    return (
        block_out,
        input_grad,
        grad_in_projection,
        grad_out_projection,
        grad_router,
        grad_norm_gains,
        grad_expert_in,
        grad_expert_down,
    )


def solution(mesh):
    both = P(AXES, None)
    split = P("expert", "dp", None)
    in_specs = (both,) * 8 + (P(None, AXES), split, split)
    out_specs = (both,) * 5 + (P(None, AXES), split, split)
    return jax.shard_map(
        per_device, mesh=mesh, in_specs=in_specs, out_specs=out_specs, check_vma=False
    )
```
